256 devices in a mesh: seq: 32 (over y_hi, z, core), head: 8 (over x, y_lo).
Axes of the slice: x: 4, y: 4 (y_hi: 2, y_lo: 2; y = y_hi * 2 + y_lo), z: 8, core: 2. Of those that a mesh axis runs over, the one named last changes fastest.
Arguments:
- q_video: bfloat16 [28672, 3072], P('seq', 'head'), may hold values from -160 to 160
- k_video: bfloat16 [8192, 3072], P('seq', 'head'), may hold values from -8 to 8
- video_value_rows: bfloat16 [8192, 3072], P('seq', 'head'), may hold values from -6 to 6
- q_text: bfloat16 [256, 3072], P('seq', 'head'), may hold values from -160 to 160
- k_text: bfloat16 [256, 3072], P('seq', 'head'), may hold values from -8 to 8
- v_text: bfloat16 [256, 3072], P('seq', 'head'), may hold values from -6 to 6
- x_video: bfloat16 [28672, 3072], P('seq', 'head'), may hold values from -24 to 24
- x_text: bfloat16 [256, 3072], P('seq', 'head'), may hold values from -24 to 24
- out_video: bfloat16 [3072, 3072], P('head'), may hold values from -0.109375 to 0.109375
- out_text: bfloat16 [3072, 3072], P('head'), may hold values from -0.109375 to 0.109375
- mod_video: float32 [3, 3072], P(None, 'head'), may hold values from -1.5 to 1.5
- mod_text: float32 [3, 3072], P(None, 'head'), may hold values from -1.5 to 1.5
Outputs:
- x_video_out: bfloat16 [28672, 3072], P('seq', 'head')
- mlp_video_in: bfloat16 [28672, 3072], P('seq', 'head')
- x_text_out: bfloat16 [256, 3072], P('seq', 'head')
- mlp_text_in: bfloat16 [256, 3072], P('seq', 'head')
The draws below stay inside these ranges and needn't reach their ends.
All inputs are finite; a program needn't handle non-finite values.
Results may differ from the reference program's by a relative error of at most 0.0075.
Values may be sent and summed in bfloat16 or wider, within the bound.
No kernel may reach another device: no remote copies, remote signals or barrier semaphores. Data moves between devices by JAX's collectives and lax.ppermute only.
A program may use at most 128 MiB of HBM per device.

```python
import math
import jax
import jax.numpy as jnp
from jax import lax

MODEL_WIDTH = 3072
HEADS = 24
DH = 128
Q_DEV = 896
TXT_DEV = 8
QROWS = 28672
VIDEO_KEY_COUNT = 8192
TXT = 256


def shared_keys(key):
    starting_key = jax.random.fold_in(key, 0)
    text_key = jax.random.fold_in(key, 2)
    video_key_rows = jnp.clip(jax.random.normal(starting_key, (VIDEO_KEY_COUNT, MODEL_WIDTH), jnp.float32), -6.0, 6.0)
    text_keys = jnp.clip(jax.random.normal(text_key, (TXT, MODEL_WIDTH), jnp.float32), -6.0, 6.0)
    return (video_key_rows, text_keys)


def drawn_queries(key, count_of_rows):
    normal_key = jax.random.fold_in(key, 3)
    normal_part = jnp.clip(jax.random.normal(normal_key, (count_of_rows, MODEL_WIDTH), jnp.float32), -6.0, 6.0)
    base = 2.5 * normal_part
    return base


def residual_field(key, count_of_rows):
    normal_key = jax.random.fold_in(key, 0)
    column_key = jax.random.fold_in(key, 2)
    normal_part = jnp.clip(jax.random.normal(normal_key, (count_of_rows, MODEL_WIDTH), jnp.float32), -6.0, 6.0)
    base = normal_part
    column = jnp.arange(MODEL_WIDTH).astype(jnp.float32)
    column_scale = jnp.sqrt(1.0 + 2.0 * column / (MODEL_WIDTH - 1)) * jnp.exp(jax.random.uniform(column_key, (MODEL_WIDTH,), jnp.float32, -0.5, 0.5))
    return base * column_scale[None, :]


def draw_k_video(key, part):
    video_key_rows, text_keys = shared_keys(key)
    return video_key_rows.astype(jnp.bfloat16)


def draw_k_text(key, part):
    video_key_rows, text_keys = shared_keys(key)
    return text_keys.astype(jnp.bfloat16)


def draw_q_video(key, part):
    key = jax.random.fold_in(key, 11)
    return drawn_queries(key, QROWS).astype(jnp.bfloat16)


def draw_q_text(key, part):
    key = jax.random.fold_in(key, 12)
    return drawn_queries(key, TXT).astype(jnp.bfloat16)


def draw_x_video(key, part):
    key = jax.random.fold_in(key, 21)
    return residual_field(key, QROWS).astype(jnp.bfloat16)


def draw_x_text(key, part):
    key = jax.random.fold_in(key, 22)
    return residual_field(key, TXT).astype(jnp.bfloat16)


def levels(own_key, shape, pieces, low, top_value):
    loudness, own = 1.0, jax.random.fold_in(own_key, 6)
    for position, parts in pieces:
        draws = jnp.exp(jax.random.uniform(jax.random.fold_in(own, position), (parts,), jnp.float32, low / len(pieces), top_value / len(pieces)))
        loudness = loudness * jnp.repeat(draws, shape[position] // parts).reshape([-1 if axis == position else 1 for axis in range(len(shape))])
    return loudness


def noise(stream_key, dims, deviation, limit, cuts=(), dtype=jnp.bfloat16):
    gain = levels(stream_key, dims, cuts, -0.22, 0.18) if cuts else 1.0
    entries = jax.random.normal(stream_key, dims, jnp.float32) * deviation * gain
    return jnp.minimum(jnp.maximum(entries, -limit), limit).astype(dtype)


def setup_inputs(seed: int = 0) -> dict:
    seeds = jax.random.split(jax.random.key(seed), 13)
    q_video = draw_q_video(jax.random.fold_in(seeds[12], 71), 0)
    k_video = draw_k_video(jax.random.fold_in(seeds[12], 71), 0)
    video_value_rows = noise(seeds[2], (VIDEO_KEY_COUNT, MODEL_WIDTH), 1.0, 6.0, ((0, 32), (1, 8)))
    q_text = draw_q_text(jax.random.fold_in(seeds[12], 71), 0)
    k_text = draw_k_text(jax.random.fold_in(seeds[12], 71), 0)
    v_text = noise(seeds[5], (TXT, MODEL_WIDTH), 1.0, 6.0, ((0, 32), (1, 8)))
    x_video = draw_x_video(jax.random.fold_in(seeds[12], 71), 0)
    x_text = draw_x_text(jax.random.fold_in(seeds[12], 71), 0)
    out_video = noise(seeds[8], (MODEL_WIDTH, MODEL_WIDTH), MODEL_WIDTH ** -0.5, 0.109375, ((0, 8),))
    out_text = noise(seeds[9], (MODEL_WIDTH, MODEL_WIDTH), MODEL_WIDTH ** -0.5, 0.109375, ((0, 8),))
    mod_video = jnp.clip(jax.random.uniform(seeds[10], (3, MODEL_WIDTH), jnp.float32, -1.5, 1.5) * levels(seeds[10], (3, MODEL_WIDTH), ((1, 8),), -0.4, 0.0), -1.5, 1.5)
    mod_text = jnp.clip(jax.random.uniform(seeds[11], (3, MODEL_WIDTH), jnp.float32, -1.5, 1.5) * levels(seeds[11], (3, MODEL_WIDTH), ((1, 8),), -0.4, 0.0), -1.5, 1.5)
    return dict(q_video=q_video, k_video=k_video, video_value_rows=video_value_rows, q_text=q_text, k_text=k_text, v_text=v_text, x_video=x_video, x_text=x_text, out_video=out_video, out_text=out_text, mod_video=mod_video, mod_text=mod_text)


def head_attention(query_head, key_head, value_head):
    row_block = Q_DEV + TXT_DEV
    blocks = query_head.reshape(-1, row_block, DH)
    factor = 1.0 / math.sqrt(DH)

    def one_block(query_rows):
        scores = jnp.dot(query_rows, key_head.T, precision=lax.Precision.HIGHEST) * factor
        top = lax.optimization_barrier(jnp.max(scores, axis=-1, keepdims=True))
        exponent = jnp.exp(scores - top)
        row_total = lax.optimization_barrier(jnp.sum(exponent, axis=-1, keepdims=True))
        weights = lax.optimization_barrier(exponent.astype(jnp.bfloat16)).astype(jnp.float32)
        mixed = jnp.dot(weights, value_head, precision=lax.Precision.HIGHEST)
        return (mixed / row_total).astype(jnp.bfloat16)
    return lax.map(one_block, blocks).reshape(-1, DH)

def finish_stream(x_rows, attended_rows, weight, modulation):
    proj = jnp.dot(attended_rows.astype(jnp.float32), weight.astype(jnp.float32), precision=lax.Precision.HIGHEST)
    residual = x_rows.astype(jnp.float32) + modulation[0] * proj
    row_mean = lax.optimization_barrier(jnp.mean(residual, axis=-1, keepdims=True))
    row_var = lax.optimization_barrier(jnp.mean(residual * residual, axis=-1, keepdims=True)) - row_mean * row_mean
    normed = (residual - row_mean) * lax.rsqrt(row_var + 1e-06)
    mlp_in = (normed * (1.0 + modulation[2]) + modulation[1]).astype(jnp.bfloat16)
    return (residual.astype(jnp.bfloat16), mlp_in)

def reference(q_video, k_video, video_value_rows, q_text, k_text, v_text, x_video, x_text, out_video, out_text, mod_video, mod_text):
    queries = jnp.concatenate([q_video, q_text], axis=0).astype(jnp.float32)
    keys_all = jnp.concatenate([k_video, k_text], axis=0).astype(jnp.float32)
    values_all = jnp.concatenate([video_value_rows, v_text], axis=0).astype(jnp.float32)
    all_rows = queries.shape[0]
    key_rows = keys_all.shape[0]
    query_heads = queries.reshape(all_rows, HEADS, DH).transpose(1, 0, 2)
    key_heads = keys_all.reshape(key_rows, HEADS, DH).transpose(1, 0, 2)
    value_heads = values_all.reshape(key_rows, HEADS, DH).transpose(1, 0, 2)

    def per_head(triple):
        return head_attention(triple[0], triple[1], triple[2])
    attended = lax.map(per_head, (query_heads, key_heads, value_heads))
    attended = attended.transpose(1, 0, 2).reshape(all_rows, MODEL_WIDTH)
    video_rows = q_video.shape[0]
    x_video_out, mlp_video_in = finish_stream(x_video, attended[:video_rows], out_video, mod_video)
    x_text_out, mlp_text_in = finish_stream(x_text, attended[video_rows:], out_text, mod_text)
    return (x_video_out, mlp_video_in, x_text_out, mlp_text_in)
```

```python
import functools
import math

import jax
import jax.numpy as jnp
from jax import lax
from jax.experimental import pallas as pl
from jax.experimental.pallas import tpu as pltpu
from jax.sharding import PartitionSpec as P

MODEL_WIDTH = 3072
DH = 128
HERE = 3
WIDTH = HERE * DH
VID = 896
HALF = VID // 2
TXTR = 8
LANES = 2 * VID + 128
SENT = VID + 128
ACC = 144
KB = 256
BLOCK = KB + 16
SUM_ROWS = 1024
SCALE = math.log2(math.e) / math.sqrt(DH)
LIMIT = 1e30
NT = (((1,), (1,)), ((), ()))
F32, BF16 = jnp.float32, jnp.bfloat16
VMEM = pl.BlockSpec(memory_space=pltpu.VMEM)
SMEM = pl.BlockSpec(memory_space=pltpu.SMEM)
ANY = pl.BlockSpec(memory_space=pl.ANY)


def params():
    return pltpu.CompilerParams(vmem_limit_bytes=30 * 2**20)


def with_ones(v):
    return jnp.concatenate([v.T, jnp.ones((ACC - DH, v.shape[0]), BF16)], axis=0)


def scores_of(k, q):
    return lax.dot_general(k, q, NT, preferred_element_type=F32) * SCALE


def rows_of(refs, columns):
    return [r[:KB, columns] for r in refs]


def text_of(refs, columns):
    rows = [r[KB:, columns].astype(F32)[:TXTR] for r in refs]
    return jnp.concatenate(rows, axis=0).astype(BF16)


def safe_head(q, keys, values, acc, top):
    for k, v in zip(keys, values, strict=True):
        s = scores_of(k, q)
        new_top = jnp.maximum(top, jnp.max(s, axis=0, keepdims=True))
        p = jnp.exp2(s - new_top).astype(BF16)
        acc = acc * jnp.exp2(top - new_top) + jnp.dot(with_ones(v), p, preferred_element_type=F32)
        top = new_top
    return acc, top


def attend_kernel(n, texts, first, unread, *refs):
    refs = list(refs)
    q_ref, blocks, text_blocks = refs[0], refs[1 : 1 + n], refs[1 : 1 + texts]
    refs = refs[1 + max(n, texts) + unread :]
    if first:
        acc_ref, top_ref = refs[:2]
    else:
        acc_in, top_in, acc_ref, top_ref = refs[:4]
    added, tops = [], []
    for h in range(HERE):
        key_at, value_at = pl.ds(h * DH, DH), pl.ds(WIDTH + h * DH, DH)
        q = q_ref[:, key_at]
        if first:
            top = jnp.max(scores_of(blocks[0][:32, key_at], q), axis=0, keepdims=True)
        else:
            top = top_in[h, :1]
        keys, values = rows_of(blocks, key_at), rows_of(blocks, value_at)
        pairs = [(keys[i : i + 2], values[i : i + 2]) for i in range(0, n, 2)]
        if texts:
            pairs.append(([text_of(text_blocks, key_at)], [text_of(text_blocks, value_at)]))
        total = None
        for k, v in pairs:
            p = jnp.exp2(scores_of(jnp.concatenate(k, axis=0), q) - top).astype(BF16)
            d = jnp.dot(with_ones(jnp.concatenate(v, axis=0)), p, preferred_element_type=F32)
            total = d if total is None else total + d
        added.append(total)
        tops.append(top)
    fine = jnp.max(jnp.concatenate([a[DH : DH + 1] for a in added], axis=0)) < LIMIT

    @pl.when(fine)
    def _():
        for h in range(HERE):
            acc_ref[h] = added[h] if first else acc_in[h] + added[h]
            top_ref[h] = jnp.broadcast_to(tops[h], (8, LANES))

    @pl.when(jnp.logical_not(fine))
    def _():
        for h in range(HERE):
            key_at, value_at = pl.ds(h * DH, DH), pl.ds(WIDTH + h * DH, DH)
            keys, values = rows_of(blocks, key_at), rows_of(blocks, value_at)
            if texts:
                keys.append(text_of(text_blocks, key_at))
                values.append(text_of(text_blocks, value_at))
            if first:
                acc, top = jnp.zeros((ACC, LANES), F32), jnp.full((1, LANES), -1e30, F32)
            else:
                acc, top = acc_in[h], top_in[h, :1]
            acc, top = safe_head(q_ref[:, key_at], keys, values, acc, top)
            acc_ref[h] = acc
            top_ref[h] = jnp.broadcast_to(top, (8, LANES))

    if texts:
        sent_ref = refs[4]
        row = lax.broadcasted_iota(jnp.int32, (ACC - DH, SENT), 0)
        for h in range(HERE):
            total = acc_ref[h, DH : DH + 1, VID:]
            level = top_ref[h, :1, VID:] + jnp.log2(total)
            hi = level.astype(BF16).astype(F32)
            mid = (level - hi).astype(BF16).astype(F32)
            low = level - hi - mid
            levels = jnp.where(row == 0, hi, jnp.where(row == 1, mid, jnp.where(row == 2, low, 0.0)))
            sent_ref[h, :DH] = (acc_ref[h, :DH, VID:] / total).astype(BF16)
            sent_ref[h, DH:] = levels.astype(BF16)


def attend(q_all, blocks, state, every=(), unread=()):
    n, texts = len(blocks), len(every)
    blocks = [*blocks, *[b for b in every if all(b is not c for c in blocks)]]
    keys = n * KB + texts * TXTR
    out_shape = [
        jax.ShapeDtypeStruct((HERE, ACC, LANES), F32),
        jax.ShapeDtypeStruct((HERE, 8, LANES), F32),
    ]
    if texts:
        out_shape.append(jax.ShapeDtypeStruct((HERE, ACC, SENT), BF16))
    first = state is None
    before = 1 + len(blocks) + len(unread)
    return pl.pallas_call(
        functools.partial(attend_kernel, n, texts, first, len(unread)),
        in_specs=[VMEM] * (1 + len(blocks)) + [ANY] * len(unread) + ([] if first else [VMEM] * 2),
        out_specs=[VMEM] * len(out_shape),
        out_shape=out_shape,
        input_output_aliases={} if first else {before: 0, before + 1: 1},
        compiler_params=params(),
        cost_estimate=pl.CostEstimate(
            flops=HERE * LANES * keys * DH * 8,
            bytes_accessed=HERE * ACC * LANES * 4,
            transcendentals=HERE * LANES * keys,
        ),
        name="attend",
    )(q_all, *blocks, *unread, *([] if first else state))


def merged(acc, top, got):
    total = acc[DH : DH + 1]
    mine = top + jnp.log2(total)
    theirs = got[DH : DH + 1] + got[DH + 1 : DH + 2] + got[DH + 2 : DH + 3]
    share = 1.0 / (1.0 + jnp.exp2(theirs - mine))
    other = 1.0 / (1.0 + jnp.exp2(mine - theirs))
    return acc[:DH] * (share / total) + got[:DH] * other


def combine_kernel(at_ref, acc_ref, top_ref, got_ref, w_ref, first_ref, *message_refs):
    text = []
    for h in range(HERE):
        at = pl.ds(h * DH, DH)
        video = merged(acc_ref[h, :, :VID], top_ref[h, :1, :VID], got_ref[h, :, :VID].astype(F32)).T.astype(BF16)
        first_ref[:, at] = video[:HALF]
        for r in message_refs:
            r[:HALF, at] = video[HALF:]
        got = pltpu.roll(got_ref[h, :, VID:].astype(F32), DH - TXTR, 1)
        text.append(merged(acc_ref[h, :, 2 * VID :], top_ref[h, :1, 2 * VID :], got).T[: 2 * TXTR].astype(BF16))
    rows = jnp.concatenate(text, axis=1)
    for k, r in enumerate(message_refs):
        columns = pl.ds(pl.multiple_of(lax.rem(at_ref[0] + 4 - k, 4) * (2 * WIDTH), 2 * WIDTH), 2 * WIDTH)
        part = jnp.dot(rows, w_ref[:, columns], preferred_element_type=F32)[:TXTR]
        r[HALF:] = jnp.concatenate([part[:, :WIDTH], part[:, WIDTH:]], axis=0).astype(BF16)


def combine(at, acc, top, got, out_text):
    return pl.pallas_call(
        combine_kernel,
        in_specs=[SMEM] + [VMEM] * 4,
        out_specs=[VMEM] * 5,
        out_shape=[jax.ShapeDtypeStruct((HALF, WIDTH), BF16)]
        + [jax.ShapeDtypeStruct((HALF + 2 * TXTR, WIDTH), BF16)] * 4,
        compiler_params=params(),
        cost_estimate=pl.CostEstimate(flops=10**9, bytes_accessed=10**7, transcendentals=0),
        name="combine",
    )(at, acc, top, got, out_text)


def project_kernel(at_ref, *refs):
    att, weights, sent_ref, mine_ref = refs[:4], refs[4:8], refs[8], refs[9]
    left = at_ref[1] == 0
    rows = sum(
        jnp.dot(a[:HALF], w[...], preferred_element_type=F32) for a, w in zip(att, weights, strict=True)
    )
    one, two = rows[:, :WIDTH], rows[:, WIDTH:]
    mine_ref[:HALF] = jnp.where(left, one, two)
    sent_ref[:HALF] = jnp.where(left, two, one).astype(BF16)
    if att[0].shape[0] > HALF:
        text = sum(a[HALF:].astype(F32) for a in att)
        mine = jnp.where(left, text[:TXTR], text[TXTR:])
        sent = jnp.where(left, text[TXTR:], text[:TXTR])
        mine_ref[HALF:] = jnp.concatenate([mine, mine], axis=0)
        sent_ref[HALF:] = jnp.concatenate([sent, sent], axis=0).astype(BF16)


def project(at, att, weights):
    rows = att[0].shape[0]
    return pl.pallas_call(
        project_kernel,
        in_specs=[SMEM] + [VMEM] * 8,
        out_specs=[VMEM] * 2,
        out_shape=[jax.ShapeDtypeStruct((rows, WIDTH), BF16), jax.ShapeDtypeStruct((rows, WIDTH), F32)],
        compiler_params=params(),
        cost_estimate=pl.CostEstimate(
            flops=2 * 2 * rows * 4 * WIDTH * 2 * WIDTH, bytes_accessed=8 * rows * WIDTH * 2, transcendentals=0
        ),
        name="project",
    )(at, *att, *weights)


def residual_kernel(
    own_a, got_a, own_b, got_b, xv_ref, xt_ref, mv_ref, mt_ref, xv_out, xt_out, res_ref, sums_ref
):
    gate = mv_ref[:1]
    upper = xv_ref[:HALF].astype(F32) + gate * (own_a[...] + got_a[...].astype(F32))
    lower = xv_ref[HALF:].astype(F32) + gate * (own_b[:HALF] + got_b[:HALF].astype(F32))
    text_proj = own_b[HALF:] + got_b[HALF:].astype(F32)
    text = xt_ref[...].astype(F32) + mt_ref[:1] * text_proj[:TXTR]
    xv_out[:HALF] = upper.astype(BF16)
    xv_out[HALF:] = lower.astype(BF16)
    xt_out[...] = text.astype(BF16)
    rows = jnp.concatenate([upper, lower, text], axis=0)
    res_ref[...] = rows
    count = VID + TXTR
    lane = lax.broadcasted_iota(jnp.int32, (count, 128), 1)
    sums = jnp.where(
        lane == 0,
        jnp.sum(rows, axis=1, keepdims=True),
        jnp.where(lane == 1, jnp.sum(rows * rows, axis=1, keepdims=True), 0.0),
    )
    sums = jnp.concatenate([sums, jnp.zeros((SUM_ROWS - count, 128), F32)], axis=0)
    sums_ref[...] = sums.T[:8]


def norm_kernel(res_ref, mv_ref, mt_ref, s0_ref, s1_ref, s2_ref, s3_ref, video_out, text_out):
    sums = (s0_ref[...] + s1_ref[...]) + (s2_ref[...] + s3_ref[...])
    sums = jnp.concatenate([sums, jnp.zeros((120, SUM_ROWS), F32)], axis=0).T
    mean = sums[: VID + TXTR, :1] / MODEL_WIDTH
    var = sums[: VID + TXTR, 1:2] / MODEL_WIDTH - mean * mean
    normed = (res_ref[...] - mean) * lax.rsqrt(var + 1e-06)
    video_out[...] = (normed[:VID] * (1.0 + mv_ref[2:3]) + mv_ref[1:2]).astype(BF16)
    text_out[...] = (normed[VID:] * (1.0 + mt_ref[2:3]) + mt_ref[1:2]).astype(BF16)


def local(
    q_video, k_video, video_value_rows, q_text, k_text, v_text, x_video, x_text, out_video, out_text, mod_video, mod_text
):
    def over_seq(move):
        pairs = []
        for y in range(2):
            for z in range(8):
                for c in range(2):
                    a, b, d = move(y, z, c)
                    pairs.append(((y * 8 + z) * 2 + c, ((a % 2) * 8 + b % 8) * 2 + d % 2))
        return lambda value: lax.ppermute(value, "seq", pairs)

    def over_head(move):
        pairs = []
        for x in range(4):
            for y in range(2):
                a, b = move(x, y)
                pairs.append((x * 2 + y, (a % 4) * 2 + b % 2))
        return lambda value: lax.ppermute(value, "head", pairs)

    other_core = over_seq(lambda y, z, c: (y, z, 1 - c))
    other_plane = over_seq(lambda y, z, c: (1 - y, z, c))
    up = over_seq(lambda y, z, c: (y, z + 1, c))
    down = over_seq(lambda y, z, c: (y, z - 1, c))
    across = over_seq(lambda y, z, c: (1 - y, z - 1, c))
    from_on = [None] + [over_head(lambda x, y, k=k: (x - k, y)) for k in (1, 2, 3)]
    pair = over_head(lambda x, y: (x, 1 - y))

    head = lax.axis_index("head")
    x_at = head // 2
    at = jnp.stack([x_at, head % 2]).astype(jnp.int32)

    own = jnp.concatenate(
        [
            jnp.concatenate([k_video, video_value_rows], axis=1),
            jnp.concatenate([k_text, v_text], axis=1),
            jnp.zeros((BLOCK - KB - TXTR, 2 * WIDTH), BF16),
        ],
        axis=0,
    )
    q_other = other_core(jnp.concatenate([q_video, q_text], axis=0))
    y0, r1, l1 = other_plane(own), up(own), down(own)
    r2, l2 = up(r1), down(l1)
    yr1, yl1 = other_plane(r1), other_plane(l1)
    r3, l3 = up(r2), down(l2)
    ry2, ly2 = up(yr1), down(yl1)
    r4, opposite = up(r3), across(l3)
    ry3, ly3 = up(ry2), down(ly2)

    slices = [
        lax.dynamic_slice_in_dim(out_video, lax.rem(x_at + 4 - k, 4) * 2 * WIDTH, 2 * WIDTH, axis=1)
        for k in range(4)
    ]
    weights = [slices[0]] + [from_on[k](slices[k]) for k in (1, 2, 3)]

    q_all = jnp.concatenate(
        [q_video, q_other[:VID], q_text, q_other[VID:], jnp.zeros((128 - 2 * TXTR, WIDTH), BF16)], axis=0
    )
    state = attend(q_all, [own], None)
    state = attend(q_all, [r1, l1], state)
    state = attend(q_all, [y0, r2, l2], state)
    state = attend(q_all, [yr1, yl1], state)
    state = attend(q_all, [r3, l3], state)
    state = attend(q_all, [ry2, ly2], state, unread=weights[1:])
    state = attend(q_all, [r4, opposite], state)
    every = [ry3, ly3, own, r1, l1, y0, r2, l2, yr1, yl1, r3, l3, ry2, ly2, r4, opposite]
    acc, top, sent = attend(q_all, [ry3, ly3], state, every=every)

    upper, *messages = combine(at, acc, top, other_core(sent), out_text)
    rows_a = [upper] + [from_on[k](upper) for k in (1, 2, 3)]
    rows_b = [messages[0]] + [from_on[k](messages[k]) for k in (1, 2, 3)]
    sent_a, own_a = project(at, rows_a, weights)
    got_a = pair(sent_a)
    sent_b, own_b = project(at, rows_b, weights)
    got_b = pair(sent_b)

    x_video_out, x_text_out, residual, sums = pl.pallas_call(
        residual_kernel,
        in_specs=[VMEM] * 8,
        out_specs=[VMEM] * 4,
        out_shape=[
            jax.ShapeDtypeStruct((VID, WIDTH), BF16),
            jax.ShapeDtypeStruct((TXTR, WIDTH), BF16),
            jax.ShapeDtypeStruct((VID + TXTR, WIDTH), F32),
            jax.ShapeDtypeStruct((8, SUM_ROWS), F32),
        ],
        compiler_params=params(),
        name="residual",
    )(own_a, got_a, own_b, got_b, x_video, x_text, mod_video, mod_text)
    sums = sums + pair(sums)
    mlp_video_in, mlp_text_in = pl.pallas_call(
        norm_kernel,
        in_specs=[VMEM] * 7,
        out_specs=[VMEM] * 2,
        out_shape=[jax.ShapeDtypeStruct((VID, WIDTH), BF16), jax.ShapeDtypeStruct((TXTR, WIDTH), BF16)],
        compiler_params=params(),
        name="norm",
    )(residual, mod_video, mod_text, sums, *[from_on[k](sums) for k in (1, 2, 3)])
    return x_video_out, mlp_video_in, x_text_out, mlp_text_in


def solution(mesh):
    tokens, rows, columns = P("seq", "head"), P("head", None), P(None, "head")
    return jax.shard_map(
        local,
        mesh=mesh,
        in_specs=(tokens,) * 8 + (rows, rows, columns, columns),
        out_specs=(tokens,) * 4,
        check_vma=False,
    )
```

```python
import functools
import math

import jax
import jax.numpy as jnp
from jax import lax
from jax.experimental import pallas as pl
from jax.experimental.pallas import tpu as pltpu
from jax.sharding import PartitionSpec as P

MODEL_WIDTH = 3072
DH = 128
HERE = 3
WIDTH = HERE * DH
VID = 896
UPPER, LOWER = 480, 416
TXTR = 8
THEIRS = VID + 128
ACC = 144
KB = 256
BLOCK = KB + 16
CHUNKS = MODEL_WIDTH // WIDTH
SUM_ROWS = 1024
SCALE = math.log2(math.e) / math.sqrt(DH)
LIMIT = 1e30
NT = (((1,), (1,)), ((), ()))
F32, BF16 = jnp.float32, jnp.bfloat16
VMEM = pl.BlockSpec(memory_space=pltpu.VMEM)
SMEM = pl.BlockSpec(memory_space=pltpu.SMEM)
ANY = pl.BlockSpec(memory_space=pl.ANY)


def params():
    return pltpu.CompilerParams(vmem_limit_bytes=30 * 2**20)


def with_ones(v):
    return jnp.concatenate([v.T, jnp.ones((ACC - DH, v.shape[0]), BF16)], axis=0)


def scores_of(k, q):
    return lax.dot_general(k, q, NT, preferred_element_type=F32) * SCALE


def rows_of(refs, columns):
    return [r[:KB, columns] for r in refs]


def text_of(refs, columns):
    rows = [r[KB:, columns].astype(F32)[:TXTR] for r in refs]
    return jnp.concatenate(rows, axis=0).astype(BF16)


def safe_head(q, keys, values, acc, top):
    for k, v in zip(keys, values, strict=True):
        s = scores_of(k, q)
        new_top = jnp.maximum(top, jnp.max(s, axis=0, keepdims=True))
        p = jnp.exp2(s - new_top).astype(BF16)
        acc = acc * jnp.exp2(top - new_top) + jnp.dot(with_ones(v), p, preferred_element_type=F32)
        top = new_top
    return acc, top


def attend_kernel(groups, n, texts, first, unread, send, *refs):
    q_refs, refs = refs[:groups], refs[groups:]
    blocks, text_blocks = refs[:n], refs[:texts]
    refs = refs[max(n, texts) + unread :]
    before, after = (None, refs) if first else (refs[: 2 * groups], refs[2 * groups :])
    places = [(g, h) for g in range(groups) for h in range(HERE)]

    def operands(h):
        key_at, value_at = pl.ds(h * DH, DH), pl.ds(WIDTH + h * DH, DH)
        keys, values = rows_of(blocks, key_at), rows_of(blocks, value_at)
        if not texts:
            return keys, values, [], []
        return keys, values, [text_of(text_blocks, key_at)], [text_of(text_blocks, value_at)]

    added, tops = {}, {}
    for g, h in places:
        q = q_refs[g][:, pl.ds(h * DH, DH)]
        keys, values, more_keys, more_values = operands(h)
        if first:
            top = jnp.max(scores_of(keys[0][:32], q), axis=0, keepdims=True)
        else:
            top = before[2 * g + 1][h, :1]
        pairs = [(keys[i : i + 2], values[i : i + 2]) for i in range(0, n, 2)]
        if texts:
            pairs.append((more_keys, more_values))
        total = None
        for k, v in pairs:
            p = jnp.exp2(scores_of(jnp.concatenate(k, axis=0), q) - top).astype(BF16)
            d = jnp.dot(with_ones(jnp.concatenate(v, axis=0)), p, preferred_element_type=F32)
            total = d if total is None else total + d
        added[g, h], tops[g, h] = total, top
    fine = jnp.max(jnp.concatenate([a[DH : DH + 1] for a in added.values()], axis=1)) < LIMIT

    @pl.when(fine)
    def _():
        for g, h in places:
            after[2 * g][h] = added[g, h] if first else before[2 * g][h] + added[g, h]
            after[2 * g + 1][h] = jnp.broadcast_to(tops[g, h], (8, tops[g, h].shape[1]))

    @pl.when(jnp.logical_not(fine))
    def _():
        for g, h in places:
            lanes = q_refs[g].shape[0]
            keys, values, more_keys, more_values = operands(h)
            if first:
                acc, top = jnp.zeros((ACC, lanes), F32), jnp.full((1, lanes), -1e30, F32)
            else:
                acc, top = before[2 * g][h], before[2 * g + 1][h, :1]
            acc, top = safe_head(
                q_refs[g][:, pl.ds(h * DH, DH)], keys + more_keys, values + more_values, acc, top
            )
            after[2 * g][h] = acc
            after[2 * g + 1][h] = jnp.broadcast_to(top, (8, lanes))

    if send:
        acc_ref, top_ref, sent_ref = after
        row = lax.broadcasted_iota(jnp.int32, (ACC - DH, acc_ref.shape[2]), 0)
        for h in range(HERE):
            total = acc_ref[h, DH : DH + 1]
            inverse = 1.0 / total
            level = top_ref[h, :1] + jnp.log2(total)
            hi = level.astype(BF16).astype(F32)
            mid = (level - hi).astype(BF16).astype(F32)
            low = level - hi - mid
            levels = jnp.where(row == 0, hi, jnp.where(row == 1, mid, jnp.where(row == 2, low, 0.0)))
            sent_ref[h, :DH] = (acc_ref[h, :DH] * inverse).astype(BF16)
            sent_ref[h, DH:] = levels.astype(BF16)


def attend(queries, blocks, states=None, every=(), unread=(), send=False):
    n, texts, groups = len(blocks), len(every), len(queries)
    blocks = [*blocks, *[b for b in every if all(b is not c for c in blocks)]]
    keys = n * KB + texts * TXTR
    lanes = sum(q.shape[0] for q in queries)
    out_shape = []
    for q in queries:
        out_shape.append(jax.ShapeDtypeStruct((HERE, ACC, q.shape[0]), F32))
        out_shape.append(jax.ShapeDtypeStruct((HERE, 8, q.shape[0]), F32))
    if send:
        out_shape.append(jax.ShapeDtypeStruct((HERE, ACC, queries[0].shape[0]), BF16))
    first = states is None
    states = [] if first else states
    before = groups + len(blocks) + len(unread)
    return pl.pallas_call(
        functools.partial(attend_kernel, groups, n, texts, first, len(unread), send),
        in_specs=[VMEM] * (groups + len(blocks)) + [ANY] * len(unread) + [VMEM] * len(states),
        out_specs=[VMEM] * len(out_shape),
        out_shape=out_shape,
        input_output_aliases={before + i: i for i in range(len(states))},
        compiler_params=params(),
        cost_estimate=pl.CostEstimate(
            flops=HERE * lanes * keys * DH * 8,
            bytes_accessed=HERE * ACC * lanes * 4,
            transcendentals=HERE * lanes * keys,
        ),
        name="attend",
    )(*queries, *blocks, *unread, *states)


def merged(acc, top, got):
    total = acc[DH : DH + 1]
    mine = top + jnp.log2(total)
    theirs = got[DH : DH + 1] + got[DH + 1 : DH + 2] + got[DH + 2 : DH + 3]
    share = 1.0 / (1.0 + jnp.exp2(theirs - mine))
    other = 1.0 / (1.0 + jnp.exp2(mine - theirs))
    return acc[:DH] * (share / total) + got[:DH] * other


def combine_kernel(acc_ref, top_ref, text_acc, text_top, got_ref, w_hbm, upper_ref, lower_ref, w_ref, sem):
    copy = pltpu.make_async_copy(w_hbm, w_ref, sem)
    copy.start()
    text = []
    for h in range(HERE):
        at = pl.ds(h * DH, DH)
        video = merged(acc_ref[h], top_ref[h, :1], got_ref[h, :, :VID].astype(F32)).T.astype(BF16)
        upper_ref[:, at] = video[:UPPER]
        lower_ref[:LOWER, at] = video[UPPER:]
        got = pltpu.roll(got_ref[h, :, VID:].astype(F32), DH - TXTR, 1)
        rows = merged(text_acc[h, :, VID:], text_top[h, :1, VID:], got).T
        text.append(rows[: 2 * TXTR].astype(BF16))
    copy.wait()
    part = jnp.dot(jnp.concatenate(text, axis=1), w_ref[...], preferred_element_type=F32)[:TXTR]
    chunks = [part[:, j * WIDTH : (j + 1) * WIDTH] for j in range(CHUNKS)]
    lower_ref[LOWER:] = jnp.concatenate(chunks, axis=0).astype(BF16)


def combine(own, theirs, got, out_text):
    return pl.pallas_call(
        combine_kernel,
        in_specs=[VMEM] * 5 + [ANY],
        out_specs=[VMEM] * 2,
        out_shape=[
            jax.ShapeDtypeStruct((UPPER, WIDTH), BF16),
            jax.ShapeDtypeStruct((LOWER + CHUNKS * TXTR, WIDTH), BF16),
        ],
        scratch_shapes=[pltpu.VMEM((WIDTH, MODEL_WIDTH), BF16), pltpu.SemaphoreType.DMA(())],
        compiler_params=params(),
        cost_estimate=pl.CostEstimate(flops=10**9, bytes_accessed=10**7, transcendentals=0),
        name="combine",
    )(*own, *theirs, got, out_text)


def slice_kernel(steps, unread, at_ref, w_ref, *refs):
    out_refs, sems = refs[unread : unread + len(steps)], refs[unread + len(steps) :]
    copies = []
    for k, out_ref, sem in zip(steps, out_refs, sems, strict=True):
        first = lax.rem(at_ref[0] + 4 - k, 4) * (2 * WIDTH)
        columns = pl.ds(pl.multiple_of(first, 2 * WIDTH), 2 * WIDTH)
        copies.append(pltpu.make_async_copy(w_ref.at[:, columns], out_ref, sem))
        copies[-1].start()
    for copy in copies:
        copy.wait()


def column_slices(at, weight, steps, unread=()):
    return pl.pallas_call(
        functools.partial(slice_kernel, steps, len(unread)),
        in_specs=[SMEM, ANY] + [ANY] * len(unread),
        out_specs=[VMEM] * len(steps),
        out_shape=[jax.ShapeDtypeStruct((WIDTH, 2 * WIDTH), BF16)] * len(steps),
        scratch_shapes=[pltpu.SemaphoreType.DMA(())] * len(steps),
        compiler_params=params(),
        name="columns",
    )(at, weight, *unread)


def own_kernel(upper_ref, lower_ref, w_ref, upper_out, lower_out):
    upper_out[...] = jnp.dot(upper_ref[...], w_ref[...], preferred_element_type=F32)
    lower_out[...] = jnp.dot(lower_ref[:LOWER], w_ref[...], preferred_element_type=F32)


def project_own(upper, lower, weight):
    return pl.pallas_call(
        own_kernel,
        in_specs=[VMEM] * 3,
        out_specs=[VMEM] * 2,
        out_shape=[jax.ShapeDtypeStruct((rows, 2 * WIDTH), F32) for rows in (UPPER, LOWER)],
        compiler_params=params(),
        cost_estimate=pl.CostEstimate(flops=10**9, bytes_accessed=5 * 10**6, transcendentals=0),
        name="project_own",
    )(upper, lower, weight)


def more_kernel(sum_ref, one_ref, two_ref, w_one, w_two, out_ref):
    rows = sum_ref.shape[0]
    out_ref[...] = (
        sum_ref[...]
        + jnp.dot(one_ref[:rows], w_one[...], preferred_element_type=F32)
        + jnp.dot(two_ref[:rows], w_two[...], preferred_element_type=F32)
    )


def project_more(total, one, two, w_one, w_two):
    return pl.pallas_call(
        more_kernel,
        in_specs=[VMEM] * 5,
        out_specs=VMEM,
        out_shape=jax.ShapeDtypeStruct(total.shape, F32),
        input_output_aliases={0: 0},
        compiler_params=params(),
        cost_estimate=pl.CostEstimate(flops=10**9, bytes_accessed=5 * 10**6, transcendentals=0),
        name="project_more",
    )(total, one, two, w_one, w_two)


def last_kernel(at_ref, sum_ref, *refs):
    att, w_ref, sent_ref, mine_ref = refs[:-3], refs[-3], refs[-2], refs[-1]
    left = at_ref[1] == 0
    count = sum_ref.shape[0]
    rows = sum_ref[...] + jnp.dot(att[0][:count], w_ref[...], preferred_element_type=F32)
    one, two = rows[:, :WIDTH], rows[:, WIDTH:]
    mine_ref[:count] = jnp.where(left, one, two)
    sent_ref[:count] = jnp.where(left, two, one).astype(BF16)
    if len(att) > 1:
        at = pl.ds(pl.multiple_of(count + at_ref[0] * (2 * TXTR), 2 * TXTR), 2 * TXTR)
        text = sum(a[at].astype(F32) for a in att)
        mine = jnp.where(left, text[:TXTR], text[TXTR:])
        sent = jnp.where(left, text[TXTR:], text[:TXTR])
        mine_ref[count:] = jnp.concatenate([mine, mine], axis=0)
        sent_ref[count:] = jnp.concatenate([sent, sent], axis=0).astype(BF16)


def project_last(at, total, att, weight):
    rows = total.shape[0] + (2 * TXTR if len(att) > 1 else 0)
    return pl.pallas_call(
        last_kernel,
        in_specs=[SMEM] + [VMEM] * (2 + len(att)),
        out_specs=[VMEM] * 2,
        out_shape=[jax.ShapeDtypeStruct((rows, WIDTH), BF16), jax.ShapeDtypeStruct((rows, WIDTH), F32)],
        compiler_params=params(),
        cost_estimate=pl.CostEstimate(flops=10**9, bytes_accessed=5 * 10**6, transcendentals=0),
        name="project_last",
    )(at, total, *att, weight)


def residual_kernel(
    own_a, got_a, own_b, got_b, xv_ref, xt_ref, mv_ref, mt_ref, xv_out, xt_out, res_ref, sums_ref
):
    gate = mv_ref[:1]
    upper = xv_ref[:UPPER].astype(F32) + gate * (own_a[...] + got_a[...].astype(F32))
    lower = xv_ref[UPPER:].astype(F32) + gate * (own_b[:LOWER] + got_b[:LOWER].astype(F32))
    text_proj = own_b[LOWER:] + got_b[LOWER:].astype(F32)
    text = xt_ref[...].astype(F32) + mt_ref[:1] * text_proj[:TXTR]
    xv_out[:UPPER] = upper.astype(BF16)
    xv_out[UPPER:] = lower.astype(BF16)
    xt_out[...] = text.astype(BF16)
    rows = jnp.concatenate([upper, lower, text], axis=0)
    res_ref[...] = rows
    count = VID + TXTR
    lane = lax.broadcasted_iota(jnp.int32, (count, 128), 1)
    sums = jnp.where(
        lane == 0,
        jnp.sum(rows, axis=1, keepdims=True),
        jnp.where(lane == 1, jnp.sum(rows * rows, axis=1, keepdims=True), 0.0),
    )
    sums = jnp.concatenate([sums, jnp.zeros((SUM_ROWS - count, 128), F32)], axis=0)
    sums_ref[...] = sums.T[:8]


def norm_kernel(res_ref, mv_ref, mt_ref, s0_ref, s1_ref, s2_ref, s3_ref, video_out, text_out):
    sums = (s0_ref[...] + s1_ref[...]) + (s2_ref[...] + s3_ref[...])
    sums = jnp.concatenate([sums, jnp.zeros((120, SUM_ROWS), F32)], axis=0).T
    mean = sums[: VID + TXTR, :1] / MODEL_WIDTH
    var = sums[: VID + TXTR, 1:2] / MODEL_WIDTH - mean * mean
    normed = (res_ref[...] - mean) * lax.rsqrt(var + 1e-06)
    video_out[...] = (normed[:VID] * (1.0 + mv_ref[2:3]) + mv_ref[1:2]).astype(BF16)
    text_out[...] = (normed[VID:] * (1.0 + mt_ref[2:3]) + mt_ref[1:2]).astype(BF16)


def local(
    q_video, k_video, video_value_rows, q_text, k_text, v_text, x_video, x_text, out_video, out_text, mod_video, mod_text
):
    def over_seq(move):
        pairs = []
        for y in range(2):
            for z in range(8):
                for c in range(2):
                    a, b, d = move(y, z, c)
                    pairs.append(((y * 8 + z) * 2 + c, ((a % 2) * 8 + b % 8) * 2 + d % 2))
        return lambda value: lax.ppermute(value, "seq", pairs)

    def over_head(move):
        pairs = []
        for x in range(4):
            for y in range(2):
                a, b = move(x, y)
                pairs.append((x * 2 + y, (a % 4) * 2 + b % 2))
        return lambda value: lax.ppermute(value, "head", pairs)

    other_core = over_seq(lambda y, z, c: (y, z, 1 - c))
    other_plane = over_seq(lambda y, z, c: (1 - y, z, c))
    up = over_seq(lambda y, z, c: (y, z + 1, c))
    down = over_seq(lambda y, z, c: (y, z - 1, c))
    across = over_seq(lambda y, z, c: (1 - y, z - 1, c))
    from_on = [None] + [over_head(lambda x, y, k=k: (x - k, y)) for k in (1, 2, 3)]
    pair = over_head(lambda x, y: (x, 1 - y))

    head = lax.axis_index("head")
    x_at = head // 2
    at = jnp.stack([x_at, head % 2]).astype(jnp.int32)

    own = jnp.concatenate(
        [
            jnp.concatenate([k_video, video_value_rows], axis=1),
            jnp.concatenate([k_text, v_text], axis=1),
            jnp.zeros((BLOCK - KB - TXTR, 2 * WIDTH), BF16),
        ],
        axis=0,
    )
    q_other = other_core(jnp.concatenate([q_video, q_text], axis=0))
    y0, r1, l1 = other_plane(own), up(own), down(own)
    r2, l2 = up(r1), down(l1)
    yr1, yl1 = other_plane(r1), other_plane(l1)
    r3, l3 = up(r2), down(l2)
    ry2, ly2 = up(yr1), down(yl1)
    r4, opposite = up(r3), across(l3)
    ry3, ly3 = up(ry2), down(ly2)

    here, slice_1 = column_slices(at, out_video, (0, 1))
    weights = [here, from_on[1](slice_1)]
    for k in (2, 3):
        [slice_k] = column_slices(at, out_video, (k,), unread=weights[k - 1 :])
        weights.append(from_on[k](slice_k))

    q_theirs = jnp.concatenate(
        [q_other[:VID], q_text, q_other[VID:], jnp.zeros((THEIRS - VID - 2 * TXTR, WIDTH), BF16)], axis=0
    )
    queries = [q_theirs, q_video]
    states = attend(queries, [own, r1, l1, y0])
    states = attend(queries, [r2, l2], states)
    states = attend(queries, [yr1, yl1], states, unread=weights[1:2])
    states = attend(queries, [r3, l3], states, unread=weights[2:3])
    states = attend(queries, [ry2, ly2], states)
    states = attend(queries, [r4, opposite], states)
    every = [ry3, ly3, own, r1, l1, y0, r2, l2, yr1, yl1, r3, l3, ry2, ly2, r4, opposite]
    *theirs, sent = attend(queries[:1], [ry3, ly3], states[:2], every=every, unread=weights[3:], send=True)
    got = other_core(sent)
    mine = attend(queries[1:], [ry3, ly3], states[2:], every=every)

    upper, lower = combine(mine, theirs, got, out_text)
    upper_1, upper_3 = from_on[1](upper), from_on[3](upper)
    lower_1, lower_3 = from_on[1](lower), from_on[3](lower)
    upper_2, lower_2 = from_on[1](upper_1), from_on[3](lower_3)
    sum_a, sum_b = project_own(upper, lower, weights[0])
    sum_a = project_more(sum_a, upper_1, upper_3, weights[1], weights[3])
    sent_a, own_a = project_last(at, sum_a, [upper_2], weights[2])
    got_a = pair(sent_a)
    sum_b = project_more(sum_b, lower_1, lower_3, weights[1], weights[3])
    sent_b, own_b = project_last(at, sum_b, [lower_2, lower, lower_1, lower_3], weights[2])
    got_b = pair(sent_b)

    x_video_out, x_text_out, residual, sums = pl.pallas_call(
        residual_kernel,
        in_specs=[VMEM] * 8,
        out_specs=[VMEM] * 4,
        out_shape=[
            jax.ShapeDtypeStruct((VID, WIDTH), BF16),
            jax.ShapeDtypeStruct((TXTR, WIDTH), BF16),
            jax.ShapeDtypeStruct((VID + TXTR, WIDTH), F32),
            jax.ShapeDtypeStruct((8, SUM_ROWS), F32),
        ],
        compiler_params=params(),
        name="residual",
    )(own_a, got_a, own_b, got_b, x_video, x_text, mod_video, mod_text)
    sums = sums + pair(sums)
    mlp_video_in, mlp_text_in = pl.pallas_call(
        norm_kernel,
        in_specs=[VMEM] * 7,
        out_specs=[VMEM] * 2,
        out_shape=[jax.ShapeDtypeStruct((VID, WIDTH), BF16), jax.ShapeDtypeStruct((TXTR, WIDTH), BF16)],
        compiler_params=params(),
        name="norm",
    )(residual, mod_video, mod_text, sums, *[from_on[k](sums) for k in (1, 2, 3)])
    return x_video_out, mlp_video_in, x_text_out, mlp_text_in


def solution(mesh):
    tokens, rows, columns = P("seq", "head"), P("head", None), P(None, "head")
    return jax.shard_map(
        local,
        mesh=mesh,
        in_specs=(tokens,) * 8 + (rows, rows, columns, columns),
        out_specs=(tokens,) * 4,
        check_vma=False,
    )
```

```python
import functools
import math

import jax
import jax.numpy as jnp
from jax import lax
from jax.experimental import pallas as pl
from jax.experimental.pallas import tpu as pltpu
from jax.sharding import PartitionSpec as P

MODEL_WIDTH = 3072
DH = 128
HERE = 3
WIDTH = HERE * DH
VID = 896
UPPER, LOWER = 480, 416
TXTR = 8
THEIRS = VID + 128
ACC = 144
KB = 256
BLOCK = KB + 16
CHUNKS = MODEL_WIDTH // WIDTH
SUM_ROWS = 1024
SCALE = math.log2(math.e) / math.sqrt(DH)
LIMIT = 1e30
NT = (((1,), (1,)), ((), ()))
F32, BF16 = jnp.float32, jnp.bfloat16
VMEM = pl.BlockSpec(memory_space=pltpu.VMEM)
SMEM = pl.BlockSpec(memory_space=pltpu.SMEM)
ANY = pl.BlockSpec(memory_space=pl.ANY)
HBM = pl.BlockSpec(memory_space=pltpu.HBM)


def params():
    return pltpu.CompilerParams(vmem_limit_bytes=30 * 2**20)


def with_ones(v):
    return jnp.concatenate([v.T, jnp.ones((ACC - DH, v.shape[0]), BF16)], axis=0)


def scores_of(k, q):
    return lax.dot_general(k, q, NT, preferred_element_type=F32) * SCALE


def rows_of(refs, columns):
    return [r[:KB, columns] for r in refs]


def text_of(refs, columns):
    rows = [r[KB:, columns].astype(F32)[:TXTR] for r in refs]
    return jnp.concatenate(rows, axis=0).astype(BF16)


def safe_head(q, keys, values, acc, top):
    for k, v in zip(keys, values, strict=True):
        s = scores_of(k, q)
        new_top = jnp.maximum(top, jnp.max(s, axis=0, keepdims=True))
        p = jnp.exp2(s - new_top).astype(BF16)
        acc = acc * jnp.exp2(top - new_top) + jnp.dot(with_ones(v), p, preferred_element_type=F32)
        top = new_top
    return acc, top


def columns_of(head):
    at = pl.multiple_of(head * DH, DH)
    return pl.ds(at, DH), pl.ds(WIDTH + at, DH)


def attend_kernel(groups, n, texts, first, unread, send, *refs):
    q_refs, refs = refs[:groups], refs[groups:]
    blocks, text_blocks = refs[:n], refs[:texts]
    refs = refs[max(n, texts) + unread :]
    before, after = (None, refs) if first else (refs[: 2 * groups], refs[2 * groups :])

    def text_operands(h):
        key_at, value_at = columns_of(h)
        if not texts:
            return [], []
        return [text_of(text_blocks, key_at)], [text_of(text_blocks, value_at)]

    @pl.loop(0, HERE)
    def _(h):
        key_at, value_at = columns_of(h)
        keys, values = rows_of(blocks, key_at), rows_of(blocks, value_at)
        pairs = [(keys[i : i + 2], values[i : i + 2]) for i in range(0, n, 2)]
        if texts:
            pairs.append(text_operands(h))
        added, tops = [], []
        for g in range(groups):
            q = q_refs[g][:, key_at]
            if first:
                top = jnp.max(scores_of(keys[0][:32], q), axis=0, keepdims=True)
            else:
                top = before[2 * g + 1][h, :1]
            total = None
            for k, v in pairs:
                p = jnp.exp2(scores_of(jnp.concatenate(k, axis=0), q) - top).astype(BF16)
                d = jnp.dot(with_ones(jnp.concatenate(v, axis=0)), p, preferred_element_type=F32)
                total = d if total is None else total + d
            added.append(total)
            tops.append(top)
        fine = jnp.max(jnp.concatenate([a[DH : DH + 1] for a in added], axis=1)) < LIMIT

        @pl.when(fine)
        def _():
            for g in range(groups):
                after[2 * g][h] = added[g] if first else before[2 * g][h] + added[g]
                after[2 * g + 1][h] = jnp.broadcast_to(tops[g], (8, tops[g].shape[1]))

        @pl.when(jnp.logical_not(fine))
        def _():
            for g in range(groups):

                @pl.loop(0, q_refs[g].shape[0] // 128)
                def _(i):
                    lanes = pl.ds(pl.multiple_of(i * 128, 128), 128)
                    more_keys, more_values = text_operands(h)
                    if first:
                        acc, top = jnp.zeros((ACC, 128), F32), jnp.full((1, 128), -1e30, F32)
                    else:
                        acc, top = before[2 * g][h, :, lanes], before[2 * g + 1][h, :1, lanes]
                    acc, top = safe_head(
                        q_refs[g][lanes, key_at],
                        rows_of(blocks, key_at) + more_keys,
                        rows_of(blocks, value_at) + more_values,
                        acc,
                        top,
                    )
                    after[2 * g][h, :, lanes] = acc
                    after[2 * g + 1][h, :, lanes] = jnp.broadcast_to(top, (8, 128))

        if send:
            acc_ref, top_ref, sent_ref = after
            row = lax.broadcasted_iota(jnp.int32, (ACC - DH, acc_ref.shape[2]), 0)
            total = acc_ref[h, DH : DH + 1]
            inverse = 1.0 / total
            level = top_ref[h, :1] + jnp.log2(total)
            hi = level.astype(BF16).astype(F32)
            mid = (level - hi).astype(BF16).astype(F32)
            low = level - hi - mid
            levels = jnp.where(row == 0, hi, jnp.where(row == 1, mid, jnp.where(row == 2, low, 0.0)))
            sent_ref[h, :DH] = (acc_ref[h, :DH] * inverse).astype(BF16)
            sent_ref[h, DH:] = levels.astype(BF16)


def attend(queries, blocks, states=None, every=(), unread=(), send=False):
    n, texts, groups = len(blocks), len(every), len(queries)
    blocks = [*blocks, *[b for b in every if all(b is not c for c in blocks)]]
    keys = n * KB + texts * TXTR
    lanes = sum(q.shape[0] for q in queries)
    out_shape = []
    for q in queries:
        out_shape.append(jax.ShapeDtypeStruct((HERE, ACC, q.shape[0]), F32))
        out_shape.append(jax.ShapeDtypeStruct((HERE, 8, q.shape[0]), F32))
    if send:
        out_shape.append(jax.ShapeDtypeStruct((HERE, ACC, queries[0].shape[0]), BF16))
    first = states is None
    states = [] if first else states
    before = groups + len(blocks) + len(unread)
    return pl.pallas_call(
        functools.partial(attend_kernel, groups, n, texts, first, len(unread), send),
        in_specs=[VMEM] * (groups + len(blocks)) + [ANY] * len(unread) + [VMEM] * len(states),
        out_specs=[VMEM] * len(out_shape),
        out_shape=out_shape,
        input_output_aliases={before + i: i for i in range(len(states))},
        compiler_params=params(),
        cost_estimate=pl.CostEstimate(
            flops=HERE * lanes * keys * DH * 8,
            bytes_accessed=HERE * ACC * lanes * 4,
            transcendentals=HERE * lanes * keys,
        ),
        name="attend",
    )(*queries, *blocks, *unread, *states)


def merged(acc, top, got):
    total = acc[DH : DH + 1]
    mine = top + jnp.log2(total)
    theirs = got[DH : DH + 1] + got[DH + 1 : DH + 2] + got[DH + 2 : DH + 3]
    share = 1.0 / (1.0 + jnp.exp2(theirs - mine))
    other = 1.0 / (1.0 + jnp.exp2(mine - theirs))
    return acc[:DH] * (share / total) + got[:DH] * other


def combine_kernel(
    acc_ref, top_ref, text_acc, text_top, got_ref, w_hbm, upper_ref, lower_ref, w_ref, rows_ref, sem
):
    copy = pltpu.make_async_copy(w_hbm, w_ref, sem)
    copy.start()

    @pl.loop(0, HERE)
    def _(h):
        at, _ = columns_of(h)
        video = merged(acc_ref[h], top_ref[h, :1], got_ref[h, :, :VID].astype(F32)).T.astype(BF16)
        upper_ref[:, at] = video[:UPPER]
        lower_ref[:LOWER, at] = video[UPPER:]
        got = pltpu.roll(got_ref[h, :, VID:].astype(F32), DH - TXTR, 1)
        rows = merged(text_acc[h, :, VID:], text_top[h, :1, VID:], got).T
        rows_ref[:, at] = rows[: 2 * TXTR].astype(BF16)

    copy.wait()
    part = jnp.dot(rows_ref[...], w_ref[...], preferred_element_type=F32)[:TXTR]
    chunks = [part[:, j * WIDTH : (j + 1) * WIDTH] for j in range(CHUNKS)]
    lower_ref[LOWER:] = jnp.concatenate(chunks, axis=0).astype(BF16)


def combine(own, theirs, got, out_text):
    return pl.pallas_call(
        combine_kernel,
        in_specs=[VMEM] * 5 + [HBM],
        out_specs=[VMEM] * 2,
        out_shape=[
            jax.ShapeDtypeStruct((UPPER, WIDTH), BF16),
            jax.ShapeDtypeStruct((LOWER + CHUNKS * TXTR, WIDTH), BF16),
        ],
        scratch_shapes=[
            pltpu.VMEM((WIDTH, MODEL_WIDTH), BF16),
            pltpu.VMEM((2 * TXTR, WIDTH), BF16),
            pltpu.SemaphoreType.DMA(()),
        ],
        compiler_params=params(),
        cost_estimate=pl.CostEstimate(flops=10**9, bytes_accessed=10**7, transcendentals=0),
        name="combine",
    )(*own, *theirs, got, out_text)


def slice_kernel(steps, unread, at_ref, w_ref, *refs):
    out_refs, sems = refs[unread : unread + len(steps)], refs[unread + len(steps) :]
    copies = []
    for k, out_ref, sem in zip(steps, out_refs, sems, strict=True):
        first = lax.rem(at_ref[0] + 4 - k, 4) * (2 * WIDTH)
        columns = pl.ds(pl.multiple_of(first, 2 * WIDTH), 2 * WIDTH)
        copies.append(pltpu.make_async_copy(w_ref.at[:, columns], out_ref, sem))
        copies[-1].start()
    for copy in copies:
        copy.wait()


def column_slices(at, weight, steps, unread=()):
    return pl.pallas_call(
        functools.partial(slice_kernel, steps, len(unread)),
        in_specs=[SMEM, HBM] + [ANY] * len(unread),
        out_specs=[VMEM] * len(steps),
        out_shape=[jax.ShapeDtypeStruct((WIDTH, 2 * WIDTH), BF16)] * len(steps),
        scratch_shapes=[pltpu.SemaphoreType.DMA(())] * len(steps),
        compiler_params=params(),
        name="columns",
    )(at, weight, *unread)


def own_kernel(upper_ref, lower_ref, w_ref, upper_out, lower_out):
    upper_out[...] = jnp.dot(upper_ref[...], w_ref[...], preferred_element_type=F32)
    lower_out[...] = jnp.dot(lower_ref[:LOWER], w_ref[...], preferred_element_type=F32)


def project_own(upper, lower, weight):
    return pl.pallas_call(
        own_kernel,
        in_specs=[VMEM] * 3,
        out_specs=[VMEM] * 2,
        out_shape=[jax.ShapeDtypeStruct((rows, 2 * WIDTH), F32) for rows in (UPPER, LOWER)],
        compiler_params=params(),
        cost_estimate=pl.CostEstimate(flops=10**9, bytes_accessed=5 * 10**6, transcendentals=0),
        name="project_own",
    )(upper, lower, weight)


def more_kernel(sum_ref, one_ref, two_ref, w_one, w_two, out_ref):
    rows = sum_ref.shape[0]
    out_ref[...] = (
        sum_ref[...]
        + jnp.dot(one_ref[:rows], w_one[...], preferred_element_type=F32)
        + jnp.dot(two_ref[:rows], w_two[...], preferred_element_type=F32)
    )


def project_more(total, one, two, w_one, w_two):
    return pl.pallas_call(
        more_kernel,
        in_specs=[VMEM] * 5,
        out_specs=VMEM,
        out_shape=jax.ShapeDtypeStruct(total.shape, F32),
        input_output_aliases={0: 0},
        compiler_params=params(),
        cost_estimate=pl.CostEstimate(flops=10**9, bytes_accessed=5 * 10**6, transcendentals=0),
        name="project_more",
    )(total, one, two, w_one, w_two)


def last_kernel(at_ref, sum_ref, *refs):
    att, w_ref, sent_ref, mine_ref = refs[:-3], refs[-3], refs[-2], refs[-1]
    left = at_ref[1] == 0
    count = sum_ref.shape[0]
    rows = sum_ref[...] + jnp.dot(att[0][:count], w_ref[...], preferred_element_type=F32)
    one, two = rows[:, :WIDTH], rows[:, WIDTH:]
    mine_ref[:count] = jnp.where(left, one, two)
    sent_ref[:count] = jnp.where(left, two, one).astype(BF16)
    if len(att) > 1:
        at = pl.ds(pl.multiple_of(count + at_ref[0] * (2 * TXTR), 2 * TXTR), 2 * TXTR)
        text = sum(a[at].astype(F32) for a in att)
        mine = jnp.where(left, text[:TXTR], text[TXTR:])
        sent = jnp.where(left, text[TXTR:], text[:TXTR])
        mine_ref[count:] = jnp.concatenate([mine, mine], axis=0)
        sent_ref[count:] = jnp.concatenate([sent, sent], axis=0).astype(BF16)


def project_last(at, total, att, weight):
    rows = total.shape[0] + (2 * TXTR if len(att) > 1 else 0)
    return pl.pallas_call(
        last_kernel,
        in_specs=[SMEM] + [VMEM] * (2 + len(att)),
        out_specs=[VMEM] * 2,
        out_shape=[jax.ShapeDtypeStruct((rows, WIDTH), BF16), jax.ShapeDtypeStruct((rows, WIDTH), F32)],
        compiler_params=params(),
        cost_estimate=pl.CostEstimate(flops=10**9, bytes_accessed=5 * 10**6, transcendentals=0),
        name="project_last",
    )(at, total, *att, weight)


def residual_kernel(
    own_a, got_a, own_b, got_b, xv_ref, xt_ref, mv_ref, mt_ref, xv_out, xt_out, res_ref, sums_ref
):
    gate = mv_ref[:1]
    upper = xv_ref[:UPPER].astype(F32) + gate * (own_a[...] + got_a[...].astype(F32))
    lower = xv_ref[UPPER:].astype(F32) + gate * (own_b[:LOWER] + got_b[:LOWER].astype(F32))
    text_proj = own_b[LOWER:] + got_b[LOWER:].astype(F32)
    text = xt_ref[...].astype(F32) + mt_ref[:1] * text_proj[:TXTR]
    xv_out[:UPPER] = upper.astype(BF16)
    xv_out[UPPER:] = lower.astype(BF16)
    xt_out[...] = text.astype(BF16)
    rows = jnp.concatenate([upper, lower, text], axis=0)
    res_ref[...] = rows
    count = VID + TXTR
    lane = lax.broadcasted_iota(jnp.int32, (count, 128), 1)
    sums = jnp.where(
        lane == 0,
        jnp.sum(rows, axis=1, keepdims=True),
        jnp.where(lane == 1, jnp.sum(rows * rows, axis=1, keepdims=True), 0.0),
    )
    sums = jnp.concatenate([sums, jnp.zeros((SUM_ROWS - count, 128), F32)], axis=0)
    sums_ref[...] = sums.T[:8]


def norm_kernel(res_ref, mv_ref, mt_ref, s0_ref, s1_ref, s2_ref, s3_ref, video_out, text_out):
    sums = (s0_ref[...] + s1_ref[...]) + (s2_ref[...] + s3_ref[...])
    sums = jnp.concatenate([sums, jnp.zeros((120, SUM_ROWS), F32)], axis=0).T
    mean = sums[: VID + TXTR, :1] / MODEL_WIDTH
    var = sums[: VID + TXTR, 1:2] / MODEL_WIDTH - mean * mean
    normed = (res_ref[...] - mean) * lax.rsqrt(var + 1e-06)
    video_out[...] = (normed[:VID] * (1.0 + mv_ref[2:3]) + mv_ref[1:2]).astype(BF16)
    text_out[...] = (normed[VID:] * (1.0 + mt_ref[2:3]) + mt_ref[1:2]).astype(BF16)


def local(
    q_video, k_video, video_value_rows, q_text, k_text, v_text, x_video, x_text, out_video, out_text, mod_video, mod_text
):
    def over_seq(move):
        pairs = []
        for y in range(2):
            for z in range(8):
                for c in range(2):
                    a, b, d = move(y, z, c)
                    pairs.append(((y * 8 + z) * 2 + c, ((a % 2) * 8 + b % 8) * 2 + d % 2))
        return lambda value: lax.ppermute(value, "seq", pairs)

    def over_head(move):
        pairs = []
        for x in range(4):
            for y in range(2):
                a, b = move(x, y)
                pairs.append((x * 2 + y, (a % 4) * 2 + b % 2))
        return lambda value: lax.ppermute(value, "head", pairs)

    other_core = over_seq(lambda y, z, c: (y, z, 1 - c))
    other_plane = over_seq(lambda y, z, c: (1 - y, z, c))
    up = over_seq(lambda y, z, c: (y, z + 1, c))
    down = over_seq(lambda y, z, c: (y, z - 1, c))
    across = over_seq(lambda y, z, c: (1 - y, z - 1, c))
    from_on = [None] + [over_head(lambda x, y, k=k: (x - k, y)) for k in (1, 2, 3)]
    pair = over_head(lambda x, y: (x, 1 - y))

    head = lax.axis_index("head")
    x_at = head // 2
    at = jnp.stack([x_at, head % 2]).astype(jnp.int32)

    own = jnp.concatenate(
        [
            jnp.concatenate([k_video, video_value_rows], axis=1),
            jnp.concatenate([k_text, v_text], axis=1),
            jnp.zeros((BLOCK - KB - TXTR, 2 * WIDTH), BF16),
        ],
        axis=0,
    )
    q_other = other_core(jnp.concatenate([q_video, q_text], axis=0))
    y0, r1, l1 = other_plane(own), up(own), down(own)
    r2, l2 = up(r1), down(l1)
    yr1, yl1 = other_plane(r1), other_plane(l1)
    r3, l3 = up(r2), down(l2)
    ry2, ly2 = up(yr1), down(yl1)
    r4, opposite = up(r3), across(l3)
    ry3, ly3 = up(ry2), down(ly2)

    here, slice_1 = column_slices(at, out_video, (0, 1))
    weights = [here, from_on[1](slice_1)]
    for k in (2, 3):
        [slice_k] = column_slices(at, out_video, (k,), unread=weights[k - 1 :])
        weights.append(from_on[k](slice_k))

    q_theirs = jnp.concatenate(
        [q_other[:VID], q_text, q_other[VID:], jnp.zeros((THEIRS - VID - 2 * TXTR, WIDTH), BF16)], axis=0
    )
    queries = [q_theirs, q_video]
    states = attend(queries, [own, r1, l1, y0])
    states = attend(queries, [r2, l2], states)
    states = attend(queries, [yr1, yl1], states, unread=weights[1:2])
    states = attend(queries, [r3, l3], states, unread=weights[2:3])
    states = attend(queries, [ry2, ly2], states)
    states = attend(queries, [r4, opposite], states)
    every = [ry3, ly3, own, r1, l1, y0, r2, l2, yr1, yl1, r3, l3, ry2, ly2, r4, opposite]
    *theirs, sent = attend(queries[:1], [ry3, ly3], states[:2], every=every, unread=weights[3:], send=True)
    got = other_core(sent)
    mine = attend(queries[1:], [ry3, ly3], states[2:], every=every)

    upper, lower = combine(mine, theirs, got, out_text)
    upper_1, upper_3 = from_on[1](upper), from_on[3](upper)
    lower_1, lower_3 = from_on[1](lower), from_on[3](lower)
    upper_2, lower_2 = from_on[1](upper_1), from_on[3](lower_3)
    sum_a, sum_b = project_own(upper, lower, weights[0])
    sum_a = project_more(sum_a, upper_1, upper_3, weights[1], weights[3])
    sent_a, own_a = project_last(at, sum_a, [upper_2], weights[2])
    got_a = pair(sent_a)
    sum_b = project_more(sum_b, lower_1, lower_3, weights[1], weights[3])
    sent_b, own_b = project_last(at, sum_b, [lower_2, lower, lower_1, lower_3], weights[2])
    got_b = pair(sent_b)

    x_video_out, x_text_out, residual, sums = pl.pallas_call(
        residual_kernel,
        in_specs=[VMEM] * 8,
        out_specs=[VMEM] * 4,
        out_shape=[
            jax.ShapeDtypeStruct((VID, WIDTH), BF16),
            jax.ShapeDtypeStruct((TXTR, WIDTH), BF16),
            jax.ShapeDtypeStruct((VID + TXTR, WIDTH), F32),
            jax.ShapeDtypeStruct((8, SUM_ROWS), F32),
        ],
        compiler_params=params(),
        name="residual",
    )(own_a, got_a, own_b, got_b, x_video, x_text, mod_video, mod_text)
    sums = sums + pair(sums)
    mlp_video_in, mlp_text_in = pl.pallas_call(
        norm_kernel,
        in_specs=[VMEM] * 7,
        out_specs=[VMEM] * 2,
        out_shape=[jax.ShapeDtypeStruct((VID, WIDTH), BF16), jax.ShapeDtypeStruct((TXTR, WIDTH), BF16)],
        compiler_params=params(),
        name="norm",
    )(residual, mod_video, mod_text, sums, *[from_on[k](sums) for k in (1, 2, 3)])
    return x_video_out, mlp_video_in, x_text_out, mlp_text_in


def solution(mesh):
    tokens, rows, columns = P("seq", "head"), P("head", None), P(None, "head")
    return jax.shard_map(
        local,
        mesh=mesh,
        in_specs=(tokens,) * 8 + (rows, rows, columns, columns),
        out_specs=(tokens,) * 4,
        check_vma=False,
    )
```

```python
import functools
import math

import jax
import jax.numpy as jnp
from jax import lax
from jax.experimental import pallas as pl
from jax.experimental.pallas import tpu as pltpu
from jax.sharding import PartitionSpec as P

MODEL_WIDTH = 3072
DH = 128
HERE = 3
WIDTH = HERE * DH
VID = 896
UPPER, LOWER = 480, 416
TXTR = 8
THEIRS = VID + 128
ACC = 144
KB = 256
BLOCK = KB + 16
CHUNKS = MODEL_WIDTH // WIDTH
SUM_ROWS = 1024
SCALE = math.log2(math.e) / math.sqrt(DH)
LIMIT = 1e30
NT = (((1,), (1,)), ((), ()))
F32, BF16 = jnp.float32, jnp.bfloat16
VMEM = pl.BlockSpec(memory_space=pltpu.VMEM)
SMEM = pl.BlockSpec(memory_space=pltpu.SMEM)
ANY = pl.BlockSpec(memory_space=pl.ANY)
HBM = pl.BlockSpec(memory_space=pltpu.HBM)


def params():
    return pltpu.CompilerParams(vmem_limit_bytes=30 * 2**20)


def with_ones(v):
    return jnp.concatenate([v.T, jnp.ones((ACC - DH, v.shape[0]), BF16)], axis=0)


def scores_of(k, q):
    return lax.dot_general(k, q, NT, preferred_element_type=F32) * SCALE


def rows_of(refs, columns):
    return [r[:KB, columns] for r in refs]


def text_of(refs, columns):
    rows = [r[KB:, columns].astype(F32)[:TXTR] for r in refs]
    return jnp.concatenate(rows, axis=0).astype(BF16)


def safe_head(q, keys, values, acc, top):
    for k, v in zip(keys, values, strict=True):
        s = scores_of(k, q)
        new_top = jnp.maximum(top, jnp.max(s, axis=0, keepdims=True))
        p = jnp.exp2(s - new_top).astype(BF16)
        acc = acc * jnp.exp2(top - new_top) + jnp.dot(with_ones(v), p, preferred_element_type=F32)
        top = new_top
    return acc, top


def columns_of(head):
    at = head * DH if isinstance(head, int) else pl.multiple_of(head * DH, DH)
    return pl.ds(at, DH), pl.ds(WIDTH + at, DH)


def attend_kernel(groups, n, texts, first, unread, send, *refs):
    q_refs, refs = refs[:groups], refs[groups:]
    blocks, text_blocks = refs[:n], refs[:texts]
    refs = refs[max(n, texts) + unread :]
    before, after = (None, refs) if first else (refs[: 2 * groups], refs[2 * groups :])

    def text_operands(h):
        key_at, value_at = columns_of(h)
        if not texts:
            return [], []
        return [text_of(text_blocks, key_at)], [text_of(text_blocks, value_at)]

    added, tops = {}, {}
    for h in range(HERE):
        key_at, value_at = columns_of(h)
        keys, values = rows_of(blocks, key_at), rows_of(blocks, value_at)
        pairs = [(keys[i : i + 2], values[i : i + 2]) for i in range(0, n, 2)]
        if texts:
            pairs.append(text_operands(h))
        for g in range(groups):
            q = q_refs[g][:, key_at]
            if first:
                top = jnp.max(scores_of(keys[0][:32], q), axis=0, keepdims=True)
            else:
                top = before[2 * g + 1][h, :1]
            total = None
            for k, v in pairs:
                p = jnp.exp2(scores_of(jnp.concatenate(k, axis=0), q) - top).astype(BF16)
                d = jnp.dot(with_ones(jnp.concatenate(v, axis=0)), p, preferred_element_type=F32)
                total = d if total is None else total + d
            added[g, h], tops[g, h] = total, top
    fine = jnp.max(jnp.concatenate([a[DH : DH + 1] for a in added.values()], axis=1)) < LIMIT

    @pl.when(fine)
    def _():
        for (g, h), total in added.items():
            after[2 * g][h] = total if first else before[2 * g][h] + total
            after[2 * g + 1][h] = jnp.broadcast_to(tops[g, h], (8, total.shape[1]))

    @pl.when(jnp.logical_not(fine))
    def _():
        @pl.loop(0, HERE)
        def _(h):
            key_at, value_at = columns_of(h)
            for g in range(groups):

                @pl.loop(0, q_refs[g].shape[0] // 128)
                def _(i):
                    lanes = pl.ds(pl.multiple_of(i * 128, 128), 128)
                    more_keys, more_values = text_operands(h)
                    if first:
                        acc, top = jnp.zeros((ACC, 128), F32), jnp.full((1, 128), -1e30, F32)
                    else:
                        acc, top = before[2 * g][h, :, lanes], before[2 * g + 1][h, :1, lanes]
                    acc, top = safe_head(
                        q_refs[g][lanes, key_at],
                        rows_of(blocks, key_at) + more_keys,
                        rows_of(blocks, value_at) + more_values,
                        acc,
                        top,
                    )
                    after[2 * g][h, :, lanes] = acc
                    after[2 * g + 1][h, :, lanes] = jnp.broadcast_to(top, (8, 128))

    if send:
        acc_ref, top_ref, sent_ref = after
        row = lax.broadcasted_iota(jnp.int32, (ACC - DH, acc_ref.shape[2]), 0)

        @pl.loop(0, HERE)
        def _(h):
            total = acc_ref[h, DH : DH + 1]
            inverse = 1.0 / total
            level = top_ref[h, :1] + jnp.log2(total)
            hi = level.astype(BF16).astype(F32)
            mid = (level - hi).astype(BF16).astype(F32)
            low = level - hi - mid
            levels = jnp.where(row == 0, hi, jnp.where(row == 1, mid, jnp.where(row == 2, low, 0.0)))
            sent_ref[h, :DH] = (acc_ref[h, :DH] * inverse).astype(BF16)
            sent_ref[h, DH:] = levels.astype(BF16)


def attend(queries, blocks, states=None, every=(), unread=(), send=False):
    n, texts, groups = len(blocks), len(every), len(queries)
    blocks = [*blocks, *[b for b in every if all(b is not c for c in blocks)]]
    keys = n * KB + texts * TXTR
    lanes = sum(q.shape[0] for q in queries)
    out_shape = []
    for q in queries:
        out_shape.append(jax.ShapeDtypeStruct((HERE, ACC, q.shape[0]), F32))
        out_shape.append(jax.ShapeDtypeStruct((HERE, 8, q.shape[0]), F32))
    if send:
        out_shape.append(jax.ShapeDtypeStruct((HERE, ACC, queries[0].shape[0]), BF16))
    first = states is None
    states = [] if first else states
    before = groups + len(blocks) + len(unread)
    return pl.pallas_call(
        functools.partial(attend_kernel, groups, n, texts, first, len(unread), send),
        in_specs=[VMEM] * (groups + len(blocks)) + [ANY] * len(unread) + [VMEM] * len(states),
        out_specs=[VMEM] * len(out_shape),
        out_shape=out_shape,
        input_output_aliases={before + i: i for i in range(len(states))},
        compiler_params=params(),
        cost_estimate=pl.CostEstimate(
            flops=HERE * lanes * keys * DH * 8,
            bytes_accessed=HERE * ACC * lanes * 4,
            transcendentals=HERE * lanes * keys,
        ),
        name="attend",
    )(*queries, *blocks, *unread, *states)


def merged(acc, top, got):
    total = acc[DH : DH + 1]
    mine = top + jnp.log2(total)
    theirs = got[DH : DH + 1] + got[DH + 1 : DH + 2] + got[DH + 2 : DH + 3]
    share = 1.0 / (1.0 + jnp.exp2(theirs - mine))
    other = 1.0 / (1.0 + jnp.exp2(mine - theirs))
    return acc[:DH] * (share / total) + got[:DH] * other


def combine_kernel(
    acc_ref, top_ref, text_acc, text_top, got_ref, w_hbm, upper_ref, lower_ref, w_ref, rows_ref, sem
):
    copy = pltpu.make_async_copy(w_hbm, w_ref, sem)
    copy.start()

    @pl.loop(0, HERE)
    def _(h):
        at, _ = columns_of(h)
        video = merged(acc_ref[h], top_ref[h, :1], got_ref[h, :, :VID].astype(F32)).T.astype(BF16)
        upper_ref[:, at] = video[:UPPER]
        lower_ref[:LOWER, at] = video[UPPER:]
        got = pltpu.roll(got_ref[h, :, VID:].astype(F32), DH - TXTR, 1)
        rows = merged(text_acc[h, :, VID:], text_top[h, :1, VID:], got).T
        rows_ref[:, at] = rows[: 2 * TXTR].astype(BF16)

    copy.wait()
    part = jnp.dot(rows_ref[...], w_ref[...], preferred_element_type=F32)[:TXTR]
    chunks = [part[:, j * WIDTH : (j + 1) * WIDTH] for j in range(CHUNKS)]
    lower_ref[LOWER:] = jnp.concatenate(chunks, axis=0).astype(BF16)


def combine(own, theirs, got, out_text):
    return pl.pallas_call(
        combine_kernel,
        in_specs=[VMEM] * 5 + [HBM],
        out_specs=[VMEM] * 2,
        out_shape=[
            jax.ShapeDtypeStruct((UPPER, WIDTH), BF16),
            jax.ShapeDtypeStruct((LOWER + CHUNKS * TXTR, WIDTH), BF16),
        ],
        scratch_shapes=[
            pltpu.VMEM((WIDTH, MODEL_WIDTH), BF16),
            pltpu.VMEM((2 * TXTR, WIDTH), BF16),
            pltpu.SemaphoreType.DMA(()),
        ],
        compiler_params=params(),
        cost_estimate=pl.CostEstimate(flops=10**9, bytes_accessed=10**7, transcendentals=0),
        name="combine",
    )(*own, *theirs, got, out_text)


def slice_kernel(steps, unread, at_ref, w_ref, *refs):
    out_refs, sems = refs[unread : unread + len(steps)], refs[unread + len(steps) :]
    copies = []
    for k, out_ref, sem in zip(steps, out_refs, sems, strict=True):
        first = lax.rem(at_ref[0] + 4 - k, 4) * (2 * WIDTH)
        columns = pl.ds(pl.multiple_of(first, 2 * WIDTH), 2 * WIDTH)
        copies.append(pltpu.make_async_copy(w_ref.at[:, columns], out_ref, sem))
        copies[-1].start()
    for copy in copies:
        copy.wait()


def column_slices(at, weight, steps, unread=()):
    return pl.pallas_call(
        functools.partial(slice_kernel, steps, len(unread)),
        in_specs=[SMEM, HBM] + [ANY] * len(unread),
        out_specs=[VMEM] * len(steps),
        out_shape=[jax.ShapeDtypeStruct((WIDTH, 2 * WIDTH), BF16)] * len(steps),
        scratch_shapes=[pltpu.SemaphoreType.DMA(())] * len(steps),
        compiler_params=params(),
        name="columns",
    )(at, weight, *unread)


def own_kernel(arrived_ref, upper_ref, lower_ref, w_ref, upper_out, lower_out, again_ref):
    del arrived_ref
    again_ref[...] = lower_ref[...]
    upper_out[...] = jnp.dot(upper_ref[...], w_ref[...], preferred_element_type=F32)
    lower_out[...] = jnp.dot(lower_ref[:LOWER], w_ref[...], preferred_element_type=F32)


def project_own(arrived, upper, lower, weight):
    return pl.pallas_call(
        own_kernel,
        in_specs=[ANY] + [VMEM] * 3,
        out_specs=[VMEM] * 3,
        out_shape=[
            *[jax.ShapeDtypeStruct((rows, 2 * WIDTH), F32) for rows in (UPPER, LOWER)],
            jax.ShapeDtypeStruct(lower.shape, BF16),
        ],
        compiler_params=params(),
        cost_estimate=pl.CostEstimate(flops=10**9, bytes_accessed=5 * 10**6, transcendentals=0),
        name="project_own",
    )(arrived, upper, lower, weight)


def more_kernel(sum_ref, one_ref, two_ref, w_one, w_two, out_ref):
    rows = sum_ref.shape[0]
    out_ref[...] = (
        sum_ref[...]
        + jnp.dot(one_ref[:rows], w_one[...], preferred_element_type=F32)
        + jnp.dot(two_ref[:rows], w_two[...], preferred_element_type=F32)
    )


def project_more(total, one, two, w_one, w_two):
    return pl.pallas_call(
        more_kernel,
        in_specs=[VMEM] * 5,
        out_specs=VMEM,
        out_shape=jax.ShapeDtypeStruct(total.shape, F32),
        input_output_aliases={0: 0},
        compiler_params=params(),
        cost_estimate=pl.CostEstimate(flops=10**9, bytes_accessed=5 * 10**6, transcendentals=0),
        name="project_more",
    )(total, one, two, w_one, w_two)


def last_kernel(at_ref, sum_ref, *refs):
    att, w_ref, sent_ref, mine_ref = refs[:-3], refs[-3], refs[-2], refs[-1]
    left = at_ref[1] == 0
    count = sum_ref.shape[0]
    rows = sum_ref[...] + jnp.dot(att[0][:count], w_ref[...], preferred_element_type=F32)
    one, two = rows[:, :WIDTH], rows[:, WIDTH:]
    mine_ref[:count] = jnp.where(left, one, two)
    sent_ref[:count] = jnp.where(left, two, one).astype(BF16)
    if len(att) > 1:
        at = pl.ds(pl.multiple_of(count + at_ref[0] * (2 * TXTR), 2 * TXTR), 2 * TXTR)
        text = sum(a[at].astype(F32) for a in att)
        mine = jnp.where(left, text[:TXTR], text[TXTR:])
        sent = jnp.where(left, text[TXTR:], text[:TXTR])
        mine_ref[count:] = jnp.concatenate([mine, mine], axis=0)
        sent_ref[count:] = jnp.concatenate([sent, sent], axis=0).astype(BF16)


def project_last(at, total, att, weight):
    rows = total.shape[0] + (2 * TXTR if len(att) > 1 else 0)
    return pl.pallas_call(
        last_kernel,
        in_specs=[SMEM] + [VMEM] * (2 + len(att)),
        out_specs=[VMEM] * 2,
        out_shape=[jax.ShapeDtypeStruct((rows, WIDTH), BF16), jax.ShapeDtypeStruct((rows, WIDTH), F32)],
        compiler_params=params(),
        cost_estimate=pl.CostEstimate(flops=10**9, bytes_accessed=5 * 10**6, transcendentals=0),
        name="project_last",
    )(at, total, *att, weight)


def residual_kernel(
    own_a, got_a, own_b, got_b, xv_ref, xt_ref, mv_ref, mt_ref, xv_out, xt_out, res_ref, sums_ref
):
    gate = mv_ref[:1]
    upper = xv_ref[:UPPER].astype(F32) + gate * (own_a[...] + got_a[...].astype(F32))
    lower = xv_ref[UPPER:].astype(F32) + gate * (own_b[:LOWER] + got_b[:LOWER].astype(F32))
    text_proj = own_b[LOWER:] + got_b[LOWER:].astype(F32)
    text = xt_ref[...].astype(F32) + mt_ref[:1] * text_proj[:TXTR]
    xv_out[:UPPER] = upper.astype(BF16)
    xv_out[UPPER:] = lower.astype(BF16)
    xt_out[...] = text.astype(BF16)
    rows = jnp.concatenate([upper, lower, text], axis=0)
    res_ref[...] = rows
    count = VID + TXTR
    lane = lax.broadcasted_iota(jnp.int32, (count, 128), 1)
    sums = jnp.where(
        lane == 0,
        jnp.sum(rows, axis=1, keepdims=True),
        jnp.where(lane == 1, jnp.sum(rows * rows, axis=1, keepdims=True), 0.0),
    )
    sums = jnp.concatenate([sums, jnp.zeros((SUM_ROWS - count, 128), F32)], axis=0)
    sums_ref[...] = sums.T[:8]


def norm_kernel(res_ref, mv_ref, mt_ref, s0_ref, s1_ref, s2_ref, s3_ref, video_out, text_out):
    sums = (s0_ref[...] + s1_ref[...]) + (s2_ref[...] + s3_ref[...])
    sums = jnp.concatenate([sums, jnp.zeros((120, SUM_ROWS), F32)], axis=0).T
    mean = sums[: VID + TXTR, :1] / MODEL_WIDTH
    var = sums[: VID + TXTR, 1:2] / MODEL_WIDTH - mean * mean
    normed = (res_ref[...] - mean) * lax.rsqrt(var + 1e-06)
    video_out[...] = (normed[:VID] * (1.0 + mv_ref[2:3]) + mv_ref[1:2]).astype(BF16)
    text_out[...] = (normed[VID:] * (1.0 + mt_ref[2:3]) + mt_ref[1:2]).astype(BF16)


def local(
    q_video, k_video, video_value_rows, q_text, k_text, v_text, x_video, x_text, out_video, out_text, mod_video, mod_text
):
    def over_seq(move):
        pairs = []
        for y in range(2):
            for z in range(8):
                for c in range(2):
                    a, b, d = move(y, z, c)
                    pairs.append(((y * 8 + z) * 2 + c, ((a % 2) * 8 + b % 8) * 2 + d % 2))
        return lambda value: lax.ppermute(value, "seq", pairs)

    def over_head(move):
        pairs = []
        for x in range(4):
            for y in range(2):
                a, b = move(x, y)
                pairs.append((x * 2 + y, (a % 4) * 2 + b % 2))
        return lambda value: lax.ppermute(value, "head", pairs)

    other_core = over_seq(lambda y, z, c: (y, z, 1 - c))
    other_plane = over_seq(lambda y, z, c: (1 - y, z, c))
    up = over_seq(lambda y, z, c: (y, z + 1, c))
    down = over_seq(lambda y, z, c: (y, z - 1, c))
    across = over_seq(lambda y, z, c: (1 - y, z - 1, c))
    from_on = [None] + [over_head(lambda x, y, k=k: (x - k, y)) for k in (1, 2, 3)]
    pair = over_head(lambda x, y: (x, 1 - y))

    head = lax.axis_index("head")
    x_at = head // 2
    at = jnp.stack([x_at, head % 2]).astype(jnp.int32)

    own = jnp.concatenate(
        [
            jnp.concatenate([k_video, video_value_rows], axis=1),
            jnp.concatenate([k_text, v_text], axis=1),
            jnp.zeros((BLOCK - KB - TXTR, 2 * WIDTH), BF16),
        ],
        axis=0,
    )
    q_other = other_core(jnp.concatenate([q_video, q_text], axis=0))
    y0, r1, l1 = other_plane(own), up(own), down(own)
    r2, l2 = up(r1), down(l1)
    yr1, yl1 = other_plane(r1), other_plane(l1)
    r3, l3 = up(r2), down(l2)
    ry2, ly2 = up(yr1), down(yl1)
    r4, opposite = up(r3), across(l3)
    ry3, ly3 = up(ry2), down(ly2)

    slice_1 = lax.dynamic_slice_in_dim(out_video, lax.rem(x_at + 3, 4) * 2 * WIDTH, 2 * WIDTH, axis=1)
    weight_1 = from_on[1](slice_1)
    here, slice_2 = column_slices(at, out_video, (0, 2), unread=[weight_1])
    weight_2 = from_on[2](slice_2)
    [slice_3] = column_slices(at, out_video, (3,), unread=[weight_2])
    weights = [here, weight_1, weight_2, from_on[3](slice_3)]

    q_theirs = jnp.concatenate(
        [q_other[:VID], q_text, q_other[VID:], jnp.zeros((THEIRS - VID - 2 * TXTR, WIDTH), BF16)], axis=0
    )
    queries = [q_theirs, q_video]
    states = attend(queries, [own, r1, l1, y0])
    states = attend(queries, [r2, l2, yr1, yl1], states, unread=weights[1:2])
    states = attend(queries, [r3, l3, ry2, ly2], states, unread=weights[2:3])
    states = attend(queries, [r4, opposite], states)
    every = [ry3, ly3, own, r1, l1, y0, r2, l2, yr1, yl1, r3, l3, ry2, ly2, r4, opposite]
    *theirs, sent = attend(queries[:1], [ry3, ly3], states[:2], every=every, unread=weights[3:], send=True)
    got = other_core(sent)
    mine = attend(queries[1:], [ry3, ly3], states[2:], every=every)

    upper, lower = combine(mine, theirs, got, out_text)
    upper_1, upper_3, lower_3 = from_on[1](upper), from_on[3](upper), from_on[3](lower)
    upper_2 = from_on[1](upper_1)
    sum_a, sum_b, lower_again = project_own(upper_1, upper, lower, weights[0])
    lower_1, lower_2 = from_on[1](lower_again), from_on[3](lower_3)
    sum_a = project_more(sum_a, upper_1, upper_3, weights[1], weights[3])
    sent_a, own_a = project_last(at, sum_a, [upper_2], weights[2])
    got_a = pair(sent_a)
    sum_b = project_more(sum_b, lower_1, lower_3, weights[1], weights[3])
    sent_b, own_b = project_last(at, sum_b, [lower_2, lower, lower_1, lower_3], weights[2])
    got_b = pair(sent_b)

    x_video_out, x_text_out, residual, sums = pl.pallas_call(
        residual_kernel,
        in_specs=[VMEM] * 8,
        out_specs=[VMEM] * 4,
        out_shape=[
            jax.ShapeDtypeStruct((VID, WIDTH), BF16),
            jax.ShapeDtypeStruct((TXTR, WIDTH), BF16),
            jax.ShapeDtypeStruct((VID + TXTR, WIDTH), F32),
            jax.ShapeDtypeStruct((8, SUM_ROWS), F32),
        ],
        compiler_params=params(),
        name="residual",
    )(own_a, got_a, own_b, got_b, x_video, x_text, mod_video, mod_text)
    sums = sums + pair(sums)
    mlp_video_in, mlp_text_in = pl.pallas_call(
        norm_kernel,
        in_specs=[VMEM] * 7,
        out_specs=[VMEM] * 2,
        out_shape=[jax.ShapeDtypeStruct((VID, WIDTH), BF16), jax.ShapeDtypeStruct((TXTR, WIDTH), BF16)],
        compiler_params=params(),
        name="norm",
    )(residual, mod_video, mod_text, sums, *[from_on[k](sums) for k in (1, 2, 3)])
    return x_video_out, mlp_video_in, x_text_out, mlp_text_in


def solution(mesh):
    tokens, rows, columns = P("seq", "head"), P("head", None), P(None, "head")
    return jax.shard_map(
        local,
        mesh=mesh,
        in_specs=(tokens,) * 8 + (rows, rows, columns, columns),
        out_specs=(tokens,) * 4,
        check_vma=False,
    )
```

```python
import functools
import math

import jax
import jax.numpy as jnp
from jax import lax
from jax.experimental import pallas as pl
from jax.experimental.pallas import tpu as pltpu
from jax.sharding import PartitionSpec as P

MODEL_WIDTH = 3072
DH = 128
HERE = 3
WIDTH = HERE * DH
VID = 896
UPPER, LOWER = 480, 416
TXTR = 8
THEIRS = VID + 128
ACC = 144
KB = 256
BLOCK = KB + 16
CHUNKS = MODEL_WIDTH // WIDTH
SUM_ROWS = 1024
SCALE = math.log2(math.e) / math.sqrt(DH)
LIMIT = 1e30
NT = (((1,), (1,)), ((), ()))
F32, BF16 = jnp.float32, jnp.bfloat16
VMEM = pl.BlockSpec(memory_space=pltpu.VMEM)
SMEM = pl.BlockSpec(memory_space=pltpu.SMEM)
ANY = pl.BlockSpec(memory_space=pl.ANY)
HBM = pl.BlockSpec(memory_space=pltpu.HBM)


def params(mib=30):
    return pltpu.CompilerParams(vmem_limit_bytes=mib * 2**20)


def with_ones(v):
    return jnp.concatenate([v.T, jnp.ones((ACC - DH, v.shape[0]), BF16)], axis=0)


def scores_of(k, q):
    return lax.dot_general(k, q, NT, preferred_element_type=F32) * SCALE


def rows_of(refs, columns):
    return [r[:KB, columns] for r in refs]


def text_of(refs, columns):
    rows = [r[KB:, columns].astype(F32)[:TXTR] for r in refs]
    return jnp.concatenate(rows, axis=0).astype(BF16)


def safe_head(q, keys, values, acc, top):
    for k, v in zip(keys, values, strict=True):
        s = scores_of(k, q)
        new_top = jnp.maximum(top, jnp.max(s, axis=0, keepdims=True))
        p = jnp.exp2(s - new_top).astype(BF16)
        acc = acc * jnp.exp2(top - new_top) + jnp.dot(with_ones(v), p, preferred_element_type=F32)
        top = new_top
    return acc, top


def columns_of(head):
    at = head * DH if isinstance(head, int) else pl.multiple_of(head * DH, DH)
    return pl.ds(at, DH), pl.ds(WIDTH + at, DH)


def attend_kernel(groups, n, texts, first, unread, send, *refs):
    q_refs, refs = refs[:groups], refs[groups:]
    blocks, text_blocks = refs[:n], refs[:texts]
    refs = refs[max(n, texts) + unread :]
    before, after = (None, refs) if first else (refs[: 2 * groups], refs[2 * groups :])

    def text_operands(h):
        key_at, value_at = columns_of(h)
        if not texts:
            return [], []
        return [text_of(text_blocks, key_at)], [text_of(text_blocks, value_at)]

    added, tops = {}, {}
    for h in range(HERE):
        key_at, value_at = columns_of(h)
        keys, values = rows_of(blocks, key_at), rows_of(blocks, value_at)
        pairs = [(keys[i : i + 2], values[i : i + 2]) for i in range(0, n, 2)]
        if texts:
            pairs.append(text_operands(h))
        for g in range(groups):
            q = q_refs[g][:, key_at]
            top = jnp.zeros((1, q.shape[0]), F32) if first else before[2 * g + 1][h, :1]
            total = None
            for k, v in pairs:
                p = jnp.exp2(scores_of(jnp.concatenate(k, axis=0), q) - top).astype(BF16)
                d = jnp.dot(with_ones(jnp.concatenate(v, axis=0)), p, preferred_element_type=F32)
                total = d if total is None else total + d
            added[g, h], tops[g, h] = total, top
    totals = jnp.concatenate([a[DH : DH + 1] for a in added.values()], axis=1)
    fine = jnp.max(totals) < LIMIT
    if first:
        fine = jnp.logical_and(fine, jnp.min(totals) > 1e-20)

    @pl.when(fine)
    def _():
        for (g, h), total in added.items():
            after[2 * g][h] = total if first else before[2 * g][h] + total
            after[2 * g + 1][h] = jnp.broadcast_to(tops[g, h], (8, total.shape[1]))

    @pl.when(jnp.logical_not(fine))
    def _():
        @pl.loop(0, HERE)
        def _(h):
            key_at, value_at = columns_of(h)
            for g in range(groups):

                @pl.loop(0, q_refs[g].shape[0] // 128)
                def _(i):
                    lanes = pl.ds(pl.multiple_of(i * 128, 128), 128)
                    more_keys, more_values = text_operands(h)
                    if first:
                        acc, top = jnp.zeros((ACC, 128), F32), jnp.full((1, 128), -1e30, F32)
                    else:
                        acc, top = before[2 * g][h, :, lanes], before[2 * g + 1][h, :1, lanes]
                    acc, top = safe_head(
                        q_refs[g][lanes, key_at],
                        rows_of(blocks, key_at) + more_keys,
                        rows_of(blocks, value_at) + more_values,
                        acc,
                        top,
                    )
                    after[2 * g][h, :, lanes] = acc
                    after[2 * g + 1][h, :, lanes] = jnp.broadcast_to(top, (8, 128))

    if send:
        acc_ref, top_ref, sent_ref = after
        row = lax.broadcasted_iota(jnp.int32, (ACC - DH, acc_ref.shape[2]), 0)

        @pl.loop(0, HERE)
        def _(h):
            total = acc_ref[h, DH : DH + 1]
            inverse = 1.0 / total
            level = top_ref[h, :1] + jnp.log2(total)
            hi = level.astype(BF16).astype(F32)
            mid = (level - hi).astype(BF16).astype(F32)
            low = level - hi - mid
            levels = jnp.where(row == 0, hi, jnp.where(row == 1, mid, jnp.where(row == 2, low, 0.0)))
            sent_ref[h, :DH] = (acc_ref[h, :DH] * inverse).astype(BF16)
            sent_ref[h, DH:] = levels.astype(BF16)


def attend(queries, blocks, states=None, every=(), unread=(), send=False):
    n, texts, groups = len(blocks), len(every), len(queries)
    blocks = [*blocks, *[b for b in every if all(b is not c for c in blocks)]]
    keys = n * KB + texts * TXTR
    lanes = sum(q.shape[0] for q in queries)
    out_shape = []
    for q in queries:
        out_shape.append(jax.ShapeDtypeStruct((HERE, ACC, q.shape[0]), F32))
        out_shape.append(jax.ShapeDtypeStruct((HERE, 8, q.shape[0]), F32))
    if send:
        out_shape.append(jax.ShapeDtypeStruct((HERE, ACC, queries[0].shape[0]), BF16))
    first = states is None
    states = [] if first else states
    before = groups + len(blocks) + len(unread)
    return pl.pallas_call(
        functools.partial(attend_kernel, groups, n, texts, first, len(unread), send),
        in_specs=[VMEM] * (groups + len(blocks)) + [ANY] * len(unread) + [VMEM] * len(states),
        out_specs=[VMEM] * len(out_shape),
        out_shape=out_shape,
        input_output_aliases={before + i: i for i in range(len(states))},
        compiler_params=params(),
        cost_estimate=pl.CostEstimate(
            flops=HERE * lanes * keys * DH * 8,
            bytes_accessed=HERE * ACC * lanes * 4,
            transcendentals=HERE * lanes * keys,
        ),
        name="attend",
    )(*queries, *blocks, *unread, *states)


def merged(acc, top, got):
    total = acc[DH : DH + 1]
    mine = top + jnp.log2(total)
    theirs = got[DH : DH + 1] + got[DH + 1 : DH + 2] + got[DH + 2 : DH + 3]
    share = 1.0 / (1.0 + jnp.exp2(theirs - mine))
    other = 1.0 / (1.0 + jnp.exp2(mine - theirs))
    return acc[:DH] * (share / total) + got[:DH] * other


def combine_kernel(
    acc_ref, top_ref, text_acc, text_top, got_ref, w_hbm, upper_ref, lower_ref, w_ref, rows_ref, sem
):
    copy = pltpu.make_async_copy(w_hbm, w_ref, sem)
    copy.start()

    @pl.loop(0, HERE)
    def _(h):
        at, _ = columns_of(h)
        video = merged(acc_ref[h], top_ref[h, :1], got_ref[h, :, :VID].astype(F32)).T.astype(BF16)
        upper_ref[:, at] = video[:UPPER]
        lower_ref[:LOWER, at] = video[UPPER:]
        got = pltpu.roll(got_ref[h, :, VID:].astype(F32), DH - TXTR, 1)
        rows = merged(text_acc[h, :, VID:], text_top[h, :1, VID:], got).T
        rows_ref[:, at] = rows[: 2 * TXTR].astype(BF16)

    copy.wait()
    part = jnp.dot(rows_ref[...], w_ref[...], preferred_element_type=F32)[:TXTR]
    chunks = [part[:, j * WIDTH : (j + 1) * WIDTH] for j in range(CHUNKS)]
    lower_ref[LOWER:] = jnp.concatenate(chunks, axis=0).astype(BF16)


def combine(own, theirs, got, out_text):
    return pl.pallas_call(
        combine_kernel,
        in_specs=[VMEM] * 5 + [HBM],
        out_specs=[VMEM] * 2,
        out_shape=[
            jax.ShapeDtypeStruct((UPPER, WIDTH), BF16),
            jax.ShapeDtypeStruct((LOWER + CHUNKS * TXTR, WIDTH), BF16),
        ],
        scratch_shapes=[
            pltpu.VMEM((WIDTH, MODEL_WIDTH), BF16),
            pltpu.VMEM((2 * TXTR, WIDTH), BF16),
            pltpu.SemaphoreType.DMA(()),
        ],
        compiler_params=params(),
        cost_estimate=pl.CostEstimate(flops=10**9, bytes_accessed=10**7, transcendentals=0),
        name="combine",
    )(*own, *theirs, got, out_text)


def slice_kernel(steps, unread, at_ref, w_ref, *refs):
    out_refs, sems = refs[unread : unread + len(steps)], refs[unread + len(steps) :]
    copies = []
    for k, out_ref, sem in zip(steps, out_refs, sems, strict=True):
        first = lax.rem(at_ref[0] + 4 - k, 4) * (2 * WIDTH)
        columns = pl.ds(pl.multiple_of(first, 2 * WIDTH), 2 * WIDTH)
        copies.append(pltpu.make_async_copy(w_ref.at[:, columns], out_ref, sem))
        copies[-1].start()
    for copy in copies:
        copy.wait()


def column_slices(at, weight, steps, unread=()):
    return pl.pallas_call(
        functools.partial(slice_kernel, steps, len(unread)),
        in_specs=[SMEM, HBM] + [ANY] * len(unread),
        out_specs=[VMEM] * len(steps),
        out_shape=[jax.ShapeDtypeStruct((WIDTH, 2 * WIDTH), BF16)] * len(steps),
        scratch_shapes=[pltpu.SemaphoreType.DMA(())] * len(steps),
        compiler_params=params(61 if len(steps) > 1 else 30),
        name="columns",
    )(at, weight, *unread)


def own_kernel(arrived_ref, upper_ref, lower_ref, w_ref, upper_out, lower_out, again_ref):
    del arrived_ref
    again_ref[...] = lower_ref[...]
    upper_out[...] = jnp.dot(upper_ref[...], w_ref[...], preferred_element_type=F32)
    lower_out[...] = jnp.dot(lower_ref[:LOWER], w_ref[...], preferred_element_type=F32)


def project_own(arrived, upper, lower, weight):
    return pl.pallas_call(
        own_kernel,
        in_specs=[ANY] + [VMEM] * 3,
        out_specs=[VMEM] * 3,
        out_shape=[
            *[jax.ShapeDtypeStruct((rows, 2 * WIDTH), F32) for rows in (UPPER, LOWER)],
            jax.ShapeDtypeStruct(lower.shape, BF16),
        ],
        compiler_params=params(),
        cost_estimate=pl.CostEstimate(flops=10**9, bytes_accessed=5 * 10**6, transcendentals=0),
        name="project_own",
    )(arrived, upper, lower, weight)


def more_kernel(sum_ref, one_ref, two_ref, w_one, w_two, out_ref):
    rows = sum_ref.shape[0]
    out_ref[...] = (
        sum_ref[...]
        + jnp.dot(one_ref[:rows], w_one[...], preferred_element_type=F32)
        + jnp.dot(two_ref[:rows], w_two[...], preferred_element_type=F32)
    )


def project_more(total, one, two, w_one, w_two):
    return pl.pallas_call(
        more_kernel,
        in_specs=[VMEM] * 5,
        out_specs=VMEM,
        out_shape=jax.ShapeDtypeStruct(total.shape, F32),
        input_output_aliases={0: 0},
        compiler_params=params(),
        cost_estimate=pl.CostEstimate(flops=10**9, bytes_accessed=5 * 10**6, transcendentals=0),
        name="project_more",
    )(total, one, two, w_one, w_two)


def last_kernel(at_ref, sum_ref, *refs):
    att, w_ref, sent_ref, mine_ref = refs[:-3], refs[-3], refs[-2], refs[-1]
    left = at_ref[1] == 0
    count = sum_ref.shape[0]
    rows = sum_ref[...] + jnp.dot(att[0][:count], w_ref[...], preferred_element_type=F32)
    one, two = rows[:, :WIDTH], rows[:, WIDTH:]
    mine_ref[:count] = jnp.where(left, one, two)
    sent_ref[:count] = jnp.where(left, two, one).astype(BF16)
    if len(att) > 1:
        at = pl.ds(pl.multiple_of(count + at_ref[0] * (2 * TXTR), 2 * TXTR), 2 * TXTR)
        text = sum(a[at].astype(F32) for a in att)
        mine = jnp.where(left, text[:TXTR], text[TXTR:])
        sent = jnp.where(left, text[TXTR:], text[:TXTR])
        mine_ref[count:] = jnp.concatenate([mine, mine], axis=0)
        sent_ref[count:] = jnp.concatenate([sent, sent], axis=0).astype(BF16)


def project_last(at, total, att, weight):
    rows = total.shape[0] + (2 * TXTR if len(att) > 1 else 0)
    return pl.pallas_call(
        last_kernel,
        in_specs=[SMEM] + [VMEM] * (2 + len(att)),
        out_specs=[VMEM] * 2,
        out_shape=[jax.ShapeDtypeStruct((rows, WIDTH), BF16), jax.ShapeDtypeStruct((rows, WIDTH), F32)],
        compiler_params=params(),
        cost_estimate=pl.CostEstimate(flops=10**9, bytes_accessed=5 * 10**6, transcendentals=0),
        name="project_last",
    )(at, total, *att, weight)


def residual_kernel(
    own_a, got_a, own_b, got_b, xv_ref, xt_ref, mv_ref, mt_ref, xv_out, xt_out, res_ref, sums_ref
):
    gate = mv_ref[:1]
    upper = xv_ref[:UPPER].astype(F32) + gate * (own_a[...] + got_a[...].astype(F32))
    lower = xv_ref[UPPER:].astype(F32) + gate * (own_b[:LOWER] + got_b[:LOWER].astype(F32))
    text_proj = own_b[LOWER:] + got_b[LOWER:].astype(F32)
    text = xt_ref[...].astype(F32) + mt_ref[:1] * text_proj[:TXTR]
    xv_out[:UPPER] = upper.astype(BF16)
    xv_out[UPPER:] = lower.astype(BF16)
    xt_out[...] = text.astype(BF16)
    rows = jnp.concatenate([upper, lower, text], axis=0)
    res_ref[...] = rows
    count = VID + TXTR
    lane = lax.broadcasted_iota(jnp.int32, (count, 128), 1)
    sums = jnp.where(
        lane == 0,
        jnp.sum(rows, axis=1, keepdims=True),
        jnp.where(lane == 1, jnp.sum(rows * rows, axis=1, keepdims=True), 0.0),
    )
    sums = jnp.concatenate([sums, jnp.zeros((SUM_ROWS - count, 128), F32)], axis=0)
    sums_ref[...] = sums.T[:8]


def norm_kernel(res_ref, mv_ref, mt_ref, s0_ref, s1_ref, s2_ref, s3_ref, video_out, text_out):
    sums = (s0_ref[...] + s1_ref[...]) + (s2_ref[...] + s3_ref[...])
    sums = jnp.concatenate([sums, jnp.zeros((120, SUM_ROWS), F32)], axis=0).T
    mean = sums[: VID + TXTR, :1] / MODEL_WIDTH
    var = sums[: VID + TXTR, 1:2] / MODEL_WIDTH - mean * mean
    normed = (res_ref[...] - mean) * lax.rsqrt(var + 1e-06)
    video_out[...] = (normed[:VID] * (1.0 + mv_ref[2:3]) + mv_ref[1:2]).astype(BF16)
    text_out[...] = (normed[VID:] * (1.0 + mt_ref[2:3]) + mt_ref[1:2]).astype(BF16)


def local(
    q_video, k_video, video_value_rows, q_text, k_text, v_text, x_video, x_text, out_video, out_text, mod_video, mod_text
):
    def over_seq(move):
        pairs = []
        for y in range(2):
            for z in range(8):
                for c in range(2):
                    a, b, d = move(y, z, c)
                    pairs.append(((y * 8 + z) * 2 + c, ((a % 2) * 8 + b % 8) * 2 + d % 2))
        return lambda value: lax.ppermute(value, "seq", pairs)

    def over_head(move):
        pairs = []
        for x in range(4):
            for y in range(2):
                a, b = move(x, y)
                pairs.append((x * 2 + y, (a % 4) * 2 + b % 2))
        return lambda value: lax.ppermute(value, "head", pairs)

    other_core = over_seq(lambda y, z, c: (y, z, 1 - c))
    other_plane = over_seq(lambda y, z, c: (1 - y, z, c))
    up = over_seq(lambda y, z, c: (y, z + 1, c))
    down = over_seq(lambda y, z, c: (y, z - 1, c))
    across = over_seq(lambda y, z, c: (1 - y, z - 1, c))
    from_on = [None] + [over_head(lambda x, y, k=k: (x - k, y)) for k in (1, 2, 3)]
    pair = over_head(lambda x, y: (x, 1 - y))

    head = lax.axis_index("head")
    x_at = head // 2
    at = jnp.stack([x_at, head % 2]).astype(jnp.int32)

    own = jnp.concatenate(
        [
            jnp.concatenate([k_video, video_value_rows], axis=1),
            jnp.concatenate([k_text, v_text], axis=1),
            jnp.zeros((BLOCK - KB - TXTR, 2 * WIDTH), BF16),
        ],
        axis=0,
    )
    q_other = other_core(jnp.concatenate([q_video, q_text], axis=0))
    y0, r1, l1 = other_plane(own), up(own), down(own)
    r2, l2 = up(r1), down(l1)
    yr1, yl1 = other_plane(r1), other_plane(l1)
    r3, l3 = up(r2), down(l2)
    ry2, ly2 = up(yr1), down(yl1)
    r4, opposite = up(r3), across(l3)
    ry3, ly3 = up(ry2), down(ly2)

    here, slice_1 = column_slices(at, out_video, (0, 1), unread=[own])
    weight_1 = from_on[1](slice_1)
    [slice_2] = column_slices(at, out_video, (2,), unread=[y0, weight_1])
    weight_2 = from_on[2](slice_2)
    [slice_3] = column_slices(at, out_video, (3,), unread=[weight_2])
    weights = [here, weight_1, weight_2, from_on[3](slice_3)]

    q_theirs = jnp.concatenate(
        [q_other[:VID], q_text, q_other[VID:], jnp.zeros((THEIRS - VID - 2 * TXTR, WIDTH), BF16)], axis=0
    )
    queries = [q_theirs, q_video]
    states = attend(queries, [own, r1, l1, y0], unread=weights[1:2])
    states = attend(queries, [r2, l2, yr1, yl1], states)
    states = attend(queries, [r3, l3, ry2, ly2], states, unread=weights[2:3])
    states = attend(queries, [r4, opposite], states)
    every = [ry3, ly3, own, r1, l1, y0, r2, l2, yr1, yl1, r3, l3, ry2, ly2, r4, opposite]
    *theirs, sent = attend(queries[:1], [ry3, ly3], states[:2], every=every, unread=weights[3:], send=True)
    got = other_core(sent)
    mine = attend(queries[1:], [ry3, ly3], states[2:], every=every)

    upper, lower = combine(mine, theirs, got, out_text)
    upper_1, upper_3, lower_3 = from_on[1](upper), from_on[3](upper), from_on[3](lower)
    upper_2 = from_on[1](upper_1)
    sum_a, sum_b, lower_again = project_own(upper_1, upper, lower, weights[0])
    lower_1, lower_2 = from_on[1](lower_again), from_on[3](lower_3)
    sum_a = project_more(sum_a, upper_1, upper_3, weights[1], weights[3])
    sent_a, own_a = project_last(at, sum_a, [upper_2], weights[2])
    got_a = pair(sent_a)
    sum_b = project_more(sum_b, lower_1, lower_3, weights[1], weights[3])
    sent_b, own_b = project_last(at, sum_b, [lower_2, lower, lower_1, lower_3], weights[2])
    got_b = pair(sent_b)

    x_video_out, x_text_out, residual, sums = pl.pallas_call(
        residual_kernel,
        in_specs=[VMEM] * 8,
        out_specs=[VMEM] * 4,
        out_shape=[
            jax.ShapeDtypeStruct((VID, WIDTH), BF16),
            jax.ShapeDtypeStruct((TXTR, WIDTH), BF16),
            jax.ShapeDtypeStruct((VID + TXTR, WIDTH), F32),
            jax.ShapeDtypeStruct((8, SUM_ROWS), F32),
        ],
        compiler_params=params(),
        name="residual",
    )(own_a, got_a, own_b, got_b, x_video, x_text, mod_video, mod_text)
    sums = sums + pair(sums)
    mlp_video_in, mlp_text_in = pl.pallas_call(
        norm_kernel,
        in_specs=[VMEM] * 7,
        out_specs=[VMEM] * 2,
        out_shape=[jax.ShapeDtypeStruct((VID, WIDTH), BF16), jax.ShapeDtypeStruct((TXTR, WIDTH), BF16)],
        compiler_params=params(),
        name="norm",
    )(residual, mod_video, mod_text, sums, *[from_on[k](sums) for k in (1, 2, 3)])
    return x_video_out, mlp_video_in, x_text_out, mlp_text_in


def solution(mesh):
    tokens, rows, columns = P("seq", "head"), P("head", None), P(None, "head")
    return jax.shard_map(
        local,
        mesh=mesh,
        in_specs=(tokens,) * 8 + (rows, rows, columns, columns),
        out_specs=(tokens,) * 4,
        check_vma=False,
    )
```

```python
import functools
import math

import jax
import jax.numpy as jnp
from jax import lax
from jax.experimental import pallas as pl
from jax.experimental.pallas import tpu as pltpu
from jax.sharding import PartitionSpec as P

MODEL_WIDTH = 3072
DH = 128
HERE = 3
WIDTH = HERE * DH
VID = 896
UPPER, LOWER = 480, 416
TXTR = 8
THEIRS = VID + 128
ACC = 144
KB = 256
BLOCK = KB + 16
CHUNKS = MODEL_WIDTH // WIDTH
SUM_ROWS = 1024
SCALE = math.log2(math.e) / math.sqrt(DH)
LIMIT = 1e30
NT = (((1,), (1,)), ((), ()))
F32, BF16 = jnp.float32, jnp.bfloat16
VMEM = pl.BlockSpec(memory_space=pltpu.VMEM)
SMEM = pl.BlockSpec(memory_space=pltpu.SMEM)
ANY = pl.BlockSpec(memory_space=pl.ANY)
HBM = pl.BlockSpec(memory_space=pltpu.HBM)


def params():
    return pltpu.CompilerParams(vmem_limit_bytes=30 * 2**20)


def with_ones(v):
    return jnp.concatenate([v.T, jnp.ones((ACC - DH, v.shape[0]), BF16)], axis=0)


def scores_of(k, q):
    return lax.dot_general(k, q, NT, preferred_element_type=F32) * SCALE


def rows_of(refs, columns):
    return [r[:KB, columns] for r in refs]


def text_of(refs, columns):
    rows = [r[KB:, columns].astype(F32)[:TXTR] for r in refs]
    return jnp.concatenate(rows, axis=0).astype(BF16)


def safe_head(q, keys, values, acc, top):
    for k, v in zip(keys, values, strict=True):
        s = scores_of(k, q)
        new_top = jnp.maximum(top, jnp.max(s, axis=0, keepdims=True))
        p = jnp.exp2(s - new_top).astype(BF16)
        acc = acc * jnp.exp2(top - new_top) + jnp.dot(with_ones(v), p, preferred_element_type=F32)
        top = new_top
    return acc, top


def columns_of(head):
    at = head * DH if isinstance(head, int) else pl.multiple_of(head * DH, DH)
    return pl.ds(at, DH), pl.ds(WIDTH + at, DH)


def attend_kernel(groups, n, texts, first, unread, send, *refs):
    q_refs, refs = refs[:groups], refs[groups:]
    blocks, text_blocks = refs[:n], refs[:texts]
    refs = refs[max(n, texts) + unread :]
    before, after = (None, refs) if first else (refs[: 2 * groups], refs[2 * groups :])

    def text_operands(h):
        key_at, value_at = columns_of(h)
        if not texts:
            return [], []
        return [text_of(text_blocks, key_at)], [text_of(text_blocks, value_at)]

    added, tops = {}, {}
    for h in range(HERE):
        key_at, value_at = columns_of(h)
        keys, values = rows_of(blocks, key_at), rows_of(blocks, value_at)
        pairs = [(keys[i : i + 2], values[i : i + 2]) for i in range(0, n, 2)]
        if texts:
            pairs.append(text_operands(h))
        for g in range(groups):
            q = q_refs[g][:, key_at]
            top = jnp.zeros((1, q.shape[0]), F32) if first else before[2 * g + 1][h, :1]
            total = None
            for k, v in pairs:
                p = jnp.exp2(scores_of(jnp.concatenate(k, axis=0), q) - top).astype(BF16)
                d = jnp.dot(with_ones(jnp.concatenate(v, axis=0)), p, preferred_element_type=F32)
                total = d if total is None else total + d
            added[g, h], tops[g, h] = total, top
    totals = jnp.concatenate([a[DH : DH + 1] for a in added.values()], axis=1)
    fine = jnp.max(totals) < LIMIT
    if first:
        fine = jnp.logical_and(fine, jnp.min(totals) > 1e-20)

    @pl.when(fine)
    def _():
        for (g, h), total in added.items():
            after[2 * g][h] = total if first else before[2 * g][h] + total
            after[2 * g + 1][h] = jnp.broadcast_to(tops[g, h], (8, total.shape[1]))

    @pl.when(jnp.logical_not(fine))
    def _():
        @pl.loop(0, HERE)
        def _(h):
            key_at, value_at = columns_of(h)
            for g in range(groups):

                @pl.loop(0, q_refs[g].shape[0] // 128)
                def _(i):
                    lanes = pl.ds(pl.multiple_of(i * 128, 128), 128)
                    more_keys, more_values = text_operands(h)
                    if first:
                        acc, top = jnp.zeros((ACC, 128), F32), jnp.full((1, 128), -1e30, F32)
                    else:
                        acc, top = before[2 * g][h, :, lanes], before[2 * g + 1][h, :1, lanes]
                    acc, top = safe_head(
                        q_refs[g][lanes, key_at],
                        rows_of(blocks, key_at) + more_keys,
                        rows_of(blocks, value_at) + more_values,
                        acc,
                        top,
                    )
                    after[2 * g][h, :, lanes] = acc
                    after[2 * g + 1][h, :, lanes] = jnp.broadcast_to(top, (8, 128))

    if send:
        acc_ref, top_ref, sent_ref = after
        row = lax.broadcasted_iota(jnp.int32, (ACC - DH, acc_ref.shape[2]), 0)

        @pl.loop(0, HERE)
        def _(h):
            total = acc_ref[h, DH : DH + 1]
            inverse = 1.0 / total
            level = top_ref[h, :1] + jnp.log2(total)
            hi = level.astype(BF16).astype(F32)
            mid = (level - hi).astype(BF16).astype(F32)
            low = level - hi - mid
            levels = jnp.where(row == 0, hi, jnp.where(row == 1, mid, jnp.where(row == 2, low, 0.0)))
            sent_ref[h, :DH] = (acc_ref[h, :DH] * inverse).astype(BF16)
            sent_ref[h, DH:] = levels.astype(BF16)


def attend(queries, blocks, states=None, every=(), unread=(), send=False):
    n, texts, groups = len(blocks), len(every), len(queries)
    blocks = [*blocks, *[b for b in every if all(b is not c for c in blocks)]]
    keys = n * KB + texts * TXTR
    lanes = sum(q.shape[0] for q in queries)
    out_shape = []
    for q in queries:
        out_shape.append(jax.ShapeDtypeStruct((HERE, ACC, q.shape[0]), F32))
        out_shape.append(jax.ShapeDtypeStruct((HERE, 8, q.shape[0]), F32))
    if send:
        out_shape.append(jax.ShapeDtypeStruct((HERE, ACC, queries[0].shape[0]), BF16))
    first = states is None
    states = [] if first else states
    before = groups + len(blocks) + len(unread)
    return pl.pallas_call(
        functools.partial(attend_kernel, groups, n, texts, first, len(unread), send),
        in_specs=[VMEM] * (groups + len(blocks)) + [ANY] * len(unread) + [VMEM] * len(states),
        out_specs=[VMEM] * len(out_shape),
        out_shape=out_shape,
        input_output_aliases={before + i: i for i in range(len(states))},
        compiler_params=params(),
        cost_estimate=pl.CostEstimate(
            flops=HERE * lanes * keys * DH * 8,
            bytes_accessed=HERE * ACC * lanes * 4,
            transcendentals=HERE * lanes * keys,
        ),
        name="attend",
    )(*queries, *blocks, *unread, *states)


def merged(acc, top, got):
    total = acc[DH : DH + 1]
    mine = top + jnp.log2(total)
    theirs = got[DH : DH + 1] + got[DH + 1 : DH + 2] + got[DH + 2 : DH + 3]
    share = 1.0 / (1.0 + jnp.exp2(theirs - mine))
    other = 1.0 / (1.0 + jnp.exp2(mine - theirs))
    return acc[:DH] * (share / total) + got[:DH] * other


def combine_kernel(
    acc_ref, top_ref, text_acc, text_top, got_ref, w_hbm, upper_ref, lower_ref, w_ref, rows_ref, sem
):
    copy = pltpu.make_async_copy(w_hbm, w_ref, sem)
    copy.start()

    @pl.loop(0, HERE)
    def _(h):
        at, _ = columns_of(h)
        video = merged(acc_ref[h], top_ref[h, :1], got_ref[h, :, :VID].astype(F32)).T.astype(BF16)
        upper_ref[:, at] = video[:UPPER]
        lower_ref[:LOWER, at] = video[UPPER:]
        got = pltpu.roll(got_ref[h, :, VID:].astype(F32), TXTR, 1)
        rows = merged(text_acc[h, :, VID:], text_top[h, :1, VID:], got).T
        rows_ref[:, at] = rows[: 2 * TXTR].astype(BF16)

    copy.wait()
    part = jnp.dot(rows_ref[...], w_ref[...], preferred_element_type=F32)[TXTR:]
    chunks = [part[:, j * WIDTH : (j + 1) * WIDTH] for j in range(CHUNKS)]
    lower_ref[LOWER:] = jnp.concatenate(chunks, axis=0).astype(BF16)


def combine(own, theirs, got, out_text):
    return pl.pallas_call(
        combine_kernel,
        in_specs=[VMEM] * 5 + [HBM],
        out_specs=[VMEM] * 2,
        out_shape=[
            jax.ShapeDtypeStruct((UPPER, WIDTH), BF16),
            jax.ShapeDtypeStruct((LOWER + CHUNKS * TXTR, WIDTH), BF16),
        ],
        scratch_shapes=[
            pltpu.VMEM((WIDTH, MODEL_WIDTH), BF16),
            pltpu.VMEM((2 * TXTR, WIDTH), BF16),
            pltpu.SemaphoreType.DMA(()),
        ],
        compiler_params=params(),
        cost_estimate=pl.CostEstimate(flops=10**9, bytes_accessed=10**7, transcendentals=0),
        name="combine",
    )(*own, *theirs, got, out_text)


def slice_kernel(steps, unread, at_ref, w_ref, *refs):
    out_refs, sems = refs[unread : unread + len(steps)], refs[unread + len(steps) :]
    copies = []
    for k, out_ref, sem in zip(steps, out_refs, sems, strict=True):
        first = lax.rem(at_ref[0] + 4 - k, 4) * (2 * WIDTH)
        columns = pl.ds(pl.multiple_of(first, 2 * WIDTH), 2 * WIDTH)
        copies.append(pltpu.make_async_copy(w_ref.at[:, columns], out_ref, sem))
        copies[-1].start()
    for copy in copies:
        copy.wait()


def column_slices(at, weight, steps, unread=()):
    return pl.pallas_call(
        functools.partial(slice_kernel, steps, len(unread)),
        in_specs=[SMEM, HBM] + [ANY] * len(unread),
        out_specs=[VMEM] * len(steps),
        out_shape=[jax.ShapeDtypeStruct((WIDTH, 2 * WIDTH), BF16)] * len(steps),
        scratch_shapes=[pltpu.SemaphoreType.DMA(())] * len(steps),
        compiler_params=params(),
        name="columns",
    )(at, weight, *unread)


def own_kernel(arrived_ref, upper_ref, lower_ref, w_ref, upper_out, lower_out, again_ref):
    del arrived_ref
    again_ref[...] = lower_ref[...]
    upper_out[...] = jnp.dot(upper_ref[...], w_ref[...], preferred_element_type=F32)
    lower_out[...] = jnp.dot(lower_ref[:LOWER], w_ref[...], preferred_element_type=F32)


def project_own(arrived, upper, lower, weight):
    return pl.pallas_call(
        own_kernel,
        in_specs=[ANY] + [VMEM] * 3,
        out_specs=[VMEM] * 3,
        out_shape=[
            *[jax.ShapeDtypeStruct((rows, 2 * WIDTH), F32) for rows in (UPPER, LOWER)],
            jax.ShapeDtypeStruct(lower.shape, BF16),
        ],
        compiler_params=params(),
        cost_estimate=pl.CostEstimate(flops=10**9, bytes_accessed=5 * 10**6, transcendentals=0),
        name="project_own",
    )(arrived, upper, lower, weight)


def more_kernel(sum_ref, one_ref, two_ref, w_one, w_two, out_ref):
    rows = sum_ref.shape[0]
    out_ref[...] = (
        sum_ref[...]
        + jnp.dot(one_ref[:rows], w_one[...], preferred_element_type=F32)
        + jnp.dot(two_ref[:rows], w_two[...], preferred_element_type=F32)
    )


def project_more(total, one, two, w_one, w_two):
    return pl.pallas_call(
        more_kernel,
        in_specs=[VMEM] * 5,
        out_specs=VMEM,
        out_shape=jax.ShapeDtypeStruct(total.shape, F32),
        input_output_aliases={0: 0},
        compiler_params=params(),
        cost_estimate=pl.CostEstimate(flops=10**9, bytes_accessed=5 * 10**6, transcendentals=0),
        name="project_more",
    )(total, one, two, w_one, w_two)


def last_kernel(at_ref, sum_ref, *refs):
    att, w_ref, sent_ref, mine_ref = refs[:-3], refs[-3], refs[-2], refs[-1]
    left = at_ref[1] == 0
    count = sum_ref.shape[0]
    rows = sum_ref[...] + jnp.dot(att[0][:count], w_ref[...], preferred_element_type=F32)
    one, two = rows[:, :WIDTH], rows[:, WIDTH:]
    mine_ref[:count] = jnp.where(left, one, two)
    sent_ref[:count] = jnp.where(left, two, one).astype(BF16)
    if len(att) > 1:
        at = pl.ds(pl.multiple_of(count + at_ref[0] * (2 * TXTR), 2 * TXTR), 2 * TXTR)
        text = sum(a[at].astype(F32) for a in att)
        mine = jnp.where(left, text[:TXTR], text[TXTR:])
        sent = jnp.where(left, text[TXTR:], text[:TXTR])
        mine_ref[count:] = jnp.concatenate([mine, mine], axis=0)
        sent_ref[count:] = jnp.concatenate([sent, sent], axis=0).astype(BF16)


def project_last(at, total, att, weight):
    rows = total.shape[0] + (2 * TXTR if len(att) > 1 else 0)
    return pl.pallas_call(
        last_kernel,
        in_specs=[SMEM] + [VMEM] * (2 + len(att)),
        out_specs=[VMEM] * 2,
        out_shape=[jax.ShapeDtypeStruct((rows, WIDTH), BF16), jax.ShapeDtypeStruct((rows, WIDTH), F32)],
        compiler_params=params(),
        cost_estimate=pl.CostEstimate(flops=10**9, bytes_accessed=5 * 10**6, transcendentals=0),
        name="project_last",
    )(at, total, *att, weight)


def residual_kernel(
    own_a, got_a, own_b, got_b, xv_ref, xt_ref, mv_ref, mt_ref, xv_out, xt_out, res_ref, sums_ref
):
    gate = mv_ref[:1]
    upper = xv_ref[:UPPER].astype(F32) + gate * (own_a[...] + got_a[...].astype(F32))
    lower = xv_ref[UPPER:].astype(F32) + gate * (own_b[:LOWER] + got_b[:LOWER].astype(F32))
    text_proj = own_b[LOWER:] + got_b[LOWER:].astype(F32)
    text = xt_ref[...].astype(F32) + mt_ref[:1] * text_proj[:TXTR]
    xv_out[:UPPER] = upper.astype(BF16)
    xv_out[UPPER:] = lower.astype(BF16)
    xt_out[...] = text.astype(BF16)
    rows = jnp.concatenate([upper, lower, text], axis=0)
    res_ref[...] = rows
    count = VID + TXTR
    lane = lax.broadcasted_iota(jnp.int32, (count, 128), 1)
    sums = jnp.where(
        lane == 0,
        jnp.sum(rows, axis=1, keepdims=True),
        jnp.where(lane == 1, jnp.sum(rows * rows, axis=1, keepdims=True), 0.0),
    )
    sums = jnp.concatenate([sums, jnp.zeros((SUM_ROWS - count, 128), F32)], axis=0)
    sums_ref[...] = sums.T[:8]


def norm_kernel(res_ref, mv_ref, mt_ref, s0_ref, s1_ref, s2_ref, s3_ref, video_out, text_out):
    sums = (s0_ref[...] + s1_ref[...]) + (s2_ref[...] + s3_ref[...])
    sums = jnp.concatenate([sums, jnp.zeros((120, SUM_ROWS), F32)], axis=0).T
    mean = sums[: VID + TXTR, :1] / MODEL_WIDTH
    var = sums[: VID + TXTR, 1:2] / MODEL_WIDTH - mean * mean
    normed = (res_ref[...] - mean) * lax.rsqrt(var + 1e-06)
    video_out[...] = (normed[:VID] * (1.0 + mv_ref[2:3]) + mv_ref[1:2]).astype(BF16)
    text_out[...] = (normed[VID:] * (1.0 + mt_ref[2:3]) + mt_ref[1:2]).astype(BF16)


def local(
    q_video, k_video, video_value_rows, q_text, k_text, v_text, x_video, x_text, out_video, out_text, mod_video, mod_text
):
    def over_seq(move):
        pairs = []
        for y in range(2):
            for z in range(8):
                for c in range(2):
                    a, b, d = move(y, z, c)
                    pairs.append(((y * 8 + z) * 2 + c, ((a % 2) * 8 + b % 8) * 2 + d % 2))
        return lambda value: lax.ppermute(value, "seq", pairs)

    def over_head(move):
        pairs = []
        for x in range(4):
            for y in range(2):
                a, b = move(x, y)
                pairs.append((x * 2 + y, (a % 4) * 2 + b % 2))
        return lambda value: lax.ppermute(value, "head", pairs)

    other_core = over_seq(lambda y, z, c: (y, z, 1 - c))
    other_plane = over_seq(lambda y, z, c: (1 - y, z, c))
    up = over_seq(lambda y, z, c: (y, z + 1, c))
    down = over_seq(lambda y, z, c: (y, z - 1, c))
    across = over_seq(lambda y, z, c: (1 - y, z - 1, c))
    from_on = [None] + [over_head(lambda x, y, k=k: (x - k, y)) for k in (1, 2, 3)]
    pair = over_head(lambda x, y: (x, 1 - y))

    head = lax.axis_index("head")
    x_at = head // 2
    at = jnp.stack([x_at, head % 2]).astype(jnp.int32)

    own = jnp.concatenate(
        [
            jnp.concatenate([k_video, video_value_rows], axis=1),
            jnp.concatenate([k_text, v_text], axis=1),
            jnp.zeros((BLOCK - KB - TXTR, 2 * WIDTH), BF16),
        ],
        axis=0,
    )
    q_other = other_core(jnp.concatenate([q_video, q_text], axis=0))
    y0, r1, l1 = other_plane(own), up(own), down(own)
    r2, l2 = up(r1), down(l1)
    yr1, yl1 = other_plane(r1), other_plane(l1)
    r3, l3 = up(r2), down(l2)
    ry2, ly2 = up(yr1), down(yl1)
    r4, opposite = up(r3), across(l3)
    ry3, ly3 = up(ry2), down(ly2)

    here, slice_1 = column_slices(at, out_video, (0, 1), unread=[q_other])
    weight_1 = from_on[1](slice_1)
    [slice_2] = column_slices(at, out_video, (2,), unread=[y0, weight_1])
    weight_2 = from_on[2](slice_2)
    [slice_3] = column_slices(at, out_video, (3,), unread=[weight_2])
    weights = [here, weight_1, weight_2, from_on[3](slice_3)]

    q_theirs = jnp.concatenate([q_other, q_text, jnp.zeros((THEIRS - VID - 2 * TXTR, WIDTH), BF16)], axis=0)
    queries = [q_theirs, q_video]
    states = attend(queries, [own, r1, l1, y0])
    states = attend(queries, [r2, l2, yr1, yl1], states)
    states = attend(queries, [r3, l3, ry2, ly2], states, unread=[weights[2]])
    states = attend(queries, [r4, opposite], states)
    every = [ry3, ly3, own, r1, l1, y0, r2, l2, yr1, yl1, r3, l3, ry2, ly2, r4, opposite]
    *theirs, sent = attend(queries[:1], [ry3, ly3], states[:2], every=every, unread=[weights[3]], send=True)
    got = other_core(sent)
    mine = attend(queries[1:], [ry3, ly3], states[2:], every=every)

    upper, lower = combine(mine, theirs, got, out_text)
    upper_1, upper_3, lower_3 = from_on[1](upper), from_on[3](upper), from_on[3](lower)
    upper_2 = from_on[1](upper_1)
    sum_a, sum_b, lower_again = project_own(upper_1, upper, lower, weights[0])
    lower_1, lower_2 = from_on[1](lower_again), from_on[3](lower_3)
    sum_a = project_more(sum_a, upper_1, upper_3, weights[1], weights[3])
    sent_a, own_a = project_last(at, sum_a, [upper_2], weights[2])
    got_a = pair(sent_a)
    sum_b = project_more(sum_b, lower_1, lower_3, weights[1], weights[3])
    sent_b, own_b = project_last(at, sum_b, [lower_2, lower, lower_1, lower_3], weights[2])
    got_b = pair(sent_b)

    x_video_out, x_text_out, residual, sums = pl.pallas_call(
        residual_kernel,
        in_specs=[VMEM] * 8,
        out_specs=[VMEM] * 4,
        out_shape=[
            jax.ShapeDtypeStruct((VID, WIDTH), BF16),
            jax.ShapeDtypeStruct((TXTR, WIDTH), BF16),
            jax.ShapeDtypeStruct((VID + TXTR, WIDTH), F32),
            jax.ShapeDtypeStruct((8, SUM_ROWS), F32),
        ],
        compiler_params=params(),
        name="residual",
    )(own_a, got_a, own_b, got_b, x_video, x_text, mod_video, mod_text)
    sums = sums + pair(sums)
    mlp_video_in, mlp_text_in = pl.pallas_call(
        norm_kernel,
        in_specs=[VMEM] * 7,
        out_specs=[VMEM] * 2,
        out_shape=[jax.ShapeDtypeStruct((VID, WIDTH), BF16), jax.ShapeDtypeStruct((TXTR, WIDTH), BF16)],
        compiler_params=params(),
        name="norm",
    )(residual, mod_video, mod_text, sums, *[from_on[k](sums) for k in (1, 2, 3)])
    return x_video_out, mlp_video_in, x_text_out, mlp_text_in


def solution(mesh):
    tokens, rows, columns = P("seq", "head"), P("head", None), P(None, "head")
    return jax.shard_map(
        local,
        mesh=mesh,
        in_specs=(tokens,) * 8 + (rows, rows, columns, columns),
        out_specs=(tokens,) * 4,
        check_vma=False,
    )
```

```python
import functools
import math

import jax
import jax.numpy as jnp
from jax import lax
from jax.experimental import pallas as pl
from jax.experimental.pallas import tpu as pltpu
from jax.sharding import PartitionSpec as P

MODEL_WIDTH = 3072
DH = 128
HERE = 3
WIDTH = HERE * DH
VID = 896
UPPER, LOWER = 480, 416
TXTR = 8
THEIRS = VID + 128
ACC = 144
KB = 256
BLOCK = KB + 16
CHUNKS = MODEL_WIDTH // WIDTH
SUM_ROWS = 1024
SCALE = math.log2(math.e) / math.sqrt(DH)
LIMIT = 1e30
NT = (((1,), (1,)), ((), ()))
F32, BF16 = jnp.float32, jnp.bfloat16
VMEM = pl.BlockSpec(memory_space=pltpu.VMEM)
SMEM = pl.BlockSpec(memory_space=pltpu.SMEM)
ANY = pl.BlockSpec(memory_space=pl.ANY)
HBM = pl.BlockSpec(memory_space=pltpu.HBM)


def params():
    return pltpu.CompilerParams(vmem_limit_bytes=30 * 2**20)


def with_ones(v):
    return jnp.concatenate([v.T, jnp.ones((ACC - DH, v.shape[0]), BF16)], axis=0)


def scores_of(k, q):
    return lax.dot_general(k, q, NT, preferred_element_type=F32) * SCALE


def rows_of(refs, columns):
    return [r[:KB, columns] for r in refs]


def text_of(refs, columns):
    rows = [r[KB:, columns].astype(F32)[:TXTR] for r in refs]
    return jnp.concatenate(rows, axis=0).astype(BF16)


def safe_head(q, keys, values, acc, top):
    for k, v in zip(keys, values, strict=True):
        s = scores_of(k, q)
        new_top = jnp.maximum(top, jnp.max(s, axis=0, keepdims=True))
        p = jnp.exp2(s - new_top).astype(BF16)
        acc = acc * jnp.exp2(top - new_top) + jnp.dot(with_ones(v), p, preferred_element_type=F32)
        top = new_top
    return acc, top


def columns_of(head):
    at = head * DH if isinstance(head, int) else pl.multiple_of(head * DH, DH)
    return pl.ds(at, DH), pl.ds(WIDTH + at, DH)


def attend_kernel(groups, n, texts, first, unread, send, *refs):
    q_refs, refs = refs[:groups], refs[groups:]
    blocks, text_blocks = refs[:n], refs[:texts]
    refs = refs[max(n, texts) + unread :]
    before, after = (None, refs) if first else (refs[: 2 * groups], refs[2 * groups :])

    def text_operands(h):
        key_at, value_at = columns_of(h)
        if not texts:
            return [], []
        return [text_of(text_blocks, key_at)], [text_of(text_blocks, value_at)]

    added, tops = {}, {}
    for h in range(HERE):
        key_at, value_at = columns_of(h)
        keys, values = rows_of(blocks, key_at), rows_of(blocks, value_at)
        pairs = [(keys[i : i + 2], values[i : i + 2]) for i in range(0, n, 2)]
        if texts:
            pairs.append(text_operands(h))
        for g in range(groups):
            q = q_refs[g][:, key_at]
            top = jnp.zeros((1, q.shape[0]), F32) if first else before[2 * g + 1][h, :1]
            total = None
            for k, v in pairs:
                p = jnp.exp2(scores_of(jnp.concatenate(k, axis=0), q) - top).astype(BF16)
                d = jnp.dot(with_ones(jnp.concatenate(v, axis=0)), p, preferred_element_type=F32)
                total = d if total is None else total + d
            added[g, h], tops[g, h] = total, top
    totals = jnp.concatenate([a[DH : DH + 1] for a in added.values()], axis=1)
    fine = jnp.max(totals) < LIMIT
    if first:
        fine = jnp.logical_and(fine, jnp.min(totals) > 1e-20)

    @pl.when(fine)
    def _():
        for (g, h), total in added.items():
            after[2 * g][h] = total if first else before[2 * g][h] + total
            after[2 * g + 1][h] = jnp.broadcast_to(tops[g, h], (8, total.shape[1]))

    @pl.when(jnp.logical_not(fine))
    def _():
        @pl.loop(0, HERE)
        def _(h):
            key_at, value_at = columns_of(h)
            for g in range(groups):

                @pl.loop(0, q_refs[g].shape[0] // 128)
                def _(i):
                    lanes = pl.ds(pl.multiple_of(i * 128, 128), 128)
                    more_keys, more_values = text_operands(h)
                    if first:
                        acc, top = jnp.zeros((ACC, 128), F32), jnp.full((1, 128), -1e30, F32)
                    else:
                        acc, top = before[2 * g][h, :, lanes], before[2 * g + 1][h, :1, lanes]
                    acc, top = safe_head(
                        q_refs[g][lanes, key_at],
                        rows_of(blocks, key_at) + more_keys,
                        rows_of(blocks, value_at) + more_values,
                        acc,
                        top,
                    )
                    after[2 * g][h, :, lanes] = acc
                    after[2 * g + 1][h, :, lanes] = jnp.broadcast_to(top, (8, 128))

    if send:
        acc_ref, top_ref, sent_ref = after
        row = lax.broadcasted_iota(jnp.int32, (ACC - DH, acc_ref.shape[2]), 0)

        @pl.loop(0, HERE)
        def _(h):
            total = acc_ref[h, DH : DH + 1]
            inverse = 1.0 / total
            level = top_ref[h, :1] + jnp.log2(total)
            hi = level.astype(BF16).astype(F32)
            mid = (level - hi).astype(BF16).astype(F32)
            low = level - hi - mid
            levels = jnp.where(row == 0, hi, jnp.where(row == 1, mid, jnp.where(row == 2, low, 0.0)))
            sent_ref[h, :DH] = (acc_ref[h, :DH] * inverse).astype(BF16)
            sent_ref[h, DH:] = levels.astype(BF16)


def attend(queries, blocks, states=None, every=(), unread=(), send=False):
    n, texts, groups = len(blocks), len(every), len(queries)
    blocks = [*blocks, *[b for b in every if all(b is not c for c in blocks)]]
    keys = n * KB + texts * TXTR
    lanes = sum(q.shape[0] for q in queries)
    out_shape = []
    for q in queries:
        out_shape.append(jax.ShapeDtypeStruct((HERE, ACC, q.shape[0]), F32))
        out_shape.append(jax.ShapeDtypeStruct((HERE, 8, q.shape[0]), F32))
    if send:
        out_shape.append(jax.ShapeDtypeStruct((HERE, ACC, queries[0].shape[0]), BF16))
    first = states is None
    states = [] if first else states
    before = groups + len(blocks) + len(unread)
    return pl.pallas_call(
        functools.partial(attend_kernel, groups, n, texts, first, len(unread), send),
        in_specs=[VMEM] * (groups + len(blocks)) + [ANY] * len(unread) + [VMEM] * len(states),
        out_specs=[VMEM] * len(out_shape),
        out_shape=out_shape,
        input_output_aliases={before + i: i for i in range(len(states))},
        compiler_params=params(),
        cost_estimate=pl.CostEstimate(
            flops=HERE * lanes * keys * DH * 8,
            bytes_accessed=HERE * ACC * lanes * 4,
            transcendentals=HERE * lanes * keys,
        ),
        name="attend",
    )(*queries, *blocks, *unread, *states)


def merged(acc, top, got):
    total = acc[DH : DH + 1]
    mine = top + jnp.log2(total)
    theirs = got[DH : DH + 1] + got[DH + 1 : DH + 2] + got[DH + 2 : DH + 3]
    share = 1.0 / (1.0 + jnp.exp2(theirs - mine))
    other = 1.0 / (1.0 + jnp.exp2(mine - theirs))
    return acc[:DH] * (share / total) + got[:DH] * other


def combine_kernel(
    acc_ref, top_ref, text_acc, text_top, got_ref, w_hbm, upper_ref, lower_ref, w_ref, rows_ref, sem
):
    copy = pltpu.make_async_copy(w_hbm, w_ref, sem)
    copy.start()

    @pl.loop(0, HERE)
    def _(h):
        at, _ = columns_of(h)
        video = merged(acc_ref[h], top_ref[h, :1], got_ref[h, :, :VID].astype(F32)).T.astype(BF16)
        upper_ref[:, at] = video[:UPPER]
        lower_ref[:LOWER, at] = video[UPPER:]
        got = pltpu.roll(got_ref[h, :, VID:].astype(F32), TXTR, 1)
        rows = merged(text_acc[h, :, VID:], text_top[h, :1, VID:], got).T
        rows_ref[:, at] = rows[: 2 * TXTR].astype(BF16)

    copy.wait()
    part = jnp.dot(rows_ref[...], w_ref[...], preferred_element_type=F32)[TXTR:]
    chunks = [part[:, j * WIDTH : (j + 1) * WIDTH] for j in range(CHUNKS)]
    lower_ref[LOWER:] = jnp.concatenate(chunks, axis=0).astype(BF16)


def combine(own, theirs, got, out_text):
    return pl.pallas_call(
        combine_kernel,
        in_specs=[VMEM] * 5 + [HBM],
        out_specs=[VMEM] * 2,
        out_shape=[
            jax.ShapeDtypeStruct((UPPER, WIDTH), BF16),
            jax.ShapeDtypeStruct((LOWER + CHUNKS * TXTR, WIDTH), BF16),
        ],
        scratch_shapes=[
            pltpu.VMEM((WIDTH, MODEL_WIDTH), BF16),
            pltpu.VMEM((2 * TXTR, WIDTH), BF16),
            pltpu.SemaphoreType.DMA(()),
        ],
        compiler_params=params(),
        cost_estimate=pl.CostEstimate(flops=10**9, bytes_accessed=10**7, transcendentals=0),
        name="combine",
    )(*own, *theirs, got, out_text)


def slice_kernel(steps, unread, at_ref, w_ref, *refs):
    out_refs, sems = refs[unread : unread + len(steps)], refs[unread + len(steps) :]
    copies = []
    for k, out_ref, sem in zip(steps, out_refs, sems, strict=True):
        first = lax.rem(at_ref[0] + 4 - k, 4) * (2 * WIDTH)
        columns = pl.ds(pl.multiple_of(first, 2 * WIDTH), 2 * WIDTH)
        copies.append(pltpu.make_async_copy(w_ref.at[:, columns], out_ref, sem))
        copies[-1].start()
    for copy in copies:
        copy.wait()


def column_slices(at, weight, steps, unread=()):
    return pl.pallas_call(
        functools.partial(slice_kernel, steps, len(unread)),
        in_specs=[SMEM, HBM] + [ANY] * len(unread),
        out_specs=[VMEM] * len(steps),
        out_shape=[jax.ShapeDtypeStruct((WIDTH, 2 * WIDTH), BF16)] * len(steps),
        scratch_shapes=[pltpu.SemaphoreType.DMA(())] * len(steps),
        compiler_params=params(),
        name="columns",
    )(at, weight, *unread)


def own_kernel(arrived_ref, upper_ref, lower_ref, w_ref, upper_out, lower_out, again_ref):
    del arrived_ref
    again_ref[...] = lower_ref[...]
    upper_out[...] = jnp.dot(upper_ref[...], w_ref[...], preferred_element_type=F32)
    lower_out[...] = jnp.dot(lower_ref[:LOWER], w_ref[...], preferred_element_type=F32)


def project_own(arrived, upper, lower, weight):
    return pl.pallas_call(
        own_kernel,
        in_specs=[ANY] + [VMEM] * 3,
        out_specs=[VMEM] * 3,
        out_shape=[
            *[jax.ShapeDtypeStruct((rows, 2 * WIDTH), F32) for rows in (UPPER, LOWER)],
            jax.ShapeDtypeStruct(lower.shape, BF16),
        ],
        compiler_params=params(),
        cost_estimate=pl.CostEstimate(flops=10**9, bytes_accessed=5 * 10**6, transcendentals=0),
        name="project_own",
    )(arrived, upper, lower, weight)


def more_kernel(sum_ref, one_ref, two_ref, w_one, w_two, out_ref):
    rows = sum_ref.shape[0]
    out_ref[...] = (
        sum_ref[...]
        + jnp.dot(one_ref[:rows], w_one[...], preferred_element_type=F32)
        + jnp.dot(two_ref[:rows], w_two[...], preferred_element_type=F32)
    )


def project_more(total, one, two, w_one, w_two):
    return pl.pallas_call(
        more_kernel,
        in_specs=[VMEM] * 5,
        out_specs=VMEM,
        out_shape=jax.ShapeDtypeStruct(total.shape, F32),
        input_output_aliases={0: 0},
        compiler_params=params(),
        cost_estimate=pl.CostEstimate(flops=10**9, bytes_accessed=5 * 10**6, transcendentals=0),
        name="project_more",
    )(total, one, two, w_one, w_two)


def last_kernel(at_ref, sum_ref, *refs):
    att, w_ref, sent_ref, mine_ref = refs[:-3], refs[-3], refs[-2], refs[-1]
    left = at_ref[1] == 0
    count = sum_ref.shape[0]
    rows = sum_ref[...] + jnp.dot(att[0][:count], w_ref[...], preferred_element_type=F32)
    one, two = rows[:, :WIDTH], rows[:, WIDTH:]
    mine_ref[:count] = jnp.where(left, one, two)
    sent_ref[:count] = jnp.where(left, two, one).astype(BF16)
    if len(att) > 1:
        at = pl.ds(pl.multiple_of(count + at_ref[0] * (2 * TXTR), 2 * TXTR), 2 * TXTR)
        text = sum(a[at].astype(F32) for a in att)
        mine = jnp.where(left, text[:TXTR], text[TXTR:])
        sent = jnp.where(left, text[TXTR:], text[:TXTR])
        mine_ref[count:] = jnp.concatenate([mine, mine], axis=0)
        sent_ref[count:] = jnp.concatenate([sent, sent], axis=0).astype(BF16)


def project_last(at, total, att, weight):
    rows = total.shape[0] + (2 * TXTR if len(att) > 1 else 0)
    return pl.pallas_call(
        last_kernel,
        in_specs=[SMEM] + [VMEM] * (2 + len(att)),
        out_specs=[VMEM] * 2,
        out_shape=[jax.ShapeDtypeStruct((rows, WIDTH), BF16), jax.ShapeDtypeStruct((rows, WIDTH), F32)],
        compiler_params=params(),
        cost_estimate=pl.CostEstimate(flops=10**9, bytes_accessed=5 * 10**6, transcendentals=0),
        name="project_last",
    )(at, total, *att, weight)


def residual_kernel(
    own_a, got_a, own_b, got_b, xv_ref, xt_ref, mv_ref, mt_ref, xv_out, xt_out, res_ref, sums_ref
):
    gate = mv_ref[:1]
    upper = xv_ref[:UPPER].astype(F32) + gate * (own_a[...] + got_a[...].astype(F32))
    lower = xv_ref[UPPER:].astype(F32) + gate * (own_b[:LOWER] + got_b[:LOWER].astype(F32))
    text_proj = own_b[LOWER:] + got_b[LOWER:].astype(F32)
    text = xt_ref[...].astype(F32) + mt_ref[:1] * text_proj[:TXTR]
    xv_out[:UPPER] = upper.astype(BF16)
    xv_out[UPPER:] = lower.astype(BF16)
    xt_out[...] = text.astype(BF16)
    rows = jnp.concatenate([upper, lower, text], axis=0)
    res_ref[...] = rows
    count = VID + TXTR
    lane = lax.broadcasted_iota(jnp.int32, (count, 128), 1)
    sums = jnp.where(
        lane == 0,
        jnp.sum(rows, axis=1, keepdims=True),
        jnp.where(lane == 1, jnp.sum(rows * rows, axis=1, keepdims=True), 0.0),
    )
    sums = jnp.concatenate([sums, jnp.zeros((SUM_ROWS - count, 128), F32)], axis=0)
    sums_ref[...] = sums.T[:8]


def norm_kernel(res_ref, mv_ref, mt_ref, s0_ref, s1_ref, s2_ref, s3_ref, video_out, text_out):
    sums = (s0_ref[...] + s1_ref[...]) + (s2_ref[...] + s3_ref[...])
    sums = jnp.concatenate([sums, jnp.zeros((120, SUM_ROWS), F32)], axis=0).T
    mean = sums[: VID + TXTR, :1] / MODEL_WIDTH
    var = sums[: VID + TXTR, 1:2] / MODEL_WIDTH - mean * mean
    normed = (res_ref[...] - mean) * lax.rsqrt(var + 1e-06)
    video_out[...] = (normed[:VID] * (1.0 + mv_ref[2:3]) + mv_ref[1:2]).astype(BF16)
    text_out[...] = (normed[VID:] * (1.0 + mt_ref[2:3]) + mt_ref[1:2]).astype(BF16)


def local(
    q_video, k_video, video_value_rows, q_text, k_text, v_text, x_video, x_text, out_video, out_text, mod_video, mod_text
):
    def over_seq(move):
        pairs = []
        for y in range(2):
            for z in range(8):
                for c in range(2):
                    a, b, d = move(y, z, c)
                    pairs.append(((y * 8 + z) * 2 + c, ((a % 2) * 8 + b % 8) * 2 + d % 2))
        return lambda value: lax.ppermute(value, "seq", pairs)

    def over_head(move):
        pairs = []
        for x in range(4):
            for y in range(2):
                a, b = move(x, y)
                pairs.append((x * 2 + y, (a % 4) * 2 + b % 2))
        return lambda value: lax.ppermute(value, "head", pairs)

    other_core = over_seq(lambda y, z, c: (y, z, 1 - c))
    other_plane = over_seq(lambda y, z, c: (1 - y, z, c))
    up = over_seq(lambda y, z, c: (y, z + 1, c))
    down = over_seq(lambda y, z, c: (y, z - 1, c))
    across = over_seq(lambda y, z, c: (1 - y, z - 1, c))
    from_on = [None] + [over_head(lambda x, y, k=k: (x - k, y)) for k in (1, 2, 3)]
    pair = over_head(lambda x, y: (x, 1 - y))

    head = lax.axis_index("head")
    x_at = head // 2
    at = jnp.stack([x_at, head % 2]).astype(jnp.int32)

    own = jnp.concatenate(
        [
            jnp.concatenate([k_video, video_value_rows], axis=1),
            jnp.concatenate([k_text, v_text], axis=1),
            jnp.zeros((BLOCK - KB - TXTR, 2 * WIDTH), BF16),
        ],
        axis=0,
    )
    q_other = other_core(jnp.concatenate([q_video, q_text], axis=0))
    y0, r1, l1 = other_plane(own), up(own), down(own)
    r2, l2 = up(r1), down(l1)
    yr1, yl1 = other_plane(r1), other_plane(l1)
    r3, l3 = up(r2), down(l2)
    ry2, ly2 = up(yr1), down(yl1)
    r4, opposite = up(r3), across(l3)
    ry3, ly3 = up(ry2), down(ly2)

    q_theirs = jnp.concatenate([q_other, q_text, jnp.zeros((THEIRS - VID - 2 * TXTR, WIDTH), BF16)], axis=0)
    queries = [q_theirs, q_video]
    states = attend(queries, [own, r1, l1, y0])

    here, slice_1 = column_slices(at, out_video, (0, 1), unread=[own])
    weight_1 = from_on[1](slice_1)
    [slice_2] = column_slices(at, out_video, (2,), unread=[weight_1, states[1]])
    weight_2 = from_on[2](slice_2)
    [slice_3] = column_slices(at, out_video, (3,), unread=[weight_2])
    weights = [here, weight_1, weight_2, from_on[3](slice_3)]

    states = attend(queries, [r2, l2, yr1, yl1], states)
    states = attend(queries, [r3, l3, ry2, ly2], states, unread=[weights[2]])
    states = attend(queries, [r4, opposite], states)
    every = [ry3, ly3, own, r1, l1, y0, r2, l2, yr1, yl1, r3, l3, ry2, ly2, r4, opposite]
    *theirs, sent = attend(queries[:1], [ry3, ly3], states[:2], every=every, unread=[weights[3]], send=True)
    got = other_core(sent)
    mine = attend(queries[1:], [ry3, ly3], states[2:], every=every)

    upper, lower = combine(mine, theirs, got, out_text)
    upper_1, upper_3, lower_3 = from_on[1](upper), from_on[3](upper), from_on[3](lower)
    upper_2 = from_on[1](upper_1)
    sum_a, sum_b, lower_again = project_own(upper_1, upper, lower, weights[0])
    lower_1, lower_2 = from_on[1](lower_again), from_on[3](lower_3)
    sum_a = project_more(sum_a, upper_1, upper_3, weights[1], weights[3])
    sent_a, own_a = project_last(at, sum_a, [upper_2], weights[2])
    got_a = pair(sent_a)
    sum_b = project_more(sum_b, lower_1, lower_3, weights[1], weights[3])
    sent_b, own_b = project_last(at, sum_b, [lower_2, lower, lower_1, lower_3], weights[2])
    got_b = pair(sent_b)

    x_video_out, x_text_out, residual, sums = pl.pallas_call(
        residual_kernel,
        in_specs=[VMEM] * 8,
        out_specs=[VMEM] * 4,
        out_shape=[
            jax.ShapeDtypeStruct((VID, WIDTH), BF16),
            jax.ShapeDtypeStruct((TXTR, WIDTH), BF16),
            jax.ShapeDtypeStruct((VID + TXTR, WIDTH), F32),
            jax.ShapeDtypeStruct((8, SUM_ROWS), F32),
        ],
        compiler_params=params(),
        name="residual",
    )(own_a, got_a, own_b, got_b, x_video, x_text, mod_video, mod_text)
    sums = sums + pair(sums)
    mlp_video_in, mlp_text_in = pl.pallas_call(
        norm_kernel,
        in_specs=[VMEM] * 7,
        out_specs=[VMEM] * 2,
        out_shape=[jax.ShapeDtypeStruct((VID, WIDTH), BF16), jax.ShapeDtypeStruct((TXTR, WIDTH), BF16)],
        compiler_params=params(),
        name="norm",
    )(residual, mod_video, mod_text, sums, *[from_on[k](sums) for k in (1, 2, 3)])
    return x_video_out, mlp_video_in, x_text_out, mlp_text_in


def solution(mesh):
    tokens, rows, columns = P("seq", "head"), P("head", None), P(None, "head")
    return jax.shard_map(
        local,
        mesh=mesh,
        in_specs=(tokens,) * 8 + (rows, rows, columns, columns),
        out_specs=(tokens,) * 4,
        check_vma=False,
    )
```

```python
import functools
import math

import jax
import jax.numpy as jnp
from jax import lax
from jax.experimental import pallas as pl
from jax.experimental.pallas import tpu as pltpu
from jax.sharding import PartitionSpec as P

MODEL_WIDTH = 3072
DH = 128
HERE = 3
WIDTH = HERE * DH
VID = 896
UPPER, LOWER = 480, 416
TXTR = 8
THEIRS = VID + 128
ACC = 144
KB = 256
BLOCK = KB + 16
CHUNKS = MODEL_WIDTH // WIDTH
SUM_ROWS = 1024
SCALE = math.log2(math.e) / math.sqrt(DH)
LIMIT = 1e30
NT = (((1,), (1,)), ((), ()))
F32, BF16 = jnp.float32, jnp.bfloat16
VMEM = pl.BlockSpec(memory_space=pltpu.VMEM)
SMEM = pl.BlockSpec(memory_space=pltpu.SMEM)
ANY = pl.BlockSpec(memory_space=pl.ANY)
HBM = pl.BlockSpec(memory_space=pltpu.HBM)


def params():
    return pltpu.CompilerParams(vmem_limit_bytes=30 * 2**20)


def with_ones(v):
    return jnp.concatenate([v.T, jnp.ones((ACC - DH, v.shape[0]), BF16)], axis=0)


def scores_of(k, q):
    return lax.dot_general(k, q, NT, preferred_element_type=F32) * SCALE


def rows_of(refs, columns):
    return [r[:KB, columns] for r in refs]


def text_of(refs, columns):
    rows = [r[KB:, columns].astype(F32)[:TXTR] for r in refs]
    return jnp.concatenate(rows, axis=0).astype(BF16)


def safe_head(q, keys, values, acc, top):
    for k, v in zip(keys, values, strict=True):
        s = scores_of(k, q)
        new_top = jnp.maximum(top, jnp.max(s, axis=0, keepdims=True))
        p = jnp.exp2(s - new_top).astype(BF16)
        acc = acc * jnp.exp2(top - new_top) + jnp.dot(with_ones(v), p, preferred_element_type=F32)
        top = new_top
    return acc, top


def columns_of(head):
    at = head * DH if isinstance(head, int) else pl.multiple_of(head * DH, DH)
    return pl.ds(at, DH), pl.ds(WIDTH + at, DH)


def attend_kernel(groups, n, texts, first, unread, send, *refs):
    q_refs, refs = refs[:groups], refs[groups:]
    blocks, text_blocks = refs[:n], refs[:texts]
    refs = refs[max(n, texts) + unread :]
    before, after = (None, refs) if first else (refs[: 2 * groups], refs[2 * groups :])

    def text_operands(h):
        key_at, value_at = columns_of(h)
        if not texts:
            return [], []
        return [text_of(text_blocks, key_at)], [text_of(text_blocks, value_at)]

    added, tops = {}, {}
    for h in range(HERE):
        key_at, value_at = columns_of(h)
        keys, values = rows_of(blocks, key_at), rows_of(blocks, value_at)
        pairs = [(keys[i : i + 2], values[i : i + 2]) for i in range(0, n, 2)]
        if texts:
            pairs.append(text_operands(h))
        for g in range(groups):
            q = q_refs[g][:, key_at]
            top = jnp.zeros((1, q.shape[0]), F32) if first else before[2 * g + 1][h, :1]
            total = None
            for k, v in pairs:
                p = jnp.exp2(scores_of(jnp.concatenate(k, axis=0), q) - top).astype(BF16)
                d = jnp.dot(with_ones(jnp.concatenate(v, axis=0)), p, preferred_element_type=F32)
                total = d if total is None else total + d
            added[g, h], tops[g, h] = total, top
    totals = jnp.concatenate([a[DH : DH + 1] for a in added.values()], axis=1)
    fine = jnp.max(totals) < LIMIT
    if first:
        fine = jnp.logical_and(fine, jnp.min(totals) > 1e-20)

    @pl.when(fine)
    def _():
        for (g, h), total in added.items():
            after[2 * g][h] = total if first else before[2 * g][h] + total
            after[2 * g + 1][h] = jnp.broadcast_to(tops[g, h], (8, total.shape[1]))

    @pl.when(jnp.logical_not(fine))
    def _():
        @pl.loop(0, HERE)
        def _(h):
            key_at, value_at = columns_of(h)
            for g in range(groups):

                @pl.loop(0, q_refs[g].shape[0] // 128)
                def _(i):
                    lanes = pl.ds(pl.multiple_of(i * 128, 128), 128)
                    more_keys, more_values = text_operands(h)
                    if first:
                        acc, top = jnp.zeros((ACC, 128), F32), jnp.full((1, 128), -1e30, F32)
                    else:
                        acc, top = before[2 * g][h, :, lanes], before[2 * g + 1][h, :1, lanes]
                    acc, top = safe_head(
                        q_refs[g][lanes, key_at],
                        rows_of(blocks, key_at) + more_keys,
                        rows_of(blocks, value_at) + more_values,
                        acc,
                        top,
                    )
                    after[2 * g][h, :, lanes] = acc
                    after[2 * g + 1][h, :, lanes] = jnp.broadcast_to(top, (8, 128))

    if send:
        acc_ref, top_ref, sent_ref = after
        row = lax.broadcasted_iota(jnp.int32, (ACC - DH, acc_ref.shape[2]), 0)

        @pl.loop(0, HERE)
        def _(h):
            total = acc_ref[h, DH : DH + 1]
            inverse = 1.0 / total
            level = top_ref[h, :1] + jnp.log2(total)
            hi = level.astype(BF16).astype(F32)
            mid = (level - hi).astype(BF16).astype(F32)
            low = level - hi - mid
            levels = jnp.where(row == 0, hi, jnp.where(row == 1, mid, jnp.where(row == 2, low, 0.0)))
            sent_ref[h, :DH] = (acc_ref[h, :DH] * inverse).astype(BF16)
            sent_ref[h, DH:] = levels.astype(BF16)


def attend(queries, blocks, states=None, every=(), unread=(), send=False):
    n, texts, groups = len(blocks), len(every), len(queries)
    blocks = [*blocks, *[b for b in every if all(b is not c for c in blocks)]]
    keys = n * KB + texts * TXTR
    lanes = sum(q.shape[0] for q in queries)
    out_shape = []
    for q in queries:
        out_shape.append(jax.ShapeDtypeStruct((HERE, ACC, q.shape[0]), F32))
        out_shape.append(jax.ShapeDtypeStruct((HERE, 8, q.shape[0]), F32))
    if send:
        out_shape.append(jax.ShapeDtypeStruct((HERE, ACC, queries[0].shape[0]), BF16))
    first = states is None
    states = [] if first else states
    before = groups + len(blocks) + len(unread)
    return pl.pallas_call(
        functools.partial(attend_kernel, groups, n, texts, first, len(unread), send),
        in_specs=[VMEM] * (groups + len(blocks)) + [ANY] * len(unread) + [VMEM] * len(states),
        out_specs=[VMEM] * len(out_shape),
        out_shape=out_shape,
        input_output_aliases={before + i: i for i in range(len(states))},
        compiler_params=params(),
        cost_estimate=pl.CostEstimate(
            flops=HERE * lanes * keys * DH * 8,
            bytes_accessed=HERE * ACC * lanes * 4,
            transcendentals=HERE * lanes * keys,
        ),
        name="attend",
    )(*queries, *blocks, *unread, *states)


def merged(acc, top, got):
    total = acc[DH : DH + 1]
    mine = top + jnp.log2(total)
    theirs = got[DH : DH + 1] + got[DH + 1 : DH + 2] + got[DH + 2 : DH + 3]
    share = 1.0 / (1.0 + jnp.exp2(theirs - mine))
    other = 1.0 / (1.0 + jnp.exp2(mine - theirs))
    return acc[:DH] * (share / total) + got[:DH] * other


def combine_kernel(
    acc_ref, top_ref, text_acc, text_top, got_ref, w_hbm, upper_ref, lower_ref, w_ref, rows_ref, sem
):
    copy = pltpu.make_async_copy(w_hbm, w_ref, sem)
    copy.start()

    @pl.loop(0, HERE)
    def _(h):
        at, _ = columns_of(h)
        video = merged(acc_ref[h], top_ref[h, :1], got_ref[h, :, :VID].astype(F32)).T.astype(BF16)
        upper_ref[:, at] = video[:UPPER]
        lower_ref[:LOWER, at] = video[UPPER:]
        got = pltpu.roll(got_ref[h, :, VID:].astype(F32), TXTR, 1)
        rows = merged(text_acc[h, :, VID:], text_top[h, :1, VID:], got).T
        rows_ref[:, at] = rows[: 2 * TXTR].astype(BF16)

    copy.wait()
    part = jnp.dot(rows_ref[...], w_ref[...], preferred_element_type=F32)[TXTR:]
    chunks = [part[:, j * WIDTH : (j + 1) * WIDTH] for j in range(CHUNKS)]
    lower_ref[LOWER:] = jnp.concatenate(chunks, axis=0).astype(BF16)


def combine(own, theirs, got, out_text):
    return pl.pallas_call(
        combine_kernel,
        in_specs=[VMEM] * 5 + [HBM],
        out_specs=[VMEM] * 2,
        out_shape=[
            jax.ShapeDtypeStruct((UPPER, WIDTH), BF16),
            jax.ShapeDtypeStruct((LOWER + CHUNKS * TXTR, WIDTH), BF16),
        ],
        scratch_shapes=[
            pltpu.VMEM((WIDTH, MODEL_WIDTH), BF16),
            pltpu.VMEM((2 * TXTR, WIDTH), BF16),
            pltpu.SemaphoreType.DMA(()),
        ],
        compiler_params=params(),
        cost_estimate=pl.CostEstimate(flops=10**9, bytes_accessed=10**7, transcendentals=0),
        name="combine",
    )(*own, *theirs, got, out_text)


def slice_kernel(steps, unread, at_ref, w_ref, *refs):
    out_refs, sems = refs[unread : unread + len(steps)], refs[unread + len(steps) :]
    copies = []
    for k, out_ref, sem in zip(steps, out_refs, sems, strict=True):
        first = lax.rem(at_ref[0] + 4 - k, 4) * (2 * WIDTH)
        columns = pl.ds(pl.multiple_of(first, 2 * WIDTH), 2 * WIDTH)
        copies.append(pltpu.make_async_copy(w_ref.at[:, columns], out_ref, sem))
        copies[-1].start()
    for copy in copies:
        copy.wait()


def column_slices(at, weight, steps, unread=()):
    return pl.pallas_call(
        functools.partial(slice_kernel, steps, len(unread)),
        in_specs=[SMEM, HBM] + [ANY] * len(unread),
        out_specs=[VMEM] * len(steps),
        out_shape=[jax.ShapeDtypeStruct((WIDTH, 2 * WIDTH), BF16)] * len(steps),
        scratch_shapes=[pltpu.SemaphoreType.DMA(())] * len(steps),
        compiler_params=params(),
        name="columns",
    )(at, weight, *unread)


def own_kernel(arrived_ref, upper_ref, lower_ref, w_ref, upper_out, lower_out, again_ref):
    del arrived_ref
    again_ref[...] = lower_ref[...]
    upper_out[...] = jnp.dot(upper_ref[...], w_ref[...], preferred_element_type=F32)
    lower_out[...] = jnp.dot(lower_ref[:LOWER], w_ref[...], preferred_element_type=F32)


def project_own(arrived, upper, lower, weight):
    return pl.pallas_call(
        own_kernel,
        in_specs=[ANY] + [VMEM] * 3,
        out_specs=[VMEM] * 3,
        out_shape=[
            *[jax.ShapeDtypeStruct((rows, 2 * WIDTH), F32) for rows in (UPPER, LOWER)],
            jax.ShapeDtypeStruct(lower.shape, BF16),
        ],
        compiler_params=params(),
        cost_estimate=pl.CostEstimate(flops=10**9, bytes_accessed=5 * 10**6, transcendentals=0),
        name="project_own",
    )(arrived, upper, lower, weight)


def products(total, att, weights):
    for a, w in zip(att, weights, strict=True):
        total = total + jnp.dot(a[: total.shape[0]], w[...], preferred_element_type=F32)
    return total


def more_kernel(n, sum_ref, *refs):
    refs[2 * n][...] = products(sum_ref[...], refs[:n], refs[n : 2 * n])


def project_more(total, att, weights):
    n = len(att)
    return pl.pallas_call(
        functools.partial(more_kernel, n),
        in_specs=[VMEM] * (1 + 2 * n),
        out_specs=VMEM,
        out_shape=jax.ShapeDtypeStruct(total.shape, F32),
        input_output_aliases={0: 0},
        compiler_params=params(),
        cost_estimate=pl.CostEstimate(flops=10**9, bytes_accessed=5 * 10**6, transcendentals=0),
        name="project_more",
    )(total, *att, *weights)


def last_kernel(n, at_ref, sum_ref, *refs):
    att, weights, texts, sent_ref, mine_ref = refs[:n], refs[n : 2 * n], refs[2 * n : -2], refs[-2], refs[-1]
    left = at_ref[1] == 0
    count = sum_ref.shape[0]
    rows = products(sum_ref[...], att, weights)
    one, two = rows[:, :WIDTH], rows[:, WIDTH:]
    mine_ref[:count] = jnp.where(left, one, two)
    sent_ref[:count] = jnp.where(left, two, one).astype(BF16)
    if texts:
        at = pl.ds(pl.multiple_of(count + at_ref[0] * (2 * TXTR), 2 * TXTR), 2 * TXTR)
        text = sum(a[at].astype(F32) for a in texts)
        mine = jnp.where(left, text[:TXTR], text[TXTR:])
        sent = jnp.where(left, text[TXTR:], text[:TXTR])
        mine_ref[count:] = jnp.concatenate([mine, mine], axis=0)
        sent_ref[count:] = jnp.concatenate([sent, sent], axis=0).astype(BF16)


def project_last(at, total, att, weights, texts=()):
    rows = total.shape[0] + (2 * TXTR if texts else 0)
    return pl.pallas_call(
        functools.partial(last_kernel, len(att)),
        in_specs=[SMEM] + [VMEM] * (1 + 2 * len(att) + len(texts)),
        out_specs=[VMEM] * 2,
        out_shape=[jax.ShapeDtypeStruct((rows, WIDTH), BF16), jax.ShapeDtypeStruct((rows, WIDTH), F32)],
        compiler_params=params(),
        cost_estimate=pl.CostEstimate(flops=10**9, bytes_accessed=5 * 10**6, transcendentals=0),
        name="project_last",
    )(at, total, *att, *weights, *texts)


def residual_kernel(
    own_a, got_a, own_b, got_b, xv_ref, xt_ref, mv_ref, mt_ref, xv_out, xt_out, res_ref, sums_ref
):
    gate = mv_ref[:1]
    upper = xv_ref[:UPPER].astype(F32) + gate * (own_a[...] + got_a[...].astype(F32))
    lower = xv_ref[UPPER:].astype(F32) + gate * (own_b[:LOWER] + got_b[:LOWER].astype(F32))
    text_proj = own_b[LOWER:] + got_b[LOWER:].astype(F32)
    text = xt_ref[...].astype(F32) + mt_ref[:1] * text_proj[:TXTR]
    xv_out[:UPPER] = upper.astype(BF16)
    xv_out[UPPER:] = lower.astype(BF16)
    xt_out[...] = text.astype(BF16)
    rows = jnp.concatenate([upper, lower, text], axis=0)
    res_ref[...] = rows
    count = VID + TXTR
    lane = lax.broadcasted_iota(jnp.int32, (count, 128), 1)
    sums = jnp.where(
        lane == 0,
        jnp.sum(rows, axis=1, keepdims=True),
        jnp.where(lane == 1, jnp.sum(rows * rows, axis=1, keepdims=True), 0.0),
    )
    sums = jnp.concatenate([sums, jnp.zeros((SUM_ROWS - count, 128), F32)], axis=0)
    sums_ref[...] = sums.T[:8]


def norm_kernel(res_ref, mv_ref, mt_ref, s0_ref, s1_ref, s2_ref, s3_ref, video_out, text_out):
    sums = (s0_ref[...] + s1_ref[...]) + (s2_ref[...] + s3_ref[...])
    sums = jnp.concatenate([sums, jnp.zeros((120, SUM_ROWS), F32)], axis=0).T
    mean = sums[: VID + TXTR, :1] / MODEL_WIDTH
    var = sums[: VID + TXTR, 1:2] / MODEL_WIDTH - mean * mean
    normed = (res_ref[...] - mean) * lax.rsqrt(var + 1e-06)
    video_out[...] = (normed[:VID] * (1.0 + mv_ref[2:3]) + mv_ref[1:2]).astype(BF16)
    text_out[...] = (normed[VID:] * (1.0 + mt_ref[2:3]) + mt_ref[1:2]).astype(BF16)


def local(
    q_video, k_video, video_value_rows, q_text, k_text, v_text, x_video, x_text, out_video, out_text, mod_video, mod_text
):
    def over_seq(move):
        pairs = []
        for y in range(2):
            for z in range(8):
                for c in range(2):
                    a, b, d = move(y, z, c)
                    pairs.append(((y * 8 + z) * 2 + c, ((a % 2) * 8 + b % 8) * 2 + d % 2))
        return lambda value: lax.ppermute(value, "seq", pairs)

    def over_head(move):
        pairs = []
        for x in range(4):
            for y in range(2):
                a, b = move(x, y)
                pairs.append((x * 2 + y, (a % 4) * 2 + b % 2))
        return lambda value: lax.ppermute(value, "head", pairs)

    other_core = over_seq(lambda y, z, c: (y, z, 1 - c))
    other_plane = over_seq(lambda y, z, c: (1 - y, z, c))
    up = over_seq(lambda y, z, c: (y, z + 1, c))
    down = over_seq(lambda y, z, c: (y, z - 1, c))
    across = over_seq(lambda y, z, c: (1 - y, z - 1, c))
    from_on = [None] + [over_head(lambda x, y, k=k: (x - k, y)) for k in (1, 2, 3)]
    pair = over_head(lambda x, y: (x, 1 - y))

    head = lax.axis_index("head")
    x_at = head // 2
    at = jnp.stack([x_at, head % 2]).astype(jnp.int32)

    own = jnp.concatenate(
        [
            jnp.concatenate([k_video, video_value_rows], axis=1),
            jnp.concatenate([k_text, v_text], axis=1),
            jnp.zeros((BLOCK - KB - TXTR, 2 * WIDTH), BF16),
        ],
        axis=0,
    )
    q_other = other_core(jnp.concatenate([q_video, q_text], axis=0))
    y0, r1, l1 = other_plane(own), up(own), down(own)
    r2, l2 = up(r1), down(l1)
    yr1, yl1 = other_plane(r1), other_plane(l1)
    r3, l3 = up(r2), down(l2)
    ry2, ly2 = up(yr1), down(yl1)
    r4, opposite = up(r3), across(l3)
    ry3, ly3 = up(ry2), down(ly2)

    q_theirs = jnp.concatenate([q_other, q_text, jnp.zeros((THEIRS - VID - 2 * TXTR, WIDTH), BF16)], axis=0)
    queries = [q_theirs, q_video]
    states = attend(queries, [own, r1, l1, y0])

    here, slice_1 = column_slices(at, out_video, (0, 1), unread=[own])
    weight_1 = from_on[1](slice_1)
    [slice_2] = column_slices(at, out_video, (2,), unread=[weight_1, states[1]])
    weight_2 = from_on[2](slice_2)
    [slice_3] = column_slices(at, out_video, (3,), unread=[weight_2])
    weights = [here, weight_1, weight_2, from_on[3](slice_3)]

    states = attend(queries, [r2, l2, yr1, yl1], states)
    states = attend(queries, [r3, l3, ry2, ly2], states, unread=[weights[2]])
    states = attend(queries, [r4, opposite], states)
    every = [ry3, ly3, own, r1, l1, y0, r2, l2, yr1, yl1, r3, l3, ry2, ly2, r4, opposite]
    *theirs, sent = attend(queries[:1], [ry3, ly3], states[:2], every=every, unread=[weights[3]], send=True)
    got = other_core(sent)
    mine = attend(queries[1:], [ry3, ly3], states[2:], every=every)

    upper, lower = combine(mine, theirs, got, out_text)
    upper_1, upper_3, lower_3 = from_on[1](upper), from_on[3](upper), from_on[3](lower)
    upper_2 = from_on[1](upper_1)
    sum_a, sum_b, lower_again = project_own(upper_1, upper, lower, weights[0])
    lower_1, lower_2 = from_on[1](lower_again), from_on[3](lower_3)
    sum_a = project_more(sum_a, [upper_1, upper_3], [weights[1], weights[3]])
    sent_a, own_a = project_last(at, sum_a, [upper_2], weights[2:3])
    got_a = pair(sent_a)
    sum_b = project_more(sum_b, [lower_3], weights[3:])
    messages = [lower, lower_1, lower_2, lower_3]
    sent_b, own_b = project_last(at, sum_b, messages[1:3], weights[1:3], messages)
    got_b = pair(sent_b)

    x_video_out, x_text_out, residual, sums = pl.pallas_call(
        residual_kernel,
        in_specs=[VMEM] * 8,
        out_specs=[VMEM] * 4,
        out_shape=[
            jax.ShapeDtypeStruct((VID, WIDTH), BF16),
            jax.ShapeDtypeStruct((TXTR, WIDTH), BF16),
            jax.ShapeDtypeStruct((VID + TXTR, WIDTH), F32),
            jax.ShapeDtypeStruct((8, SUM_ROWS), F32),
        ],
        compiler_params=params(),
        name="residual",
    )(own_a, got_a, own_b, got_b, x_video, x_text, mod_video, mod_text)
    sums = sums + pair(sums)
    mlp_video_in, mlp_text_in = pl.pallas_call(
        norm_kernel,
        in_specs=[VMEM] * 7,
        out_specs=[VMEM] * 2,
        out_shape=[jax.ShapeDtypeStruct((VID, WIDTH), BF16), jax.ShapeDtypeStruct((TXTR, WIDTH), BF16)],
        compiler_params=params(),
        name="norm",
    )(residual, mod_video, mod_text, sums, *[from_on[k](sums) for k in (1, 2, 3)])
    return x_video_out, mlp_video_in, x_text_out, mlp_text_in


def solution(mesh):
    tokens, rows, columns = P("seq", "head"), P("head", None), P(None, "head")
    return jax.shard_map(
        local,
        mesh=mesh,
        in_specs=(tokens,) * 8 + (rows, rows, columns, columns),
        out_specs=(tokens,) * 4,
        check_vma=False,
    )
```

```python
import functools
import math

import jax
import jax.numpy as jnp
from jax import lax
from jax.experimental import pallas as pl
from jax.experimental.pallas import tpu as pltpu
from jax.sharding import PartitionSpec as P

MODEL_WIDTH = 3072
DH = 128
HERE = 3
WIDTH = HERE * DH
VID = 896
UPPER, LOWER = 480, 416
TXTR = 8
THEIRS = VID + 128
ACC = 144
KB = 256
BLOCK = KB + 16
CHUNKS = MODEL_WIDTH // WIDTH
SUM_ROWS = 1024
SCALE = math.log2(math.e) / math.sqrt(DH)
LIMIT = 1e30
NT = (((1,), (1,)), ((), ()))
F32, BF16 = jnp.float32, jnp.bfloat16
VMEM = pl.BlockSpec(memory_space=pltpu.VMEM)
SMEM = pl.BlockSpec(memory_space=pltpu.SMEM)
ANY = pl.BlockSpec(memory_space=pl.ANY)
HBM = pl.BlockSpec(memory_space=pltpu.HBM)


def params():
    return pltpu.CompilerParams(vmem_limit_bytes=30 * 2**20)


def with_ones(v):
    return jnp.concatenate([v.T, jnp.ones((ACC - DH, v.shape[0]), BF16)], axis=0)


def scores_of(k, q):
    return lax.dot_general(k, q, NT, preferred_element_type=F32) * SCALE


def rows_of(refs, columns):
    return [r[:KB, columns] for r in refs]


def text_of(refs, columns):
    rows = [r[KB:, columns].astype(F32)[:TXTR] for r in refs]
    return jnp.concatenate(rows, axis=0).astype(BF16)


def safe_head(q, keys, values, acc, top):
    for k, v in zip(keys, values, strict=True):
        s = scores_of(k, q)
        new_top = jnp.maximum(top, jnp.max(s, axis=0, keepdims=True))
        p = jnp.exp2(s - new_top).astype(BF16)
        acc = acc * jnp.exp2(top - new_top) + jnp.dot(with_ones(v), p, preferred_element_type=F32)
        top = new_top
    return acc, top


def columns_of(head):
    at = head * DH if isinstance(head, int) else pl.multiple_of(head * DH, DH)
    return pl.ds(at, DH), pl.ds(WIDTH + at, DH)


def attend_kernel(groups, n, texts, first, unread, send, *refs):
    q_refs, refs = refs[:groups], refs[groups:]
    blocks, text_blocks = refs[:n], refs[:texts]
    refs = refs[max(n, texts) + unread :]
    before, after = (None, refs) if first else (refs[: 2 * groups], refs[2 * groups :])

    def text_operands(h):
        key_at, value_at = columns_of(h)
        if not texts:
            return [], []
        return [text_of(text_blocks, key_at)], [text_of(text_blocks, value_at)]

    added, tops = {}, {}
    for h in range(HERE):
        key_at, value_at = columns_of(h)
        keys, values = rows_of(blocks, key_at), rows_of(blocks, value_at)
        pairs = [(keys[i : i + 2], values[i : i + 2]) for i in range(0, n, 2)]
        if texts:
            pairs.append(text_operands(h))
        for g in range(groups):
            q = q_refs[g][:, key_at]
            top = jnp.zeros((1, q.shape[0]), F32) if first else before[2 * g + 1][h, :1]
            total = None
            for k, v in pairs:
                p = jnp.exp2(scores_of(jnp.concatenate(k, axis=0), q) - top).astype(BF16)
                d = jnp.dot(with_ones(jnp.concatenate(v, axis=0)), p, preferred_element_type=F32)
                total = d if total is None else total + d
            added[g, h], tops[g, h] = total, top
    totals = jnp.concatenate([a[DH : DH + 1] for a in added.values()], axis=1)
    fine = jnp.max(totals) < LIMIT
    if first:
        fine = jnp.logical_and(fine, jnp.min(totals) > 1e-20)

    @pl.when(fine)
    def _():
        for (g, h), total in added.items():
            after[2 * g][h] = total if first else before[2 * g][h] + total
            after[2 * g + 1][h] = jnp.broadcast_to(tops[g, h], (8, total.shape[1]))

    @pl.when(jnp.logical_not(fine))
    def _():
        @pl.loop(0, HERE)
        def _(h):
            key_at, value_at = columns_of(h)
            for g in range(groups):

                @pl.loop(0, q_refs[g].shape[0] // 128)
                def _(i):
                    lanes = pl.ds(pl.multiple_of(i * 128, 128), 128)
                    more_keys, more_values = text_operands(h)
                    if first:
                        acc, top = jnp.zeros((ACC, 128), F32), jnp.full((1, 128), -1e30, F32)
                    else:
                        acc, top = before[2 * g][h, :, lanes], before[2 * g + 1][h, :1, lanes]
                    acc, top = safe_head(
                        q_refs[g][lanes, key_at],
                        rows_of(blocks, key_at) + more_keys,
                        rows_of(blocks, value_at) + more_values,
                        acc,
                        top,
                    )
                    after[2 * g][h, :, lanes] = acc
                    after[2 * g + 1][h, :, lanes] = jnp.broadcast_to(top, (8, 128))

    if send:
        acc_ref, top_ref, sent_ref = after
        row = lax.broadcasted_iota(jnp.int32, (ACC - DH, acc_ref.shape[2]), 0)

        @pl.loop(0, HERE)
        def _(h):
            total = acc_ref[h, DH : DH + 1]
            inverse = 1.0 / total
            level = top_ref[h, :1] + jnp.log2(total)
            hi = level.astype(BF16).astype(F32)
            mid = (level - hi).astype(BF16).astype(F32)
            low = level - hi - mid
            levels = jnp.where(row == 0, hi, jnp.where(row == 1, mid, jnp.where(row == 2, low, 0.0)))
            sent_ref[h, :DH] = (acc_ref[h, :DH] * inverse).astype(BF16)
            sent_ref[h, DH:] = levels.astype(BF16)


def attend(queries, blocks, states=None, every=(), unread=(), send=False):
    n, texts, groups = len(blocks), len(every), len(queries)
    blocks = [*blocks, *[b for b in every if all(b is not c for c in blocks)]]
    keys = n * KB + texts * TXTR
    lanes = sum(q.shape[0] for q in queries)
    out_shape = []
    for q in queries:
        out_shape.append(jax.ShapeDtypeStruct((HERE, ACC, q.shape[0]), F32))
        out_shape.append(jax.ShapeDtypeStruct((HERE, 8, q.shape[0]), F32))
    if send:
        out_shape.append(jax.ShapeDtypeStruct((HERE, ACC, queries[0].shape[0]), BF16))
    first = states is None
    states = [] if first else states
    before = groups + len(blocks) + len(unread)
    return pl.pallas_call(
        functools.partial(attend_kernel, groups, n, texts, first, len(unread), send),
        in_specs=[VMEM] * (groups + len(blocks)) + [ANY] * len(unread) + [VMEM] * len(states),
        out_specs=[VMEM] * len(out_shape),
        out_shape=out_shape,
        input_output_aliases={before + i: i for i in range(len(states))},
        compiler_params=params(),
        cost_estimate=pl.CostEstimate(
            flops=HERE * lanes * keys * DH * 8,
            bytes_accessed=HERE * ACC * lanes * 4,
            transcendentals=HERE * lanes * keys,
        ),
        name="attend",
    )(*queries, *blocks, *unread, *states)


def merged(acc, top, got):
    total = acc[DH : DH + 1]
    mine = top + jnp.log2(total)
    theirs = got[DH : DH + 1] + got[DH + 1 : DH + 2] + got[DH + 2 : DH + 3]
    share = 1.0 / (1.0 + jnp.exp2(theirs - mine))
    other = 1.0 / (1.0 + jnp.exp2(mine - theirs))
    return acc[:DH] * (share / total) + got[:DH] * other


def combine_kernel(
    acc_ref, top_ref, text_acc, text_top, got_ref, w_hbm, upper_ref, lower_ref, w_ref, rows_ref, sem
):
    copy = pltpu.make_async_copy(w_hbm, w_ref, sem)
    copy.start()

    @pl.loop(0, HERE)
    def _(h):
        at, _ = columns_of(h)
        video = merged(acc_ref[h], top_ref[h, :1], got_ref[h, :, :VID].astype(F32)).T.astype(BF16)
        upper_ref[:, at] = video[:UPPER]
        lower_ref[:LOWER, at] = video[UPPER:]
        got = pltpu.roll(got_ref[h, :, VID:].astype(F32), TXTR, 1)
        rows = merged(text_acc[h, :, VID:], text_top[h, :1, VID:], got).T
        rows_ref[:, at] = rows[: 2 * TXTR].astype(BF16)

    copy.wait()
    part = jnp.dot(rows_ref[...], w_ref[...], preferred_element_type=F32)[TXTR:]
    chunks = [part[:, j * WIDTH : (j + 1) * WIDTH] for j in range(CHUNKS)]
    lower_ref[LOWER:] = jnp.concatenate(chunks, axis=0).astype(BF16)


def combine(own, theirs, got, out_text):
    return pl.pallas_call(
        combine_kernel,
        in_specs=[VMEM] * 5 + [HBM],
        out_specs=[VMEM] * 2,
        out_shape=[
            jax.ShapeDtypeStruct((UPPER, WIDTH), BF16),
            jax.ShapeDtypeStruct((LOWER + CHUNKS * TXTR, WIDTH), BF16),
        ],
        scratch_shapes=[
            pltpu.VMEM((WIDTH, MODEL_WIDTH), BF16),
            pltpu.VMEM((2 * TXTR, WIDTH), BF16),
            pltpu.SemaphoreType.DMA(()),
        ],
        compiler_params=params(),
        cost_estimate=pl.CostEstimate(flops=10**9, bytes_accessed=10**7, transcendentals=0),
        name="combine",
    )(*own, *theirs, got, out_text)


def slice_kernel(steps, unread, at_ref, w_ref, *refs):
    out_refs, sems = refs[unread : unread + len(steps)], refs[unread + len(steps) :]
    copies = []
    for k, out_ref, sem in zip(steps, out_refs, sems, strict=True):
        first = lax.rem(at_ref[0] + 4 - k, 4) * (2 * WIDTH)
        columns = pl.ds(pl.multiple_of(first, 2 * WIDTH), 2 * WIDTH)
        copies.append(pltpu.make_async_copy(w_ref.at[:, columns], out_ref, sem))
        copies[-1].start()
    for copy in copies:
        copy.wait()


def column_slices(at, weight, steps, unread=()):
    return pl.pallas_call(
        functools.partial(slice_kernel, steps, len(unread)),
        in_specs=[SMEM, HBM] + [ANY] * len(unread),
        out_specs=[VMEM] * len(steps),
        out_shape=[jax.ShapeDtypeStruct((WIDTH, 2 * WIDTH), BF16)] * len(steps),
        scratch_shapes=[pltpu.SemaphoreType.DMA(())] * len(steps),
        compiler_params=params(),
        name="columns",
    )(at, weight, *unread)


def own_kernel(arrived_ref, upper_ref, lower_ref, w_ref, upper_out, lower_out, again_ref):
    del arrived_ref
    again_ref[...] = lower_ref[...]
    upper_out[...] = jnp.dot(upper_ref[...], w_ref[...], preferred_element_type=F32)
    lower_out[...] = jnp.dot(lower_ref[:LOWER], w_ref[...], preferred_element_type=F32)


def project_own(arrived, upper, lower, weight):
    return pl.pallas_call(
        own_kernel,
        in_specs=[ANY] + [VMEM] * 3,
        out_specs=[VMEM] * 3,
        out_shape=[
            *[jax.ShapeDtypeStruct((rows, 2 * WIDTH), F32) for rows in (UPPER, LOWER)],
            jax.ShapeDtypeStruct(lower.shape, BF16),
        ],
        compiler_params=params(),
        cost_estimate=pl.CostEstimate(flops=10**9, bytes_accessed=5 * 10**6, transcendentals=0),
        name="project_own",
    )(arrived, upper, lower, weight)


def products(total, att, weights):
    for a, w in zip(att, weights, strict=True):
        total = total + jnp.dot(a[: total.shape[0]], w[...], preferred_element_type=F32)
    return total


def more_kernel(n, sum_ref, *refs):
    refs[2 * n][...] = products(sum_ref[...], refs[:n], refs[n : 2 * n])


def project_more(total, att, weights):
    n = len(att)
    return pl.pallas_call(
        functools.partial(more_kernel, n),
        in_specs=[VMEM] * (1 + 2 * n),
        out_specs=VMEM,
        out_shape=jax.ShapeDtypeStruct(total.shape, F32),
        input_output_aliases={0: 0},
        compiler_params=params(),
        cost_estimate=pl.CostEstimate(flops=10**9, bytes_accessed=5 * 10**6, transcendentals=0),
        name="project_more",
    )(total, *att, *weights)


def last_kernel(n, at_ref, sum_ref, *refs):
    att, weights, texts, sent_ref, mine_ref = refs[:n], refs[n : 2 * n], refs[2 * n : -2], refs[-2], refs[-1]
    left = at_ref[1] == 0
    count = sum_ref.shape[0]
    rows = products(sum_ref[...], att, weights)
    one, two = rows[:, :WIDTH], rows[:, WIDTH:]
    mine_ref[:count] = jnp.where(left, one, two)
    sent_ref[:count] = jnp.where(left, two, one).astype(BF16)
    if texts:
        at = pl.ds(pl.multiple_of(count + at_ref[0] * (2 * TXTR), 2 * TXTR), 2 * TXTR)
        text = sum(a[at].astype(F32) for a in texts)
        mine = jnp.where(left, text[:TXTR], text[TXTR:])
        sent = jnp.where(left, text[TXTR:], text[:TXTR])
        mine_ref[count:] = jnp.concatenate([mine, mine], axis=0)
        sent_ref[count:] = jnp.concatenate([sent, sent], axis=0).astype(BF16)


def project_last(at, total, att, weights, texts=()):
    rows = total.shape[0] + (2 * TXTR if texts else 0)
    return pl.pallas_call(
        functools.partial(last_kernel, len(att)),
        in_specs=[SMEM] + [VMEM] * (1 + 2 * len(att) + len(texts)),
        out_specs=[VMEM] * 2,
        out_shape=[jax.ShapeDtypeStruct((rows, WIDTH), BF16), jax.ShapeDtypeStruct((rows, WIDTH), F32)],
        compiler_params=params(),
        cost_estimate=pl.CostEstimate(flops=10**9, bytes_accessed=5 * 10**6, transcendentals=0),
        name="project_last",
    )(at, total, *att, *weights, *texts)


def residual_kernel(
    own_a, got_a, own_b, got_b, xv_ref, xt_ref, mv_ref, mt_ref, xv_out, xt_out, res_ref, sums_ref
):
    gate = mv_ref[:1]
    upper = xv_ref[:UPPER].astype(F32) + gate * (own_a[...] + got_a[...].astype(F32))
    lower = xv_ref[UPPER:].astype(F32) + gate * (own_b[:LOWER] + got_b[:LOWER].astype(F32))
    text_proj = own_b[LOWER:] + got_b[LOWER:].astype(F32)
    text = xt_ref[...].astype(F32) + mt_ref[:1] * text_proj[:TXTR]
    xv_out[:UPPER] = upper.astype(BF16)
    xv_out[UPPER:] = lower.astype(BF16)
    xt_out[...] = text.astype(BF16)
    rows = jnp.concatenate([upper, lower, text], axis=0)
    res_ref[...] = rows
    count = VID + TXTR
    lane = lax.broadcasted_iota(jnp.int32, (count, 128), 1)
    sums = jnp.where(
        lane == 0,
        jnp.sum(rows, axis=1, keepdims=True),
        jnp.where(lane == 1, jnp.sum(rows * rows, axis=1, keepdims=True), 0.0),
    )
    sums = jnp.concatenate([sums, jnp.zeros((SUM_ROWS - count, 128), F32)], axis=0)
    sums_ref[...] = sums.T[:8]


def norm_kernel(res_ref, mv_ref, mt_ref, s0_ref, s1_ref, s2_ref, s3_ref, video_out, text_out):
    sums = (s0_ref[...] + s1_ref[...]) + (s2_ref[...] + s3_ref[...])
    sums = jnp.concatenate([sums, jnp.zeros((120, SUM_ROWS), F32)], axis=0).T
    mean = sums[: VID + TXTR, :1] / MODEL_WIDTH
    var = sums[: VID + TXTR, 1:2] / MODEL_WIDTH - mean * mean
    normed = (res_ref[...] - mean) * lax.rsqrt(var + 1e-06)
    video_out[...] = (normed[:VID] * (1.0 + mv_ref[2:3]) + mv_ref[1:2]).astype(BF16)
    text_out[...] = (normed[VID:] * (1.0 + mt_ref[2:3]) + mt_ref[1:2]).astype(BF16)


def local(
    q_video, k_video, video_value_rows, q_text, k_text, v_text, x_video, x_text, out_video, out_text, mod_video, mod_text
):
    def over_seq(move):
        pairs = []
        for y in range(2):
            for z in range(8):
                for c in range(2):
                    a, b, d = move(y, z, c)
                    pairs.append(((y * 8 + z) * 2 + c, ((a % 2) * 8 + b % 8) * 2 + d % 2))
        return lambda value: lax.ppermute(value, "seq", pairs)

    def over_head(move):
        pairs = []
        for x in range(4):
            for y in range(2):
                a, b = move(x, y)
                pairs.append((x * 2 + y, (a % 4) * 2 + b % 2))
        return lambda value: lax.ppermute(value, "head", pairs)

    other_core = over_seq(lambda y, z, c: (y, z, 1 - c))
    other_plane = over_seq(lambda y, z, c: (1 - y, z, c))
    up = over_seq(lambda y, z, c: (y, z + 1, c))
    down = over_seq(lambda y, z, c: (y, z - 1, c))
    across = over_seq(lambda y, z, c: (1 - y, z - 1, c))
    from_on = [None] + [over_head(lambda x, y, k=k: (x - k, y)) for k in (1, 2, 3)]
    pair = over_head(lambda x, y: (x, 1 - y))

    head = lax.axis_index("head")
    x_at = head // 2
    at = jnp.stack([x_at, head % 2]).astype(jnp.int32)

    own = jnp.concatenate(
        [
            jnp.concatenate([k_video, video_value_rows], axis=1),
            jnp.concatenate([k_text, v_text], axis=1),
            jnp.zeros((BLOCK - KB - TXTR, 2 * WIDTH), BF16),
        ],
        axis=0,
    )
    q_other = other_core(jnp.concatenate([q_video, q_text], axis=0))
    y0, r1, l1 = other_plane(own), up(own), down(own)
    r2, l2 = up(r1), down(l1)
    yr1, yl1 = other_plane(r1), other_plane(l1)
    r3, l3 = up(r2), down(l2)
    ry2, ly2 = up(yr1), down(yl1)
    r4, opposite = up(r3), across(l3)
    ry3, ly3 = up(ry2), down(ly2)

    here, slice_1 = column_slices(at, out_video, (0, 1), unread=[q_other])
    weight_1 = from_on[1](slice_1)
    [slice_2] = column_slices(at, out_video, (2,), unread=[y0, weight_1])
    weight_2 = from_on[2](slice_2)
    [slice_3] = column_slices(at, out_video, (3,), unread=[weight_2])
    weights = [here, weight_1, weight_2, from_on[3](slice_3)]

    q_theirs = jnp.concatenate([q_other, q_text, jnp.zeros((THEIRS - VID - 2 * TXTR, WIDTH), BF16)], axis=0)
    queries = [q_theirs, q_video]
    states = attend(queries, [own, r1, l1, y0])
    states = attend(queries, [r2, l2, yr1, yl1], states)
    states = attend(queries, [r3, l3, ry2, ly2], states, unread=[weights[2]])
    states = attend(queries, [r4, opposite], states)
    every = [ry3, ly3, own, r1, l1, y0, r2, l2, yr1, yl1, r3, l3, ry2, ly2, r4, opposite]
    *theirs, sent = attend(queries[:1], [ry3, ly3], states[:2], every=every, unread=[weights[3]], send=True)
    got = other_core(sent)
    mine = attend(queries[1:], [ry3, ly3], states[2:], every=every)

    upper, lower = combine(mine, theirs, got, out_text)
    upper_1, upper_3, lower_3 = from_on[1](upper), from_on[3](upper), from_on[3](lower)
    upper_2 = from_on[1](upper_1)
    sum_a, sum_b, lower_again = project_own(upper_1, upper, lower, weights[0])
    lower_1, lower_2 = from_on[1](lower_again), from_on[3](lower_3)
    sum_a = project_more(sum_a, [upper_1, upper_3], [weights[1], weights[3]])
    sent_a, own_a = project_last(at, sum_a, [upper_2], weights[2:3])
    got_a = pair(sent_a)
    sum_b = project_more(sum_b, [lower_3], weights[3:])
    messages = [lower, lower_1, lower_2, lower_3]
    sent_b, own_b = project_last(at, sum_b, messages[1:3], weights[1:3], messages)
    got_b = pair(sent_b)

    x_video_out, x_text_out, residual, sums = pl.pallas_call(
        residual_kernel,
        in_specs=[VMEM] * 8,
        out_specs=[VMEM] * 4,
        out_shape=[
            jax.ShapeDtypeStruct((VID, WIDTH), BF16),
            jax.ShapeDtypeStruct((TXTR, WIDTH), BF16),
            jax.ShapeDtypeStruct((VID + TXTR, WIDTH), F32),
            jax.ShapeDtypeStruct((8, SUM_ROWS), F32),
        ],
        compiler_params=params(),
        name="residual",
    )(own_a, got_a, own_b, got_b, x_video, x_text, mod_video, mod_text)
    sums = sums + pair(sums)
    mlp_video_in, mlp_text_in = pl.pallas_call(
        norm_kernel,
        in_specs=[VMEM] * 7,
        out_specs=[VMEM] * 2,
        out_shape=[jax.ShapeDtypeStruct((VID, WIDTH), BF16), jax.ShapeDtypeStruct((TXTR, WIDTH), BF16)],
        compiler_params=params(),
        name="norm",
    )(residual, mod_video, mod_text, sums, *[from_on[k](sums) for k in (1, 2, 3)])
    return x_video_out, mlp_video_in, x_text_out, mlp_text_in


def solution(mesh):
    tokens, rows, columns = P("seq", "head"), P("head", None), P(None, "head")
    return jax.shard_map(
        local,
        mesh=mesh,
        in_specs=(tokens,) * 8 + (rows, rows, columns, columns),
        out_specs=(tokens,) * 4,
        check_vma=False,
    )
```

```python
import functools
import math

import jax
import jax.numpy as jnp
from jax import lax
from jax.experimental import pallas as pl
from jax.experimental.pallas import tpu as pltpu
from jax.sharding import PartitionSpec as P

MODEL_WIDTH = 3072
DH = 128
HERE = 3
WIDTH = HERE * DH
VID = 896
UPPER, LOWER = 480, 416
TXTR = 8
THEIRS = VID + 128
ACC = 144
KB = 256
BLOCK = KB + 16
CHUNKS = MODEL_WIDTH // WIDTH
SUM_ROWS = 1024
SCALE = math.log2(math.e) / math.sqrt(DH)
LIMIT = 1e30
NT = (((1,), (1,)), ((), ()))
F32, BF16 = jnp.float32, jnp.bfloat16
VMEM = pl.BlockSpec(memory_space=pltpu.VMEM)
SMEM = pl.BlockSpec(memory_space=pltpu.SMEM)
ANY = pl.BlockSpec(memory_space=pl.ANY)
HBM = pl.BlockSpec(memory_space=pltpu.HBM)


def params():
    return pltpu.CompilerParams(vmem_limit_bytes=30 * 2**20)


def with_ones(v):
    return jnp.concatenate([v.T, jnp.ones((ACC - DH, v.shape[0]), BF16)], axis=0)


def scores_of(k, q):
    return lax.dot_general(k, q, NT, preferred_element_type=F32) * SCALE


def rows_of(refs, columns):
    return [r[:KB, columns] for r in refs]


def text_of(refs, columns):
    rows = [r[KB:, columns].astype(F32)[:TXTR] for r in refs]
    return jnp.concatenate(rows, axis=0).astype(BF16)


def safe_head(q, keys, values, acc, top):
    for k, v in zip(keys, values, strict=True):
        s = scores_of(k, q)
        new_top = jnp.maximum(top, jnp.max(s, axis=0, keepdims=True))
        p = jnp.exp2(s - new_top).astype(BF16)
        acc = acc * jnp.exp2(top - new_top) + jnp.dot(with_ones(v), p, preferred_element_type=F32)
        top = new_top
    return acc, top


def columns_of(head):
    at = head * DH if isinstance(head, int) else pl.multiple_of(head * DH, DH)
    return pl.ds(at, DH), pl.ds(WIDTH + at, DH)


def attend_kernel(groups, n, texts, first, unread, send, *refs):
    q_refs, refs = refs[:groups], refs[groups:]
    blocks, text_blocks = refs[:n], refs[:texts]
    refs = refs[max(n, texts) + unread :]
    before, after = (None, refs) if first else (refs[: 2 * groups], refs[2 * groups :])

    def text_operands(h):
        key_at, value_at = columns_of(h)
        if not texts:
            return [], []
        return [text_of(text_blocks, key_at)], [text_of(text_blocks, value_at)]

    added, tops = {}, {}
    for h in range(HERE):
        key_at, value_at = columns_of(h)
        keys, values = rows_of(blocks, key_at), rows_of(blocks, value_at)
        pairs = [(keys[i : i + 2], values[i : i + 2]) for i in range(0, n, 2)]
        if texts:
            pairs.append(text_operands(h))
        for g in range(groups):
            q = q_refs[g][:, key_at]
            top = jnp.zeros((1, q.shape[0]), F32) if first else before[2 * g + 1][h, :1]
            total = None
            for k, v in pairs:
                p = jnp.exp2(scores_of(jnp.concatenate(k, axis=0), q) - top).astype(BF16)
                d = jnp.dot(with_ones(jnp.concatenate(v, axis=0)), p, preferred_element_type=F32)
                total = d if total is None else total + d
            added[g, h], tops[g, h] = total, top
    totals = jnp.concatenate([a[DH : DH + 1] for a in added.values()], axis=1)
    fine = jnp.max(totals) < LIMIT
    if first:
        fine = jnp.logical_and(fine, jnp.min(totals) > 1e-20)

    @pl.when(fine)
    def _():
        for (g, h), total in added.items():
            after[2 * g][h] = total if first else before[2 * g][h] + total
            after[2 * g + 1][h] = jnp.broadcast_to(tops[g, h], (8, total.shape[1]))

    @pl.when(jnp.logical_not(fine))
    def _():
        @pl.loop(0, HERE)
        def _(h):
            key_at, value_at = columns_of(h)
            for g in range(groups):

                @pl.loop(0, q_refs[g].shape[0] // 128)
                def _(i):
                    lanes = pl.ds(pl.multiple_of(i * 128, 128), 128)
                    more_keys, more_values = text_operands(h)
                    if first:
                        acc, top = jnp.zeros((ACC, 128), F32), jnp.full((1, 128), -1e30, F32)
                    else:
                        acc, top = before[2 * g][h, :, lanes], before[2 * g + 1][h, :1, lanes]
                    acc, top = safe_head(
                        q_refs[g][lanes, key_at],
                        rows_of(blocks, key_at) + more_keys,
                        rows_of(blocks, value_at) + more_values,
                        acc,
                        top,
                    )
                    after[2 * g][h, :, lanes] = acc
                    after[2 * g + 1][h, :, lanes] = jnp.broadcast_to(top, (8, 128))

    if send:
        acc_ref, top_ref, sent_ref = after
        row = lax.broadcasted_iota(jnp.int32, (ACC - DH, acc_ref.shape[2]), 0)

        @pl.loop(0, HERE)
        def _(h):
            total = acc_ref[h, DH : DH + 1]
            inverse = 1.0 / total
            level = top_ref[h, :1] + jnp.log2(total)
            hi = level.astype(BF16).astype(F32)
            mid = (level - hi).astype(BF16).astype(F32)
            low = level - hi - mid
            levels = jnp.where(row == 0, hi, jnp.where(row == 1, mid, jnp.where(row == 2, low, 0.0)))
            sent_ref[h, :DH] = (acc_ref[h, :DH] * inverse).astype(BF16)
            sent_ref[h, DH:] = levels.astype(BF16)


def attend(queries, blocks, states=None, every=(), unread=(), send=False):
    n, texts, groups = len(blocks), len(every), len(queries)
    blocks = [*blocks, *[b for b in every if all(b is not c for c in blocks)]]
    keys = n * KB + texts * TXTR
    lanes = sum(q.shape[0] for q in queries)
    out_shape = []
    for q in queries:
        out_shape.append(jax.ShapeDtypeStruct((HERE, ACC, q.shape[0]), F32))
        out_shape.append(jax.ShapeDtypeStruct((HERE, 8, q.shape[0]), F32))
    if send:
        out_shape.append(jax.ShapeDtypeStruct((HERE, ACC, queries[0].shape[0]), BF16))
    first = states is None
    states = [] if first else states
    before = groups + len(blocks) + len(unread)
    return pl.pallas_call(
        functools.partial(attend_kernel, groups, n, texts, first, len(unread), send),
        in_specs=[VMEM] * (groups + len(blocks)) + [ANY] * len(unread) + [VMEM] * len(states),
        out_specs=[VMEM] * len(out_shape),
        out_shape=out_shape,
        input_output_aliases={before + i: i for i in range(len(states))},
        compiler_params=params(),
        cost_estimate=pl.CostEstimate(
            flops=HERE * lanes * keys * DH * 8,
            bytes_accessed=HERE * ACC * lanes * 4,
            transcendentals=HERE * lanes * keys,
        ),
        name="attend",
    )(*queries, *blocks, *unread, *states)


def merged(acc, top, got):
    total = acc[DH : DH + 1]
    mine = top + jnp.log2(total)
    theirs = got[DH : DH + 1] + got[DH + 1 : DH + 2] + got[DH + 2 : DH + 3]
    share = 1.0 / (1.0 + jnp.exp2(theirs - mine))
    other = 1.0 / (1.0 + jnp.exp2(mine - theirs))
    return acc[:DH] * (share / total) + got[:DH] * other


def combine_kernel(
    acc_ref, top_ref, text_acc, text_top, got_ref, w_hbm, upper_ref, lower_ref, w_ref, rows_ref, sem
):
    copy = pltpu.make_async_copy(w_hbm, w_ref, sem)
    copy.start()

    @pl.loop(0, HERE)
    def _(h):
        at, _ = columns_of(h)
        video = merged(acc_ref[h], top_ref[h, :1], got_ref[h, :, :VID].astype(F32)).T.astype(BF16)
        upper_ref[:, at] = video[:UPPER]
        lower_ref[:LOWER, at] = video[UPPER:]
        got = pltpu.roll(got_ref[h, :, VID:].astype(F32), TXTR, 1)
        rows = merged(text_acc[h, :, VID:], text_top[h, :1, VID:], got).T
        rows_ref[:, at] = rows[: 2 * TXTR].astype(BF16)

    copy.wait()
    part = jnp.dot(rows_ref[...], w_ref[...], preferred_element_type=F32)[TXTR:]
    chunks = [part[:, j * WIDTH : (j + 1) * WIDTH] for j in range(CHUNKS)]
    lower_ref[LOWER:] = jnp.concatenate(chunks, axis=0).astype(BF16)


def combine(own, theirs, got, out_text):
    return pl.pallas_call(
        combine_kernel,
        in_specs=[VMEM] * 5 + [HBM],
        out_specs=[VMEM] * 2,
        out_shape=[
            jax.ShapeDtypeStruct((UPPER, WIDTH), BF16),
            jax.ShapeDtypeStruct((LOWER + CHUNKS * TXTR, WIDTH), BF16),
        ],
        scratch_shapes=[
            pltpu.VMEM((WIDTH, MODEL_WIDTH), BF16),
            pltpu.VMEM((2 * TXTR, WIDTH), BF16),
            pltpu.SemaphoreType.DMA(()),
        ],
        compiler_params=params(),
        cost_estimate=pl.CostEstimate(flops=10**9, bytes_accessed=10**7, transcendentals=0),
        name="combine",
    )(*own, *theirs, got, out_text)


def slice_kernel(steps, unread, at_ref, w_ref, *refs):
    out_refs, sems = refs[unread : unread + len(steps)], refs[unread + len(steps) :]
    copies = []
    for k, out_ref, sem in zip(steps, out_refs, sems, strict=True):
        first = lax.rem(at_ref[0] + 4 - k, 4) * (2 * WIDTH)
        columns = pl.ds(pl.multiple_of(first, 2 * WIDTH), 2 * WIDTH)
        copies.append(pltpu.make_async_copy(w_ref.at[:, columns], out_ref, sem))
        copies[-1].start()
    for copy in copies:
        copy.wait()


def column_slices(at, weight, steps, unread=()):
    return pl.pallas_call(
        functools.partial(slice_kernel, steps, len(unread)),
        in_specs=[SMEM, HBM] + [ANY] * len(unread),
        out_specs=[VMEM] * len(steps),
        out_shape=[jax.ShapeDtypeStruct((WIDTH, 2 * WIDTH), BF16)] * len(steps),
        scratch_shapes=[pltpu.SemaphoreType.DMA(())] * len(steps),
        compiler_params=params(),
        name="columns",
    )(at, weight, *unread)


def own_kernel(arrived_ref, upper_ref, lower_ref, w_ref, upper_out, lower_out, again_ref):
    del arrived_ref
    again_ref[...] = lower_ref[...]
    upper_out[...] = jnp.dot(upper_ref[...], w_ref[...], preferred_element_type=F32)
    lower_out[...] = jnp.dot(lower_ref[:LOWER], w_ref[...], preferred_element_type=F32)


def project_own(arrived, upper, lower, weight):
    return pl.pallas_call(
        own_kernel,
        in_specs=[ANY] + [VMEM] * 3,
        out_specs=[VMEM] * 3,
        out_shape=[
            *[jax.ShapeDtypeStruct((rows, 2 * WIDTH), F32) for rows in (UPPER, LOWER)],
            jax.ShapeDtypeStruct(lower.shape, BF16),
        ],
        compiler_params=params(),
        cost_estimate=pl.CostEstimate(flops=10**9, bytes_accessed=5 * 10**6, transcendentals=0),
        name="project_own",
    )(arrived, upper, lower, weight)


def products(total, att, weights):
    for a, w in zip(att, weights, strict=True):
        total = total + jnp.dot(a[: total.shape[0]], w[...], preferred_element_type=F32)
    return total


def more_kernel(n, sum_ref, *refs):
    refs[2 * n][...] = products(sum_ref[...], refs[:n], refs[n : 2 * n])


def project_more(total, att, weights):
    n = len(att)
    return pl.pallas_call(
        functools.partial(more_kernel, n),
        in_specs=[VMEM] * (1 + 2 * n),
        out_specs=VMEM,
        out_shape=jax.ShapeDtypeStruct(total.shape, F32),
        input_output_aliases={0: 0},
        compiler_params=params(),
        cost_estimate=pl.CostEstimate(flops=10**9, bytes_accessed=5 * 10**6, transcendentals=0),
        name="project_more",
    )(total, *att, *weights)


def last_kernel(n, at_ref, sum_ref, *refs):
    att, weights, texts, sent_ref, mine_ref = refs[:n], refs[n : 2 * n], refs[2 * n : -2], refs[-2], refs[-1]
    left = at_ref[1] == 0
    count = sum_ref.shape[0]
    rows = products(sum_ref[...], att, weights)
    one, two = rows[:, :WIDTH], rows[:, WIDTH:]
    mine_ref[:count] = jnp.where(left, one, two)
    sent_ref[:count] = jnp.where(left, two, one).astype(BF16)
    if texts:
        at = pl.ds(pl.multiple_of(count + at_ref[0] * (2 * TXTR), 2 * TXTR), 2 * TXTR)
        text = sum(a[at].astype(F32) for a in texts)
        mine = jnp.where(left, text[:TXTR], text[TXTR:])
        sent = jnp.where(left, text[TXTR:], text[:TXTR])
        mine_ref[count:] = jnp.concatenate([mine, mine], axis=0)
        sent_ref[count:] = jnp.concatenate([sent, sent], axis=0).astype(BF16)


def project_last(at, total, att, weights, texts=()):
    rows = total.shape[0] + (2 * TXTR if texts else 0)
    return pl.pallas_call(
        functools.partial(last_kernel, len(att)),
        in_specs=[SMEM] + [VMEM] * (1 + 2 * len(att) + len(texts)),
        out_specs=[VMEM] * 2,
        out_shape=[jax.ShapeDtypeStruct((rows, WIDTH), BF16), jax.ShapeDtypeStruct((rows, WIDTH), F32)],
        compiler_params=params(),
        cost_estimate=pl.CostEstimate(flops=10**9, bytes_accessed=5 * 10**6, transcendentals=0),
        name="project_last",
    )(at, total, *att, *weights, *texts)


def row_sums(rows):
    count = rows.shape[0]
    lane = lax.broadcasted_iota(jnp.int32, (count, 128), 1)
    sums = jnp.where(
        lane == 0,
        jnp.sum(rows, axis=1, keepdims=True),
        jnp.where(lane == 1, jnp.sum(rows * rows, axis=1, keepdims=True), 0.0),
    )
    return jnp.concatenate([sums, jnp.zeros((SUM_ROWS // 2 - count, 128), F32)], axis=0).T[:8]


def upper_kernel(own_ref, got_ref, xv_ref, mv_ref, res_ref, sums_ref):
    rows = xv_ref[:UPPER].astype(F32) + mv_ref[:1] * (own_ref[...] + got_ref[...].astype(F32))
    res_ref[...] = rows
    sums_ref[...] = row_sums(rows)


def residual_kernel(
    upper_ref, upper_sums, own_ref, got_ref, xv_ref, xt_ref, mv_ref, mt_ref, xv_out, xt_out, res_ref, sums_ref
):
    lower = xv_ref[UPPER:].astype(F32) + mv_ref[:1] * (own_ref[:LOWER] + got_ref[:LOWER].astype(F32))
    text_proj = own_ref[LOWER:] + got_ref[LOWER:].astype(F32)
    text = xt_ref[...].astype(F32) + mt_ref[:1] * text_proj[:TXTR]
    xv_out[:UPPER] = upper_ref[...].astype(BF16)
    xv_out[UPPER:] = lower.astype(BF16)
    xt_out[...] = text.astype(BF16)
    rows = jnp.concatenate([lower, text], axis=0)
    res_ref[...] = rows
    sums_ref[:, : SUM_ROWS // 2] = upper_sums[...]
    sums_ref[:, SUM_ROWS // 2 :] = row_sums(rows)


def norm_kernel(upper_ref, lower_ref, mv_ref, mt_ref, s0_ref, s1_ref, s2_ref, s3_ref, video_out, text_out):
    sums = (s0_ref[...] + s1_ref[...]) + (s2_ref[...] + s3_ref[...])
    sums = jnp.concatenate([sums, jnp.zeros((120, SUM_ROWS), F32)], axis=0).T

    def normed(res_ref, first):
        part = sums[first : first + res_ref.shape[0]]
        mean = part[:, :1] / MODEL_WIDTH
        var = part[:, 1:2] / MODEL_WIDTH - mean * mean
        return (res_ref[...] - mean) * lax.rsqrt(var + 1e-06)

    upper, lower = normed(upper_ref, 0), normed(lower_ref, SUM_ROWS // 2)
    scale, shift = 1.0 + mv_ref[2:3], mv_ref[1:2]
    video_out[:UPPER] = (upper * scale + shift).astype(BF16)
    video_out[UPPER:] = (lower[:LOWER] * scale + shift).astype(BF16)
    text_out[...] = (lower[LOWER:] * (1.0 + mt_ref[2:3]) + mt_ref[1:2]).astype(BF16)


def local(
    q_video, k_video, video_value_rows, q_text, k_text, v_text, x_video, x_text, out_video, out_text, mod_video, mod_text
):
    def over_seq(move):
        pairs = []
        for y in range(2):
            for z in range(8):
                for c in range(2):
                    a, b, d = move(y, z, c)
                    pairs.append(((y * 8 + z) * 2 + c, ((a % 2) * 8 + b % 8) * 2 + d % 2))
        return lambda value: lax.ppermute(value, "seq", pairs)

    def over_head(move):
        pairs = []
        for x in range(4):
            for y in range(2):
                a, b = move(x, y)
                pairs.append((x * 2 + y, (a % 4) * 2 + b % 2))
        return lambda value: lax.ppermute(value, "head", pairs)

    other_core = over_seq(lambda y, z, c: (y, z, 1 - c))
    other_plane = over_seq(lambda y, z, c: (1 - y, z, c))
    up = over_seq(lambda y, z, c: (y, z + 1, c))
    down = over_seq(lambda y, z, c: (y, z - 1, c))
    across = over_seq(lambda y, z, c: (1 - y, z - 1, c))
    from_on = [None] + [over_head(lambda x, y, k=k: (x - k, y)) for k in (1, 2, 3)]
    pair = over_head(lambda x, y: (x, 1 - y))

    head = lax.axis_index("head")
    x_at = head // 2
    at = jnp.stack([x_at, head % 2]).astype(jnp.int32)

    own = jnp.concatenate(
        [
            jnp.concatenate([k_video, video_value_rows], axis=1),
            jnp.concatenate([k_text, v_text], axis=1),
            jnp.zeros((BLOCK - KB - TXTR, 2 * WIDTH), BF16),
        ],
        axis=0,
    )
    q_other = other_core(jnp.concatenate([q_video, q_text], axis=0))
    y0, r1, l1 = other_plane(own), up(own), down(own)
    r2, l2 = up(r1), down(l1)
    yr1, yl1 = other_plane(r1), other_plane(l1)
    r3, l3 = up(r2), down(l2)
    ry2, ly2 = up(yr1), down(yl1)
    r4, opposite = up(r3), across(l3)
    ry3, ly3 = up(ry2), down(ly2)

    here, slice_1 = column_slices(at, out_video, (0, 1), unread=[q_other])
    weight_1 = from_on[1](slice_1)
    [slice_2] = column_slices(at, out_video, (2,), unread=[y0, weight_1])
    weight_2 = from_on[2](slice_2)
    [slice_3] = column_slices(at, out_video, (3,), unread=[weight_2])
    weights = [here, weight_1, weight_2, from_on[3](slice_3)]

    q_theirs = jnp.concatenate([q_other, q_text, jnp.zeros((THEIRS - VID - 2 * TXTR, WIDTH), BF16)], axis=0)
    queries = [q_theirs, q_video]
    states = attend(queries, [own, r1, l1, y0])
    states = attend(queries, [r2, l2, yr1, yl1], states)
    states = attend(queries, [r3, l3, ry2, ly2], states, unread=[weights[2]])
    states = attend(queries, [r4, opposite], states)
    every = [ry3, ly3, own, r1, l1, y0, r2, l2, yr1, yl1, r3, l3, ry2, ly2, r4, opposite]
    *theirs, sent = attend(queries[:1], [ry3, ly3], states[:2], every=every, unread=[weights[3]], send=True)
    got = other_core(sent)
    mine = attend(queries[1:], [ry3, ly3], states[2:], every=every)

    upper, lower = combine(mine, theirs, got, out_text)
    upper_1, upper_3, lower_3 = from_on[1](upper), from_on[3](upper), from_on[3](lower)
    upper_2 = from_on[1](upper_1)
    sum_a, sum_b, lower_again = project_own(upper_1, upper, lower, weights[0])
    lower_1, lower_2 = from_on[1](lower_again), from_on[3](lower_3)
    sum_a = project_more(sum_a, [upper_1, upper_3], [weights[1], weights[3]])
    sent_a, own_a = project_last(at, sum_a, [upper_2], weights[2:3])
    got_a = pair(sent_a)
    sum_b = project_more(sum_b, [lower_3], weights[3:])
    messages = [lower, lower_1, lower_2, lower_3]
    sent_b, own_b = project_last(at, sum_b, messages[1:3], weights[1:3], messages)
    got_b = pair(sent_b)

    upper_rows, upper_sums = pl.pallas_call(
        upper_kernel,
        in_specs=[VMEM] * 4,
        out_specs=[VMEM] * 2,
        out_shape=[
            jax.ShapeDtypeStruct((UPPER, WIDTH), F32),
            jax.ShapeDtypeStruct((8, SUM_ROWS // 2), F32),
        ],
        compiler_params=params(),
        name="residual_upper",
    )(own_a, got_a, x_video, mod_video)
    x_video_out, x_text_out, lower_rows, sums = pl.pallas_call(
        residual_kernel,
        in_specs=[VMEM] * 8,
        out_specs=[VMEM] * 4,
        out_shape=[
            jax.ShapeDtypeStruct((VID, WIDTH), BF16),
            jax.ShapeDtypeStruct((TXTR, WIDTH), BF16),
            jax.ShapeDtypeStruct((LOWER + TXTR, WIDTH), F32),
            jax.ShapeDtypeStruct((8, SUM_ROWS), F32),
        ],
        compiler_params=params(),
        name="residual",
    )(upper_rows, upper_sums, own_b, got_b, x_video, x_text, mod_video, mod_text)
    sums = sums + pair(sums)
    mlp_video_in, mlp_text_in = pl.pallas_call(
        norm_kernel,
        in_specs=[VMEM] * 8,
        out_specs=[VMEM] * 2,
        out_shape=[jax.ShapeDtypeStruct((VID, WIDTH), BF16), jax.ShapeDtypeStruct((TXTR, WIDTH), BF16)],
        compiler_params=params(),
        name="norm",
    )(upper_rows, lower_rows, mod_video, mod_text, sums, *[from_on[k](sums) for k in (1, 2, 3)])
    return x_video_out, mlp_video_in, x_text_out, mlp_text_in


def solution(mesh):
    tokens, rows, columns = P("seq", "head"), P("head", None), P(None, "head")
    return jax.shard_map(
        local,
        mesh=mesh,
        in_specs=(tokens,) * 8 + (rows, rows, columns, columns),
        out_specs=(tokens,) * 4,
        check_vma=False,
    )
```
